256 devices in a mesh: prefix: 8 (over x, core), batch: 8 (over z), narrow: 4 (over y).
Axes of the slice: x: 4, y: 4, z: 8, core: 2. Of those that a mesh axis runs over, the one named last changes fastest.
Arguments:
- queries: bfloat16 [128, 2, 128, 576], P('batch', None, 'narrow'), may hold values from -28 to 28, as said below
- new_latent: bfloat16 [128, 2, 576], P('batch'), may hold values from -4 to 4
- prefix_cache: bfloat16 [512, 64, 576], P('prefix'), may hold values from -4 to 4, as said below
- suffix_cache: bfloat16 [128, 16, 64, 576], P('batch', 'narrow'), may hold values from -4 to 4
- branch_prefix_page_lists: int32 [128, 64], P('batch'), may hold values from 0 to 511, as said below
- prefix_count: int32 [128], P('batch'), may hold values from 1 to 64, as said below
- suffix_len: int32 [128], P('batch'), may hold values from 1 to 1024, as said below
Outputs:
- attention: bfloat16 [128, 2, 128, 512], P('batch', None, ('prefix', 'narrow'))
The draws below stay inside these ranges and needn't reach their ends.
Inputs may be any that keep to these rules, and one draw needn't show every extreme that they name: The queries' values lie in this range. `prefix_cache`: the cache's values lie in this range. `branch_prefix_page_lists`: the 64 entries of a branch's list are distinct page numbers; only the first prefix_count of them are used. `prefix_count`: some branch uses its whole list. `suffix_len`: some branch fills all 1024 suffix slots.
All inputs are finite; a program needn't handle non-finite values.
Results may differ from the reference program's by a relative error of at most 0.0031.
Values may be sent and summed in bfloat16 or wider, within the bound.
A program may use at most 128 MiB of HBM per device.

```python
import jax
import jax.numpy as jnp
from jax import lax

H = 128
LAT = 512
KV = 576
PAGE = 64
STEPS = 2
TREES = 8
BRANCHES = 128
NPP = 512
MAXP = 64
SPG = 16
SUF = 1024


def forest_cache(key):
    random_child_seed = jax.random.fold_in(key, 11)
    return jnp.clip(jax.random.normal(random_child_seed, (NPP, PAGE, KV), jnp.float32), -4.0, 4.0)


def tree_grove_tables(key):
    tree_ids = jax.random.randint(jax.random.fold_in(key, 5), (BRANCHES,), 0, TREES)
    order = jax.random.permutation(jax.random.fold_in(key, 6), NPP)
    depth = jnp.arange(MAXP)
    return order[depth[None, :] * TREES + tree_ids[:, None]].astype(jnp.int32)


def draw_prefix_cache(key, part):
    base = forest_cache(key)
    return base.astype(jnp.bfloat16)


def draw_queries(key, part):
    key = jax.random.fold_in(key, 102)
    values = jnp.clip(2.0 * jax.random.normal(key, (BRANCHES, STEPS, H, KV), jnp.float32), -8.0, 8.0)
    return values.astype(jnp.bfloat16)


def draw_branch_prefix_page_lists(key, part):
    lists = tree_grove_tables(key)
    return lists


def draw_prefix_count(key, part):
    key = jax.random.fold_in(key, 104)
    counts = jax.random.randint(key, (BRANCHES,), 1, MAXP + 1)
    deepest_branch = jax.random.randint(jax.random.fold_in(key, 1), (), 0, BRANCHES)
    return counts.at[deepest_branch].set(MAXP).astype(jnp.int32)


def draw_suffix_len(key, part):
    key = jax.random.fold_in(key, 105)
    sequence_extents = jax.random.randint(key, (BRANCHES,), 1, SUF + 1)
    deepest_branch = jax.random.randint(jax.random.fold_in(key, 1), (), 0, BRANCHES)
    return sequence_extents.at[deepest_branch].set(SUF).astype(jnp.int32)


def level_of(key, dims, pieces, least, top_value):
    loudness, own = 1.0, jax.random.fold_in(key, 6)
    for dim, blocks in pieces:
        heights = jnp.exp(jax.random.uniform(jax.random.fold_in(own, dim), (blocks,), jnp.float32, least / len(pieces), top_value / len(pieces)))
        loudness = loudness * jnp.repeat(heights, dims[dim] // blocks).reshape([-1 if axis == dim else 1 for axis in range(len(dims))])
    return loudness


def normal_values(rng, dims, deviation, bound, shards=(), kind=jnp.bfloat16):
    loudness = level_of(rng, dims, shards, -0.22, 0.18) if shards else 1.0
    values = jax.random.normal(rng, dims, jnp.float32) * deviation * loudness
    return jnp.minimum(jnp.maximum(values, -bound), bound).astype(kind)


def setup_inputs(seed: int = 0) -> dict:
    arg_keys = jax.random.split(jax.random.key(seed), 8)
    queries = draw_queries(jax.random.fold_in(arg_keys[7], 71), 0)
    new_latent = normal_values(arg_keys[1], (BRANCHES, STEPS, KV), 1.0, 4.0, ((0, 8),))
    prefix_cache = draw_prefix_cache(jax.random.fold_in(arg_keys[7], 71), 0)
    suffix_cache = normal_values(arg_keys[3], (BRANCHES, SPG, PAGE, KV), 1.0, 4.0, ((0, 8), (1, 4)))
    branch_prefix_page_lists = draw_branch_prefix_page_lists(jax.random.fold_in(arg_keys[7], 71), 0)
    prefix_count = draw_prefix_count(jax.random.fold_in(arg_keys[7], 71), 0)
    suffix_len = draw_suffix_len(jax.random.fold_in(arg_keys[7], 71), 0)
    return dict(queries=queries, new_latent=new_latent, prefix_cache=prefix_cache, suffix_cache=suffix_cache, branch_prefix_page_lists=branch_prefix_page_lists, prefix_count=prefix_count, suffix_len=suffix_len)


score_scale = 192 ** -0.5
masked_score = -1e30


def reference(queries, new_latent, prefix_cache, suffix_cache, branch_prefix_page_lists, prefix_count, suffix_len):
    def one_branch(index):
        query = queries[index].astype(jnp.float32)
        listing = branch_prefix_page_lists[index]
        prefix_keys = prefix_cache[listing].reshape(MAXP * PAGE, KV)
        slot_valid_mask = jnp.arange(MAXP).astype(jnp.int32) < prefix_count[index]
        prefix_valid = jnp.repeat(slot_valid_mask, PAGE)
        suffix_keys = suffix_cache[index].reshape(SUF, KV)
        suffix_valid = jnp.arange(SUF).astype(jnp.int32) < suffix_len[index]
        fresh = new_latent[index]
        keys_all = jnp.concatenate([prefix_keys, suffix_keys, fresh], axis=0).astype(jnp.float32)
        shared_valid = jnp.concatenate([prefix_valid, suffix_valid])
        causal_ordering = jnp.arange(STEPS)[None, :] <= jnp.arange(STEPS)[:, None]
        valid = jnp.concatenate([jnp.broadcast_to(shared_valid[None, :], (STEPS, shared_valid.shape[0])), causal_ordering], axis=1)
        scores = score_scale * jnp.einsum('thd,kd->thk', query, keys_all)
        scores = jnp.where(valid[:, None, :], scores, masked_score)
        highest = jnp.max(scores, axis=-1, keepdims=True)
        expo = jnp.exp(scores - highest)
        total = jnp.sum(expo, axis=-1)
        weights = expo.astype(jnp.bfloat16).astype(jnp.float32)
        summed = jnp.einsum('thk,kd->thd', weights, keys_all[:, :LAT])
        return (summed / total[..., None]).astype(jnp.bfloat16)

    return lax.map(one_branch, jnp.arange(BRANCHES).astype(jnp.int32))
```

```python
import functools

import jax
import jax.numpy as jnp
from jax import lax
from jax.experimental import pallas as pl
from jax.experimental.pallas import tpu as pltpu
from jax.sharding import PartitionSpec as P

MESH = pl.DeviceIdType.MESH
LAT = 512
KV = 576
PAGE = 64
ROWS = 64
GROUP = 4
TILE = GROUP * PAGE
UNROLL = 4
NONE = -30000.0
MASKED = -1e30
TO_LOG2 = 192 ** -0.5 * 1.4426950408889634
LINK = jnp.int16
STEPS_OF = 32767.0
SMALL = 1e-28


def by_owner(a):
    width = a.shape[-1]
    first = a[:32].reshape(4, 8, width)
    second = a[32:].reshape(4, 8, width)
    low = lax.broadcasted_iota(jnp.int32, (4, 8, width), 1) < 4
    even = jnp.where(low, first, pltpu.roll(second, 4, 1))
    odd = jnp.where(low, pltpu.roll(first, 4, 1), second)
    return [(even if d % 2 == 0 else odd)[d // 2] for d in range(8)]


def coded(part, high, total):
    largest = jnp.maximum(jnp.max(jnp.abs(part), axis=1, keepdims=True), SMALL)
    code = jnp.round(part * (STEPS_OF / largest)).astype(jnp.int32)
    return code, high + jnp.log2(largest * (1.0 / STEPS_OF)), total * (STEPS_OF / largest)


def wide(a):
    return jnp.concatenate([a] * 4, axis=1)


def prefix_kernel(
    count_ref, lists_ref, q_any, cache_any, part_ref, stat_ref,
    q_ref, cache_ref, meta_v, meta_s, acc, top, tot, sems,
):
    q_copy = pltpu.make_async_copy(q_any, q_ref, sems.at[0])
    cache_copy = pltpu.make_async_copy(cache_any, cache_ref, sems.at[1])
    q_copy.start()
    cache_copy.start()

    base = lax.axis_index("prefix") * 64
    f32 = jnp.float32
    lists = lists_ref[...]
    row = lax.broadcasted_iota(jnp.int32, (16, 64), 0)
    col = lax.broadcasted_iota(jnp.int32, (16, 64), 1)
    counts = jnp.zeros((16, 64), jnp.int32)
    for b in range(16):
        counts = jnp.where(row == b, count_ref[b], counts)
    local = lists - base
    used = (col < counts) & (local >= 0) & (local < 64)
    page_of = jnp.where(used, local, -1).astype(f32)
    page_t = jnp.transpose(page_of)
    used_t = jnp.where(page_t >= 0, 1.0, 0.0)
    before = jnp.where(
        lax.broadcasted_iota(jnp.int32, (64, 64), 1) < lax.broadcasted_iota(jnp.int32, (64, 64), 0), 1.0, 0.0
    ).astype(jnp.bfloat16)
    rank_t = jnp.dot(before, used_t.astype(jnp.bfloat16), preferred_element_type=f32)
    place = jnp.where(used_t > 0, rank_t, -1.0)
    place_iota = lax.broadcasted_iota(jnp.int32, (64, 128), 1).astype(f32)
    meta_v[...] = jnp.zeros_like(meta_v)
    for b in range(16):
        hit = place[:, b:b + 1] == place_iota
        packed = jnp.sum(jnp.where(hit, page_t[:, b:b + 1], 0.0), axis=0, keepdims=True)
        meta_v[b:b + 1, 0:128] = packed.astype(jnp.int32)
    number = jnp.sum(jnp.where(used, 1.0, 0.0), axis=1, keepdims=True)
    number = jnp.broadcast_to(number, (16, 256))
    tiles = jnp.floor((number + (GROUP - 1)) * (1.0 / GROUP))
    earlier = jnp.where(
        lax.broadcasted_iota(jnp.int32, (16, 16), 1) < lax.broadcasted_iota(jnp.int32, (16, 16), 0), 1.0, 0.0
    ).astype(jnp.bfloat16)
    start = jnp.dot(earlier, tiles.astype(jnp.bfloat16), preferred_element_type=f32)
    slot = lax.broadcasted_iota(jnp.int32, (16, 256), 1).astype(f32)
    inside = (slot >= start) & (slot < start + tiles)
    branch = lax.broadcasted_iota(jnp.int32, (16, 256), 0).astype(f32)

    def pick(a):
        return jnp.sum(jnp.where(inside, a, 0.0), axis=0, keepdims=True).astype(jnp.int32)

    meta_v[16:17, :] = pick(branch)
    meta_v[17:18, :] = pick((slot - start) * GROUP)
    meta_v[18:19, :] = pick(jnp.clip(number - (slot - start) * GROUP, 0.0, float(GROUP)) * PAGE)
    meta_v[19:20, :] = jnp.sum(tiles, axis=0, keepdims=True).astype(jnp.int32)
    meta_copy = pltpu.make_async_copy(meta_v, meta_s, sems.at[2])
    meta_copy.start()
    acc[...] = jnp.zeros_like(acc)
    top[...] = jnp.full_like(top, NONE)
    tot[...] = jnp.zeros_like(tot)
    meta_copy.wait()
    q_copy.wait()
    cache_copy.wait()

    key_iota = lax.broadcasted_iota(jnp.int32, (ROWS, TILE), 1)

    def one(s):
        b = meta_s[16, s]
        k = meta_s[17, s]
        live = meta_s[18, s]
        keys = jnp.concatenate([cache_ref[meta_s[b, k + i]] for i in range(GROUP)], axis=0)
        score = lax.dot_general(
            q_ref[b], keys, (((1,), (1,)), ((), ())), preferred_element_type=f32
        ) * TO_LOG2
        score = jnp.where(key_iota < live, score, MASKED)
        high = jnp.maximum(jnp.max(score, axis=1, keepdims=True), NONE)
        expo = jnp.exp2(score - high)
        total = jnp.sum(expo, axis=1, keepdims=True)
        part = jnp.dot(expo.astype(jnp.bfloat16), keys[:, :LAT], preferred_element_type=f32)
        return b, high, total, part

    def some(i, carry):
        done = [one(i * UNROLL + u) for u in range(UNROLL)]
        for b, high, total, part in done:
            old = top[b]
            new = jnp.maximum(old, high)
            f_old = jnp.exp2(old - new)
            f_new = jnp.exp2(high - new)
            top[b] = new
            tot[b] = tot[b] * f_old + total * f_new
            acc[b] = acc[b] * wide(f_old) + part * wide(f_new)
        return carry

    lax.fori_loop(0, (meta_s[19, 0] + UNROLL - 1) // UNROLL, some, 0)

    lane = lax.broadcasted_iota(jnp.int32, (ROWS, 128), 1)

    def pack(i, carry):
        high_all, total_all = carry
        pieces = []
        for b in (2 * i, 2 * i + 1):
            code, high, total = coded(acc[b], top[b], tot[b])
            high_all = jnp.where(lane == b, high, high_all)
            total_all = jnp.where(lane == b, total, total_all)
            pieces.append(by_owner(code))
        left, right = pieces
        for d in range(8):
            part_ref[d, pl.ds(pl.multiple_of(16 * i, 16), 16), :] = jnp.concatenate(
                [left[d], right[d]], axis=0
            ).astype(LINK)
        return high_all, total_all

    high_all, total_all = lax.fori_loop(
        0, 8, pack, (jnp.full((ROWS, 128), NONE, f32), jnp.zeros((ROWS, 128), f32))
    )
    for d, (h, t) in enumerate(zip(by_owner(high_all), by_owner(total_all))):
        stat_ref[d, 0:8, :] = h
        stat_ref[d, 8:16, :] = t


def prefix_part(counts, lists, queries, cache):
    return pl.pallas_call(
        prefix_kernel,
        out_shape=(
            jax.ShapeDtypeStruct((8, 128, LAT), LINK),
            jax.ShapeDtypeStruct((8, 16, 128), jnp.float32),
        ),
        in_specs=[
            pl.BlockSpec(memory_space=pltpu.SMEM),
            pl.BlockSpec(memory_space=pltpu.VMEM),
            pl.BlockSpec(memory_space=pl.ANY),
            pl.BlockSpec(memory_space=pl.ANY),
        ],
        out_specs=(pl.BlockSpec(memory_space=pltpu.VMEM),) * 2,
        scratch_shapes=[
            pltpu.VMEM((16, ROWS, KV), jnp.bfloat16),
            pltpu.VMEM((64, PAGE, KV), jnp.bfloat16),
            pltpu.VMEM((24, 256), jnp.int32),
            pltpu.SMEM((24, 256), jnp.int32),
            pltpu.VMEM((16, ROWS, LAT), jnp.float32),
            pltpu.VMEM((16, ROWS, 128), jnp.float32),
            pltpu.VMEM((16, ROWS, 128), jnp.float32),
            pltpu.SemaphoreType.DMA((3,)),
        ],
        compiler_params=pltpu.CompilerParams(vmem_limit_bytes=40 << 20),
        name="prefix_part",
    )(counts, lists, queries, cache)


def owner_of(prefix):
    return 4 * lax.rem(prefix, 2) + lax.div(prefix, 2)


def join_kernel(
    len_ref, new_ref, q_any, suffix_any, part_any, stat_any, out_ref,
    q_all, keys_ref, fresh, send_part, send_stat, pre_part, pre_stat, suf_part, suf_stat, done,
    local_sems, q_send, q_recv, pre_send, pre_recv, suf_send, suf_recv, end_sems,
):
    f32 = jnp.float32
    p = lax.axis_index("prefix")
    n = lax.axis_index("narrow")
    me = 4 * p + n
    x = lax.div(p, 2)
    c = lax.rem(p, 2)
    mine = owner_of(p)

    own = [
        pltpu.make_async_copy(suffix_any.at[pl.ds(2 * p, 2)], keys_ref, local_sems.at[0]),
        pltpu.make_async_copy(q_any.at[pl.ds(2 * p, 2)], q_all.at[n], local_sems.at[1]),
        pltpu.make_async_copy(part_any.at[mine], pre_part.at[p], local_sems.at[2]),
        pltpu.make_async_copy(stat_any.at[mine], pre_stat.at[p], local_sems.at[3]),
    ]
    for copy in own:
        copy.start()

    barrier = pltpu.get_barrier_semaphore()

    def greet(k, carry):
        other = lax.rem(me + k, 32)
        pl.semaphore_signal(
            barrier, inc=1, device_id={"prefix": lax.div(other, 4), "narrow": lax.rem(other, 4)},
            device_id_type=MESH,
        )
        return carry

    lax.fori_loop(1, 32, greet, 0)
    pl.semaphore_wait(barrier, 31)

    def q_copy(k):
        return pltpu.make_async_remote_copy(
            src_ref=q_any.at[pl.ds(2 * p, 2)], dst_ref=q_all.at[n],
            send_sem=q_send.at[k], recv_sem=q_recv.at[n],
            device_id={"narrow": lax.rem(n + k, 4)}, device_id_type=MESH,
        )

    def pre_copies(k):
        other = lax.rem(p + k, 8)
        to = owner_of(other)
        return [
            pltpu.make_async_remote_copy(
                src_ref=part_any.at[to], dst_ref=pre_part.at[p],
                send_sem=pre_send.at[0, k], recv_sem=pre_recv.at[0, p],
                device_id={"prefix": other}, device_id_type=MESH,
            ),
            pltpu.make_async_remote_copy(
                src_ref=stat_any.at[to], dst_ref=pre_stat.at[p],
                send_sem=pre_send.at[1, k], recv_sem=pre_recv.at[1, p],
                device_id={"prefix": other}, device_id_type=MESH,
            ),
        ]

    for k in range(1, 4):
        q_copy(k).start()

    def pre_start(k, carry):
        for copy in pre_copies(k):
            copy.start()
        return carry

    lax.fori_loop(1, 8, pre_start, 0)

    fresh[...] = jnp.zeros_like(fresh)
    for j in range(2):
        fresh[j, 0:2, :] = new_ref[2 * p + j]
    own[0].wait()
    own[1].wait()
    for k in range(1, 4):
        source = lax.rem(n + k, 4)
        pltpu.make_async_copy(q_all.at[source], q_all.at[source], q_recv.at[source]).wait()

    width = TILE + 16
    key_at = lax.broadcasted_iota(jnp.int32, (256, width), 1)
    step = lax.rem(lax.div(lax.broadcasted_iota(jnp.int32, (256, width), 0), 32), 2)
    new_live = (key_at >= TILE) & (key_at - TILE <= step) & (key_at < TILE + 2) & (n == 0)
    results = []
    for j in range(2):
        keys = jnp.concatenate([keys_ref[j], fresh[j]], axis=0)
        score = lax.dot_general(
            q_all[:, j].reshape(256, KV), keys, (((1,), (1,)), ((), ())), preferred_element_type=f32
        ) * TO_LOG2
        live = (key_at < jnp.minimum(len_ref[2 * p + j] - n * TILE, TILE)) | new_live
        score = jnp.where(live, score, MASKED)
        high = jnp.maximum(jnp.max(score, axis=1, keepdims=True), NONE)
        expo = jnp.exp2(score - high)
        total = jnp.sum(expo, axis=1, keepdims=True)
        part = jnp.dot(expo.astype(jnp.bfloat16), keys[:, :LAT], preferred_element_type=f32)
        code, high, total = coded(part, high, total)
        results.append((high, total, code))
    lane = lax.broadcasted_iota(jnp.int32, (ROWS, 128), 1)
    for m in range(4):
        rows = slice(64 * m, 64 * m + 64)
        (h0, t0, p0), (h1, t1, p1) = [[a[rows] for a in r] for r in results]
        high = jnp.where(lane == 2 * p, h0, jnp.where(lane == 2 * p + 1, h1, NONE))
        total = jnp.where(lane == 2 * p, t0, jnp.where(lane == 2 * p + 1, t1, 0.0))
        for d, (h, t, a, b) in enumerate(zip(by_owner(high), by_owner(total), by_owner(p0), by_owner(p1))):
            send_stat[8 * m + d] = jnp.concatenate([h, t], axis=0)
            send_part[8 * m + d] = jnp.concatenate([a, b], axis=0).astype(LINK)

    rows_here = pl.ds(pl.multiple_of(16 * p, 16), 16)

    def suf_copies(k):
        other = lax.rem(me + k, 32)
        p_to, n_to = lax.div(other, 4), lax.rem(other, 4)
        piece = 8 * n_to + owner_of(p_to)
        return [
            pltpu.make_async_remote_copy(
                src_ref=send_part.at[piece], dst_ref=suf_part.at[n, rows_here],
                send_sem=suf_send.at[0, k], recv_sem=suf_recv.at[0, me],
                device_id={"prefix": p_to, "narrow": n_to}, device_id_type=MESH,
            ),
            pltpu.make_async_remote_copy(
                src_ref=send_stat.at[piece], dst_ref=suf_stat.at[n, p],
                send_sem=suf_send.at[1, k], recv_sem=suf_recv.at[1, me],
                device_id={"prefix": p_to, "narrow": n_to}, device_id_type=MESH,
            ),
        ]

    def suf_start(k, carry):
        for copy in suf_copies(k):
            copy.start()
        return carry

    lax.fori_loop(1, 32, suf_start, 0)
    mine_piece = 8 * n + mine
    kept = [
        pltpu.make_async_copy(send_part.at[mine_piece], suf_part.at[n, rows_here], local_sems.at[4]),
        pltpu.make_async_copy(send_stat.at[mine_piece], suf_stat.at[n, p], local_sems.at[5]),
    ]
    for copy in kept:
        copy.start()

    own[2].wait()
    own[3].wait()
    for copy in kept:
        copy.wait()

    def pre_wait(k, carry):
        source = lax.rem(p + k, 8)
        pltpu.make_async_copy(pre_part.at[source], pre_part.at[source], pre_recv.at[0, source]).wait()
        pltpu.make_async_copy(pre_stat.at[source], pre_stat.at[source], pre_recv.at[1, source]).wait()
        return carry

    lax.fori_loop(1, 8, pre_wait, 0)

    def suf_wait(k, carry):
        source = lax.rem(me + k, 32)
        p_from, n_from = lax.div(source, 4), lax.rem(source, 4)
        landed = suf_part.at[n_from, pl.ds(pl.multiple_of(16 * p_from, 16), 16)]
        pltpu.make_async_copy(landed, landed, suf_recv.at[0, source]).wait()
        noted = suf_stat.at[n_from, p_from]
        pltpu.make_async_copy(noted, noted, suf_recv.at[1, source]).wait()
        return carry

    lax.fori_loop(1, 32, suf_wait, 0)

    highest = jnp.full((8, 128), NONE, f32)
    for i in range(8):
        highest = jnp.maximum(highest, pre_stat[i, 0:8, :])
    for m in range(4):
        for i in range(8):
            highest = jnp.maximum(highest, suf_stat[m, i, 0:8, :])
    total = jnp.zeros((8, 128), f32)
    factors = []
    for i in range(8):
        f = jnp.exp2(pre_stat[i, 0:8, :] - highest)
        total = total + f * pre_stat[i, 8:16, :]
        factors.append(f)
    for m in range(4):
        f_sum = jnp.zeros((8, 128), f32)
        for i in range(8):
            f = jnp.exp2(suf_stat[m, i, 0:8, :] - highest)
            total = total + f * suf_stat[m, i, 8:16, :]
            f_sum = f_sum + f
        factors.append(f_sum)
    lane8 = lax.broadcasted_iota(jnp.int32, (8, 128), 1)
    inverse = 1.0 / jnp.where(lane8 < 16, total, 1.0)
    factors = [f * inverse for f in factors]
    for i in range(8):
        rows = slice(16 * i, 16 * i + 16)
        value = jnp.zeros((16, LAT), f32)
        for at, f in enumerate(factors):
            source = pre_part[at, rows, :] if at < 8 else suf_part[at - 8, rows, :]
            weight = jnp.concatenate([f[:, 2 * i:2 * i + 1], f[:, 2 * i + 1:2 * i + 2]], axis=0)
            value = value + source.astype(f32) * weight
        done[rows, :] = value.astype(jnp.bfloat16)

    last = pltpu.make_async_remote_copy(
        src_ref=done, dst_ref=out_ref, send_sem=end_sems.at[0], recv_sem=end_sems.at[1],
        device_id={"prefix": 2 * n + c, "narrow": x}, device_id_type=MESH,
    )
    stays = x == n

    @pl.when(stays)
    def _():
        out_ref[...] = done[...]

    @pl.when(jnp.logical_not(stays))
    def _():
        last.start()

    for k in range(1, 4):
        q_copy(k).wait_send()

    def pre_sent(k, carry):
        for copy in pre_copies(k):
            copy.wait_send()
        return carry

    lax.fori_loop(1, 8, pre_sent, 0)

    def suf_sent(k, carry):
        for copy in suf_copies(k):
            copy.wait_send()
        return carry

    lax.fori_loop(1, 32, suf_sent, 0)

    @pl.when(jnp.logical_not(stays))
    def _():
        last.wait()


def join(lens, new_latent, queries, suffix, part, stat):
    dma = pltpu.SemaphoreType.DMA
    return pl.pallas_call(
        join_kernel,
        out_shape=jax.ShapeDtypeStruct((128, LAT), jnp.bfloat16),
        in_specs=[
            pl.BlockSpec(memory_space=pltpu.SMEM),
            pl.BlockSpec(memory_space=pltpu.VMEM),
            pl.BlockSpec(memory_space=pl.ANY),
            pl.BlockSpec(memory_space=pl.ANY),
            pl.BlockSpec(memory_space=pl.ANY),
            pl.BlockSpec(memory_space=pl.ANY),
        ],
        out_specs=pl.BlockSpec(memory_space=pltpu.VMEM),
        scratch_shapes=[
            pltpu.VMEM((4, 2, ROWS, KV), jnp.bfloat16),
            pltpu.VMEM((2, TILE, KV), jnp.bfloat16),
            pltpu.VMEM((2, 16, KV), jnp.bfloat16),
            pltpu.VMEM((32, 16, LAT), LINK),
            pltpu.VMEM((32, 16, 128), jnp.float32),
            pltpu.VMEM((8, 128, LAT), LINK),
            pltpu.VMEM((8, 16, 128), jnp.float32),
            pltpu.VMEM((4, 128, LAT), LINK),
            pltpu.VMEM((4, 8, 16, 128), jnp.float32),
            pltpu.VMEM((128, LAT), jnp.bfloat16),
            dma((6,)),
            dma((4,)),
            dma((4,)),
            dma((2, 8)),
            dma((2, 8)),
            dma((2, 32)),
            dma((2, 32)),
            dma((2,)),
        ],
        compiler_params=pltpu.CompilerParams(
            collective_id=0, has_side_effects=True, vmem_limit_bytes=40 << 20
        ),
        name="join",
    )(lens, new_latent, queries, suffix, part, stat)


def local(queries, new_latent, prefix_cache, suffix_cache, page_lists, prefix_count, suffix_len):
    rows = queries.reshape(16, ROWS, KV)
    part, stat = prefix_part(prefix_count, page_lists, rows, prefix_cache)
    suffix = suffix_cache.reshape(16, TILE, KV)
    out = join(suffix_len, new_latent, rows, suffix, part, stat)
    return out.reshape(16, 2, 4, LAT)


def solution(mesh):
    return jax.shard_map(
        local,
        mesh=mesh,
        in_specs=(
            P("batch", None, "narrow", None),
            P("batch", None, None),
            P("prefix", None, None),
            P("batch", "narrow", None, None),
            P("batch", None),
            P("batch"),
            P("batch"),
        ),
        out_specs=P("batch", None, ("prefix", "narrow"), None),
        check_vma=False,
    )
```

```python
import functools

import jax
import jax.numpy as jnp
from jax import lax
from jax.experimental import pallas as pl
from jax.experimental.pallas import tpu as pltpu
from jax.sharding import PartitionSpec as P

MESH = pl.DeviceIdType.MESH
LAT = 512
KV = 576
PAGE = 64
ROWS = 64
GROUP = 4
TILE = GROUP * PAGE
UNROLL = 4
NONE = -30000.0
MASKED = -1e30
TO_LOG2 = 192 ** -0.5 * 1.4426950408889634
LINK = jnp.int16
STEPS_OF = 32767.0
SMALL = 1e-28


def by_owner(a):
    width = a.shape[-1]
    first = a[:32].reshape(4, 8, width)
    second = a[32:].reshape(4, 8, width)
    low = lax.broadcasted_iota(jnp.int32, (4, 8, width), 1) < 4
    even = jnp.where(low, first, pltpu.roll(second, 4, 1))
    odd = jnp.where(low, pltpu.roll(first, 4, 1), second)
    return [(even if d % 2 == 0 else odd)[d // 2] for d in range(8)]


def coded(part, high, total):
    largest = jnp.maximum(jnp.max(jnp.abs(part), axis=1, keepdims=True), SMALL)
    code = jnp.round(part * (STEPS_OF / largest)).astype(jnp.int32)
    return code, high + jnp.log2(largest * (1.0 / STEPS_OF)), total * (STEPS_OF / largest)


def wide(a):
    return jnp.concatenate([a] * 4, axis=1)


def prefix_kernel(
    count_ref, lists_ref, q_any, cache_any, part_ref, stat_ref,
    q_ref, cache_ref, meta_v, meta_s, acc, top, tot, sems,
):
    q_copy = pltpu.make_async_copy(q_any, q_ref, sems.at[0])
    cache_copy = pltpu.make_async_copy(cache_any, cache_ref, sems.at[1])
    q_copy.start()
    cache_copy.start()

    base = lax.axis_index("prefix") * 64
    f32 = jnp.float32
    lists = lists_ref[...]
    row = lax.broadcasted_iota(jnp.int32, (16, 64), 0)
    col = lax.broadcasted_iota(jnp.int32, (16, 64), 1)
    counts = jnp.zeros((16, 64), jnp.int32)
    for b in range(16):
        counts = jnp.where(row == b, count_ref[b], counts)
    local = lists - base
    used = (col < counts) & (local >= 0) & (local < 64)
    page_of = jnp.where(used, local, -1).astype(f32)
    page_t = jnp.transpose(page_of)
    used_t = jnp.where(page_t >= 0, 1.0, 0.0)
    before = jnp.where(
        lax.broadcasted_iota(jnp.int32, (64, 64), 1) < lax.broadcasted_iota(jnp.int32, (64, 64), 0), 1.0, 0.0
    ).astype(jnp.bfloat16)
    rank_t = jnp.dot(before, used_t.astype(jnp.bfloat16), preferred_element_type=f32)
    place = jnp.where(used_t > 0, rank_t, -1.0)
    place_iota = lax.broadcasted_iota(jnp.int32, (64, 128), 1).astype(f32)
    meta_v[...] = jnp.zeros_like(meta_v)
    for b in range(16):
        hit = place[:, b:b + 1] == place_iota
        packed = jnp.sum(jnp.where(hit, page_t[:, b:b + 1], 0.0), axis=0, keepdims=True)
        meta_v[b:b + 1, 0:128] = packed.astype(jnp.int32)
    number = jnp.sum(jnp.where(used, 1.0, 0.0), axis=1, keepdims=True)
    number = jnp.broadcast_to(number, (16, 256))
    tiles = jnp.floor((number + (GROUP - 1)) * (1.0 / GROUP))
    earlier = jnp.where(
        lax.broadcasted_iota(jnp.int32, (16, 16), 1) < lax.broadcasted_iota(jnp.int32, (16, 16), 0), 1.0, 0.0
    ).astype(jnp.bfloat16)
    start = jnp.dot(earlier, tiles.astype(jnp.bfloat16), preferred_element_type=f32)
    slot = lax.broadcasted_iota(jnp.int32, (16, 256), 1).astype(f32)
    inside = (slot >= start) & (slot < start + tiles)
    branch = lax.broadcasted_iota(jnp.int32, (16, 256), 0).astype(f32)

    def pick(a):
        return jnp.sum(jnp.where(inside, a, 0.0), axis=0, keepdims=True).astype(jnp.int32)

    meta_v[16:17, :] = pick(branch)
    meta_v[17:18, :] = pick((slot - start) * GROUP)
    meta_v[18:19, :] = pick(jnp.clip(number - (slot - start) * GROUP, 0.0, float(GROUP)) * PAGE)
    meta_v[19:20, :] = jnp.sum(tiles, axis=0, keepdims=True).astype(jnp.int32)
    meta_copy = pltpu.make_async_copy(meta_v, meta_s, sems.at[2])
    meta_copy.start()
    acc[...] = jnp.zeros_like(acc)
    top[...] = jnp.full_like(top, NONE)
    tot[...] = jnp.zeros_like(tot)
    meta_copy.wait()
    q_copy.wait()
    cache_copy.wait()

    key_iota = lax.broadcasted_iota(jnp.int32, (ROWS, TILE), 1)

    def one(s):
        b = meta_s[16, s]
        k = meta_s[17, s]
        live = meta_s[18, s]
        keys = jnp.concatenate([cache_ref[meta_s[b, k + i]] for i in range(GROUP)], axis=0)
        score = lax.dot_general(
            q_ref[b], keys, (((1,), (1,)), ((), ())), preferred_element_type=f32
        ) * TO_LOG2
        score = jnp.where(key_iota < live, score, MASKED)
        high = jnp.maximum(jnp.max(score, axis=1, keepdims=True), NONE)
        expo = jnp.exp2(score - high)
        total = jnp.sum(expo, axis=1, keepdims=True)
        part = jnp.dot(expo.astype(jnp.bfloat16), keys[:, :LAT], preferred_element_type=f32)
        return b, high, total, part

    def some(i, carry):
        done = [one(i * UNROLL + u) for u in range(UNROLL)]
        for b, high, total, part in done:
            old = top[b]
            new = jnp.maximum(old, high)
            f_old = jnp.exp2(old - new)
            f_new = jnp.exp2(high - new)
            top[b] = new
            tot[b] = tot[b] * f_old + total * f_new
            acc[b] = acc[b] * wide(f_old) + part * wide(f_new)
        return carry

    lax.fori_loop(0, (meta_s[19, 0] + UNROLL - 1) // UNROLL, some, 0)

    lane = lax.broadcasted_iota(jnp.int32, (ROWS, 128), 1)

    def pack(i, carry):
        high_all, total_all = carry
        pieces = []
        for b in (2 * i, 2 * i + 1):
            code, high, total = coded(acc[b], top[b], tot[b])
            high_all = jnp.where(lane == b, high, high_all)
            total_all = jnp.where(lane == b, total, total_all)
            pieces.append(by_owner(code))
        left, right = pieces
        for d in range(8):
            part_ref[d, pl.ds(pl.multiple_of(16 * i, 16), 16), :] = jnp.concatenate(
                [left[d], right[d]], axis=0
            ).astype(LINK)
        return high_all, total_all

    high_all, total_all = lax.fori_loop(
        0, 8, pack, (jnp.full((ROWS, 128), NONE, f32), jnp.zeros((ROWS, 128), f32))
    )
    for d, (h, t) in enumerate(zip(by_owner(high_all), by_owner(total_all))):
        stat_ref[d, 0:8, :] = h
        stat_ref[d, 8:16, :] = t


def prefix_part(counts, lists, queries, cache):
    return pl.pallas_call(
        prefix_kernel,
        out_shape=(
            jax.ShapeDtypeStruct((8, 128, LAT), LINK),
            jax.ShapeDtypeStruct((8, 16, 128), jnp.float32),
        ),
        in_specs=[
            pl.BlockSpec(memory_space=pltpu.SMEM),
            pl.BlockSpec(memory_space=pltpu.VMEM),
            pl.BlockSpec(memory_space=pl.ANY),
            pl.BlockSpec(memory_space=pl.ANY),
        ],
        out_specs=(pl.BlockSpec(memory_space=pltpu.VMEM),) * 2,
        scratch_shapes=[
            pltpu.VMEM((16, ROWS, KV), jnp.bfloat16),
            pltpu.VMEM((64, PAGE, KV), jnp.bfloat16),
            pltpu.VMEM((24, 256), jnp.int32),
            pltpu.SMEM((24, 256), jnp.int32),
            pltpu.VMEM((16, ROWS, LAT), jnp.float32),
            pltpu.VMEM((16, ROWS, 128), jnp.float32),
            pltpu.VMEM((16, ROWS, 128), jnp.float32),
            pltpu.SemaphoreType.DMA((3,)),
        ],
        compiler_params=pltpu.CompilerParams(vmem_limit_bytes=60 << 20),
        name="prefix_part",
    )(counts, lists, queries, cache)


def owner_of(prefix):
    return 4 * lax.rem(prefix, 2) + lax.div(prefix, 2)


def join_kernel(
    len_ref, new_ref, q_any, suffix_any, part_any, stat_any, out_ref,
    q_all, keys_ref, fresh, send_part, send_stat, pre_part, pre_stat, suf_part, suf_stat, done,
    local_sems, q_send, q_recv, pre_send, pre_recv, suf_send, suf_recv, end_sems,
):
    f32 = jnp.float32
    p = lax.axis_index("prefix")
    n = lax.axis_index("narrow")
    me = 4 * p + n
    x = lax.div(p, 2)
    c = lax.rem(p, 2)
    mine = owner_of(p)

    own = [
        pltpu.make_async_copy(suffix_any.at[pl.ds(2 * p, 2)], keys_ref, local_sems.at[0]),
        pltpu.make_async_copy(q_any.at[pl.ds(2 * p, 2)], q_all.at[n], local_sems.at[1]),
        pltpu.make_async_copy(part_any.at[mine], pre_part.at[p], local_sems.at[2]),
        pltpu.make_async_copy(stat_any.at[mine], pre_stat.at[p], local_sems.at[3]),
    ]
    for copy in own:
        copy.start()

    barrier = pltpu.get_barrier_semaphore()

    def greet(k, carry):
        other = lax.rem(me + k, 32)
        pl.semaphore_signal(
            barrier, inc=1, device_id={"prefix": lax.div(other, 4), "narrow": lax.rem(other, 4)},
            device_id_type=MESH,
        )
        return carry

    lax.fori_loop(1, 32, greet, 0)
    pl.semaphore_wait(barrier, 31)

    def q_copy(k):
        return pltpu.make_async_remote_copy(
            src_ref=q_any.at[pl.ds(2 * p, 2)], dst_ref=q_all.at[n],
            send_sem=q_send.at[k], recv_sem=q_recv.at[n],
            device_id={"narrow": lax.rem(n + k, 4)}, device_id_type=MESH,
        )

    def pre_copies(k):
        other = lax.rem(p + k, 8)
        to = owner_of(other)
        return [
            pltpu.make_async_remote_copy(
                src_ref=part_any.at[to], dst_ref=pre_part.at[p],
                send_sem=pre_send.at[0, k], recv_sem=pre_recv.at[0, p],
                device_id={"prefix": other}, device_id_type=MESH,
            ),
            pltpu.make_async_remote_copy(
                src_ref=stat_any.at[to], dst_ref=pre_stat.at[p],
                send_sem=pre_send.at[1, k], recv_sem=pre_recv.at[1, p],
                device_id={"prefix": other}, device_id_type=MESH,
            ),
        ]

    for k in range(1, 4):
        q_copy(k).start()

    def pre_start(k, carry):
        for copy in pre_copies(k):
            copy.start()
        return carry

    lax.fori_loop(1, 8, pre_start, 0)

    fresh[...] = jnp.zeros_like(fresh)
    for j in range(2):
        fresh[j, 0:2, :] = new_ref[2 * p + j]
    own[0].wait()
    own[1].wait()
    for k in range(1, 4):
        source = lax.rem(n + k, 4)
        pltpu.make_async_copy(q_all.at[source], q_all.at[source], q_recv.at[source]).wait()

    width = TILE + 16
    key_at = lax.broadcasted_iota(jnp.int32, (256, width), 1)
    step = lax.rem(lax.div(lax.broadcasted_iota(jnp.int32, (256, width), 0), 32), 2)
    new_live = (key_at >= TILE) & (key_at - TILE <= step) & (key_at < TILE + 2) & (n == 0)
    results = []
    for j in range(2):
        keys = jnp.concatenate([keys_ref[j], fresh[j]], axis=0)
        score = lax.dot_general(
            q_all[:, j].reshape(256, KV), keys, (((1,), (1,)), ((), ())), preferred_element_type=f32
        ) * TO_LOG2
        live = (key_at < jnp.minimum(len_ref[2 * p + j] - n * TILE, TILE)) | new_live
        score = jnp.where(live, score, MASKED)
        high = jnp.maximum(jnp.max(score, axis=1, keepdims=True), NONE)
        expo = jnp.exp2(score - high)
        total = jnp.sum(expo, axis=1, keepdims=True)
        part = jnp.dot(expo.astype(jnp.bfloat16), keys[:, :LAT], preferred_element_type=f32)
        code, high, total = coded(part, high, total)
        results.append((high, total, code))
    lane = lax.broadcasted_iota(jnp.int32, (ROWS, 128), 1)
    for m in range(4):
        rows = slice(64 * m, 64 * m + 64)
        (h0, t0, p0), (h1, t1, p1) = [[a[rows] for a in r] for r in results]
        high = jnp.where(lane == 2 * p, h0, jnp.where(lane == 2 * p + 1, h1, NONE))
        total = jnp.where(lane == 2 * p, t0, jnp.where(lane == 2 * p + 1, t1, 0.0))
        for d, (h, t, a, b) in enumerate(zip(by_owner(high), by_owner(total), by_owner(p0), by_owner(p1))):
            send_stat[8 * m + d] = jnp.concatenate([h, t], axis=0)
            send_part[8 * m + d] = jnp.concatenate([a, b], axis=0).astype(LINK)

    rows_here = pl.ds(pl.multiple_of(16 * p, 16), 16)

    def suf_copies(k):
        other = lax.rem(me + k, 32)
        p_to, n_to = lax.div(other, 4), lax.rem(other, 4)
        piece = 8 * n_to + owner_of(p_to)
        return [
            pltpu.make_async_remote_copy(
                src_ref=send_part.at[piece], dst_ref=suf_part.at[n, rows_here],
                send_sem=suf_send.at[0, k], recv_sem=suf_recv.at[0, me],
                device_id={"prefix": p_to, "narrow": n_to}, device_id_type=MESH,
            ),
            pltpu.make_async_remote_copy(
                src_ref=send_stat.at[piece], dst_ref=suf_stat.at[n, p],
                send_sem=suf_send.at[1, k], recv_sem=suf_recv.at[1, me],
                device_id={"prefix": p_to, "narrow": n_to}, device_id_type=MESH,
            ),
        ]

    def suf_start(k, carry):
        for copy in suf_copies(k):
            copy.start()
        return carry

    lax.fori_loop(1, 32, suf_start, 0)
    mine_piece = 8 * n + mine
    kept = [
        pltpu.make_async_copy(send_part.at[mine_piece], suf_part.at[n, rows_here], local_sems.at[4]),
        pltpu.make_async_copy(send_stat.at[mine_piece], suf_stat.at[n, p], local_sems.at[5]),
    ]
    for copy in kept:
        copy.start()

    own[2].wait()
    own[3].wait()
    for copy in kept:
        copy.wait()

    def pre_wait(k, carry):
        source = lax.rem(p + k, 8)
        pltpu.make_async_copy(pre_part.at[source], pre_part.at[source], pre_recv.at[0, source]).wait()
        pltpu.make_async_copy(pre_stat.at[source], pre_stat.at[source], pre_recv.at[1, source]).wait()
        return carry

    lax.fori_loop(1, 8, pre_wait, 0)

    def suf_wait(k, carry):
        source = lax.rem(me + k, 32)
        p_from, n_from = lax.div(source, 4), lax.rem(source, 4)
        landed = suf_part.at[n_from, pl.ds(pl.multiple_of(16 * p_from, 16), 16)]
        pltpu.make_async_copy(landed, landed, suf_recv.at[0, source]).wait()
        noted = suf_stat.at[n_from, p_from]
        pltpu.make_async_copy(noted, noted, suf_recv.at[1, source]).wait()
        return carry

    lax.fori_loop(1, 32, suf_wait, 0)

    highest = jnp.full((8, 128), NONE, f32)
    for i in range(8):
        highest = jnp.maximum(highest, pre_stat[i, 0:8, :])
    for m in range(4):
        for i in range(8):
            highest = jnp.maximum(highest, suf_stat[m, i, 0:8, :])
    total = jnp.zeros((8, 128), f32)
    factors = []
    for i in range(8):
        f = jnp.exp2(pre_stat[i, 0:8, :] - highest)
        total = total + f * pre_stat[i, 8:16, :]
        factors.append(f)
    for m in range(4):
        f_sum = jnp.zeros((8, 128), f32)
        for i in range(8):
            f = jnp.exp2(suf_stat[m, i, 0:8, :] - highest)
            total = total + f * suf_stat[m, i, 8:16, :]
            f_sum = f_sum + f
        factors.append(f_sum)
    lane8 = lax.broadcasted_iota(jnp.int32, (8, 128), 1)
    inverse = 1.0 / jnp.where(lane8 < 16, total, 1.0)
    factors = [f * inverse for f in factors]
    for i in range(8):
        rows = slice(16 * i, 16 * i + 16)
        value = jnp.zeros((16, LAT), f32)
        for at, f in enumerate(factors):
            source = pre_part[at, rows, :] if at < 8 else suf_part[at - 8, rows, :]
            weight = jnp.concatenate([f[:, 2 * i:2 * i + 1], f[:, 2 * i + 1:2 * i + 2]], axis=0)
            value = value + source.astype(f32) * weight
        done[rows, :] = value.astype(jnp.bfloat16)

    last = pltpu.make_async_remote_copy(
        src_ref=done, dst_ref=out_ref, send_sem=end_sems.at[0], recv_sem=end_sems.at[1],
        device_id={"prefix": 2 * n + c, "narrow": x}, device_id_type=MESH,
    )
    stays = x == n

    @pl.when(stays)
    def _():
        out_ref[...] = done[...]

    @pl.when(jnp.logical_not(stays))
    def _():
        last.start()

    for k in range(1, 4):
        q_copy(k).wait_send()

    def pre_sent(k, carry):
        for copy in pre_copies(k):
            copy.wait_send()
        return carry

    lax.fori_loop(1, 8, pre_sent, 0)

    def suf_sent(k, carry):
        for copy in suf_copies(k):
            copy.wait_send()
        return carry

    lax.fori_loop(1, 32, suf_sent, 0)

    @pl.when(jnp.logical_not(stays))
    def _():
        last.wait()


def join(lens, new_latent, queries, suffix, part, stat):
    dma = pltpu.SemaphoreType.DMA
    return pl.pallas_call(
        join_kernel,
        out_shape=jax.ShapeDtypeStruct((128, LAT), jnp.bfloat16),
        in_specs=[
            pl.BlockSpec(memory_space=pltpu.SMEM),
            pl.BlockSpec(memory_space=pltpu.VMEM),
            pl.BlockSpec(memory_space=pl.ANY),
            pl.BlockSpec(memory_space=pl.ANY),
            pl.BlockSpec(memory_space=pl.ANY),
            pl.BlockSpec(memory_space=pl.ANY),
        ],
        out_specs=pl.BlockSpec(memory_space=pltpu.VMEM),
        scratch_shapes=[
            pltpu.VMEM((4, 2, ROWS, KV), jnp.bfloat16),
            pltpu.VMEM((2, TILE, KV), jnp.bfloat16),
            pltpu.VMEM((2, 16, KV), jnp.bfloat16),
            pltpu.VMEM((32, 16, LAT), LINK),
            pltpu.VMEM((32, 16, 128), jnp.float32),
            pltpu.VMEM((8, 128, LAT), LINK),
            pltpu.VMEM((8, 16, 128), jnp.float32),
            pltpu.VMEM((4, 128, LAT), LINK),
            pltpu.VMEM((4, 8, 16, 128), jnp.float32),
            pltpu.VMEM((128, LAT), jnp.bfloat16),
            dma((6,)),
            dma((4,)),
            dma((4,)),
            dma((2, 8)),
            dma((2, 8)),
            dma((2, 32)),
            dma((2, 32)),
            dma((2,)),
        ],
        compiler_params=pltpu.CompilerParams(
            collective_id=0, has_side_effects=True, vmem_limit_bytes=60 << 20
        ),
        name="join",
    )(lens, new_latent, queries, suffix, part, stat)


SLOTS_A = 20
SLOTS = 36
SPAN = 2 * TILE + 16
FUSED = 4


def fused_kernel(
    count_any, len_any, lists_any, new_any, q_any, cache_any, suffix_any, out_ref, spill_ref,
    count_ref, len_ref, lists_ref, new_ref, q_ref, q_rows, q_send, q_all, cache_ref, suffix_ref, fresh,
    meta_v, meta_s, acc, top, tot, weight, weight2, key_rel,
    part_send, stat_send, pre_part, pre_stat, mix_send, mix_stat_send, mix_part, mix_stat, done, spills,
    in_sems, own_sems, q_sems, pre_sems, mix_sems, end_sems, spill_sems,
):
    f32 = jnp.float32
    bf16 = jnp.bfloat16
    p = lax.axis_index("prefix")
    n = lax.axis_index("narrow")
    z = lax.axis_index("batch")
    x = lax.div(p, 2)
    c = lax.rem(p, 2)
    mine = owner_of(p)
    stays = x == n
    across = {"prefix": 2 * n + c, "narrow": x}

    loads = [
        pltpu.make_async_copy(source, target, in_sems.at[k])
        for k, (source, target) in enumerate([
            (count_any, count_ref), (len_any, len_ref), (lists_any, lists_ref), (new_any, new_ref),
            (q_any, q_ref), (cache_any, cache_ref), (suffix_any, suffix_ref),
        ])
    ]
    for copy in loads:
        copy.start()

    barrier = pltpu.get_barrier_semaphore()

    def greet(**to):
        pl.semaphore_signal(barrier, inc=1, device_id=to, device_id_type=MESH)

    for k in range(1, 8):
        greet(prefix=lax.rem(p + k, 8))
        greet(batch=lax.rem(z + k, 8))
    for k in range(1, 4):
        greet(narrow=lax.rem(n + k, 4))

    @pl.when(jnp.logical_not(stays))
    def _():
        greet(**across)

    meta_v[...] = jnp.zeros_like(meta_v)
    fresh[...] = jnp.zeros_like(fresh)
    acc[0] = jnp.zeros((ROWS, LAT), f32)
    top[0] = jnp.full((ROWS, 128), NONE, f32)
    tot[0] = jnp.zeros((ROWS, 128), f32)
    loads[0].wait()
    loads[1].wait()
    loads[2].wait()
    lists = lists_ref[...]
    row = lax.broadcasted_iota(jnp.int32, (16, 64), 0)
    col = lax.broadcasted_iota(jnp.int32, (16, 64), 1)
    counts = jnp.zeros((16, 64), jnp.int32)
    for b in range(16):
        counts = jnp.where(row == b, count_ref[b], counts)
    listed = col < counts

    def pages_in(local):
        return listed & (local >= 0) & (local < 64)

    def tiles_of(used):
        number = jnp.sum(jnp.where(used, 1.0, 0.0), axis=1, keepdims=True)
        number = jnp.broadcast_to(number, (16, 256))
        return number, jnp.floor((number + (GROUP - 1)) * (1.0 / GROUP))

    over = jnp.zeros((1, 256), f32)
    for other in range(8):
        _, tiles = tiles_of(pages_in(lists - 64 * other))
        over = jnp.maximum(over, jnp.sum(tiles, axis=0, keepdims=True) - SLOTS)
        over = jnp.maximum(over, jnp.sum(tiles[0:8], axis=0, keepdims=True) - SLOTS_A)
    spills[z] = jnp.broadcast_to(over[:, 0:128], (8, 128))

    local = lists - 64 * p
    used = pages_in(local)
    page_t = jnp.transpose(jnp.where(used, local, -1).astype(f32))
    used_t = jnp.where(page_t >= 0, 1.0, 0.0)
    before = jnp.where(
        lax.broadcasted_iota(jnp.int32, (64, 64), 1) < lax.broadcasted_iota(jnp.int32, (64, 64), 0), 1.0, 0.0
    ).astype(bf16)
    place = jnp.where(used_t > 0, jnp.dot(before, used_t.astype(bf16), preferred_element_type=f32), -1.0)
    place_iota = lax.broadcasted_iota(jnp.int32, (64, 128), 1).astype(f32)
    for b in range(16):
        hit = place[:, b:b + 1] == place_iota
        packed = jnp.sum(jnp.where(hit, page_t[:, b:b + 1], 0.0), axis=0, keepdims=True)
        meta_v[b:b + 1, 0:128] = packed.astype(jnp.int32)
    number, tiles = tiles_of(used)
    earlier = jnp.where(
        lax.broadcasted_iota(jnp.int32, (16, 16), 1) < lax.broadcasted_iota(jnp.int32, (16, 16), 0), 1.0, 0.0
    ).astype(bf16)
    start = jnp.dot(earlier, tiles.astype(bf16), preferred_element_type=f32)
    slot = lax.broadcasted_iota(jnp.int32, (16, 256), 1).astype(f32)
    inside = (slot >= start) & (slot < start + tiles)
    branch = lax.broadcasted_iota(jnp.int32, (16, 256), 0).astype(f32)

    def pick(a):
        return jnp.sum(jnp.where(inside, a, 0.0), axis=0, keepdims=True).astype(jnp.int32)

    meta_v[16:17, :] = pick(branch)
    meta_v[17:18, :] = pick((slot - start) * GROUP)
    meta_v[18:19, :] = pick(jnp.clip(number - (slot - start) * GROUP, 0.0, float(GROUP)) * PAGE)
    meta_v[19:20, :] = pick(jnp.where(slot == start, NONE, -NONE))
    ends = jnp.where((tiles > 0) & (start + tiles <= SLOTS), start + tiles, 0.0)
    by_lane = jnp.where(branch == slot, ends, 0.0)
    meta_v[20:21, :] = jnp.sum(by_lane, axis=0, keepdims=True).astype(jnp.int32)
    meta_copy = pltpu.make_async_copy(meta_v, meta_s, own_sems.at[0])
    meta_copy.start()

    loads[4].wait()

    def order(i, carry):
        left = by_owner(q_ref[2 * i].astype(f32))
        right = by_owner(q_ref[2 * i + 1].astype(f32))
        q_rows[2 * i] = jnp.concatenate(left, axis=0).astype(bf16)
        q_rows[2 * i + 1] = jnp.concatenate(right, axis=0).astype(bf16)
        for d in range(8):
            q_send[d, pl.ds(pl.multiple_of(16 * i, 16), 16), :] = jnp.concatenate(
                [left[d], right[d]], axis=0
            ).astype(bf16)
        return carry

    lax.fori_loop(0, 8, order, 0)

    pl.semaphore_wait(barrier, jnp.where(stays, 17, 18))

    q_own = pltpu.make_async_copy(q_send.at[mine], q_all.at[n], own_sems.at[1])
    q_own.start()

    def q_copy(k):
        return pltpu.make_async_remote_copy(
            src_ref=q_send.at[mine], dst_ref=q_all.at[n],
            send_sem=q_sems.at[0, k], recv_sem=q_sems.at[1, n],
            device_id={"narrow": lax.rem(n + k, 4)}, device_id_type=MESH,
        )

    def spill_copy(k):
        return pltpu.make_async_remote_copy(
            src_ref=spills.at[z], dst_ref=spills.at[z],
            send_sem=spill_sems.at[0, k], recv_sem=spill_sems.at[1, z],
            device_id={"batch": lax.rem(z + k, 8)}, device_id_type=MESH,
        )

    for k in (1, 3, 2):
        q_copy(k).start()
    for k in range(1, 8):
        spill_copy(k).start()

    meta_copy.wait()
    loads[5].wait()
    key_iota = lax.broadcasted_iota(jnp.int32, (ROWS, TILE), 1)

    def tile_scores(s, u):
        b = jnp.clip(meta_s[16, s], 0, 15)
        k = jnp.clip(meta_s[17, s], 0, 60)
        live = meta_s[18, s]
        pages = [jnp.clip(meta_s[b, k + i], 0, 63) for i in range(GROUP)]
        keys = jnp.concatenate([cache_ref[page] for page in pages], axis=0)
        score = lax.dot_general(
            q_rows[b], keys, (((1,), (1,)), ((), ())), preferred_element_type=f32
        ) * TO_LOG2
        score = jnp.where(key_iota < live, score, MASKED)
        high = jnp.maximum(jnp.max(score, axis=1, keepdims=True), NONE)
        expo = jnp.exp2(score - high)
        weight[u] = expo.astype(bf16)
        return pages, high, jnp.sum(expo, axis=1, keepdims=True)

    def tile_group(i, carry):
        ready = [tile_scores(i * FUSED + u, u) for u in range(FUSED)]
        for u, (pages, high, total) in enumerate(ready):
            s = i * FUSED + u
            values = jnp.concatenate([cache_ref[page, :, :LAT] for page in pages], axis=0)
            part = jnp.dot(weight[u], values, preferred_element_type=f32)
            old = jnp.minimum(top[s], meta_s[19, s].astype(f32))
            new = jnp.maximum(old, high)
            f_old = jnp.exp2(old - new)
            f_new = jnp.exp2(high - new)
            top[s + 1] = new
            tot[s + 1] = tot[s] * f_old + total * f_new
            acc[s + 1] = acc[s] * wide(f_old) + part * wide(f_new)
        return carry

    lane64 = lax.broadcasted_iota(jnp.int32, (ROWS, 128), 1)

    def pack(i, carry):
        high_all, total_all = carry
        pieces = []
        for b in (2 * i, 2 * i + 1):
            at = jnp.clip(meta_s[20, b], 0, SLOTS)
            code, high, total = coded(acc[at], top[at], tot[at])
            high_all = jnp.where(lane64 == b, high, high_all)
            total_all = jnp.where(lane64 == b, total, total_all)
            pieces.append(code)
        left, right = pieces
        for d in range(8):
            rows = slice(8 * d, 8 * d + 8)
            part_send[d, pl.ds(pl.multiple_of(16 * i, 16), 16), :] = jnp.concatenate(
                [left[rows], right[rows]], axis=0
            ).astype(LINK)
        return high_all, total_all

    def pre_copies(h, k):
        other = lax.rem(p + k, 8)
        to = owner_of(other)
        half = pl.ds(64 * h, 64)
        return [
            pltpu.make_async_remote_copy(
                src_ref=part_send.at[to, half], dst_ref=pre_part.at[p, half],
                send_sem=pre_sems.at[0, h, 0, k], recv_sem=pre_sems.at[1, h, 0, p],
                device_id={"prefix": other}, device_id_type=MESH,
            ),
            pltpu.make_async_remote_copy(
                src_ref=stat_send.at[h, to], dst_ref=pre_stat.at[h, p],
                send_sem=pre_sems.at[0, h, 1, k], recv_sem=pre_sems.at[1, h, 1, p],
                device_id={"prefix": other}, device_id_type=MESH,
            ),
        ]

    def pre_own(h):
        half = pl.ds(64 * h, 64)
        return [
            pltpu.make_async_copy(part_send.at[mine, half], pre_part.at[p, half], own_sems.at[2 + 2 * h]),
            pltpu.make_async_copy(stat_send.at[h, mine], pre_stat.at[h, p], own_sems.at[3 + 2 * h]),
        ]

    for h, (first, last) in enumerate([(0, SLOTS_A), (SLOTS_A, SLOTS)]):
        lax.fori_loop(first // FUSED, last // FUSED, tile_group, 0)
        high_all, total_all = lax.fori_loop(
            4 * h, 4 * h + 4, pack, (jnp.full((ROWS, 128), NONE, f32), jnp.zeros((ROWS, 128), f32))
        )
        for d in range(8):
            stat_send[h, d, 0:8, :] = high_all[8 * d:8 * d + 8]
            stat_send[h, d, 8:16, :] = total_all[8 * d:8 * d + 8]

        def pre_start(k, carry, h=h):
            for copy in pre_copies(h, k):
                copy.start()
            return carry

        lax.fori_loop(1, 8, pre_start, 0)
        for copy in pre_own(h):
            copy.start()

    loads[3].wait()
    for b in range(16):
        at = 2 * (b % 2)
        fresh[b // 2, at:at + 2, :] = new_ref[b]
    key_at = lax.broadcasted_iota(jnp.int32, (ROWS, SPAN), 1)
    row_at = lax.broadcasted_iota(jnp.int32, (ROWS, SPAN), 0)
    side = lax.rem(lax.div(row_at, 8), 2)
    step = lax.rem(lax.div(row_at, 4), 2)
    new_at = key_at - 2 * TILE
    new_live = (new_at >= 2 * side) & (new_at <= 2 * side + step) & (n == 0)
    cached = (key_at < 2 * TILE) & (lax.div(key_at, TILE) == side)
    key_rel[...] = jnp.where(new_live, -(1 << 20), jnp.where(cached, lax.rem(key_at, TILE), 1 << 20))
    q_own.wait()
    for k in range(1, 4):
        source = lax.rem(n + k, 4)
        pltpu.make_async_copy(q_all.at[source], q_all.at[source], q_sems.at[1, source]).wait()
    loads[6].wait()
    lane8 = lax.broadcasted_iota(jnp.int32, (8, 128), 1)
    side_row = lax.rem(lax.div(lax.broadcasted_iota(jnp.int32, (ROWS, SPAN), 0), 8), 2)

    def mix_copies(h, k):
        other = lax.rem(n + k, 4)
        half = pl.ds(64 * h, 64)
        return [
            pltpu.make_async_remote_copy(
                src_ref=mix_send.at[other, half], dst_ref=mix_part.at[n, half],
                send_sem=mix_sems.at[0, h, 0, k], recv_sem=mix_sems.at[1, h, 0, n],
                device_id={"narrow": other}, device_id_type=MESH,
            ),
            pltpu.make_async_remote_copy(
                src_ref=mix_stat_send.at[h, other], dst_ref=mix_stat.at[h, n],
                send_sem=mix_sems.at[0, h, 1, k], recv_sem=mix_sems.at[1, h, 1, n],
                device_id={"narrow": other}, device_id_type=MESH,
            ),
        ]

    def mix_own(h):
        half = pl.ds(64 * h, 64)
        return [
            pltpu.make_async_copy(mix_send.at[n, half], mix_part.at[n, half], own_sems.at[6 + 2 * h]),
            pltpu.make_async_copy(mix_stat_send.at[h, n], mix_stat.at[h, n], own_sems.at[7 + 2 * h]),
        ]

    def mix_scores(i, u):
        rows = pl.ds(pl.multiple_of(16 * i, 16), 16)
        queries = jnp.concatenate([q_all[m, rows, :] for m in range(4)], axis=0)
        keys = jnp.concatenate([suffix_ref[2 * i], suffix_ref[2 * i + 1], fresh[i]], axis=0)
        score = lax.dot_general(
            queries, keys, (((1,), (1,)), ((), ())), preferred_element_type=f32
        ) * TO_LOG2
        limit = jnp.where(side_row == 0, len_ref[2 * i] - n * TILE, len_ref[2 * i + 1] - n * TILE)
        score = jnp.where(key_rel[...] < limit, score, MASKED)
        high = jnp.maximum(jnp.max(score, axis=1, keepdims=True), NONE)
        expo = jnp.exp2(score - high)
        weight2[u] = expo.astype(bf16)
        return high, jnp.sum(expo, axis=1, keepdims=True)

    def mix_pairs(g, carry):
        stats = list(carry)
        ready = [mix_scores(2 * g + u, u) for u in range(2)]
        for u, (high, total) in enumerate(ready):
            i = 2 * g + u
            values = jnp.concatenate(
                [suffix_ref[2 * i, :, :LAT], suffix_ref[2 * i + 1, :, :LAT], fresh[i, :, :LAT]], axis=0
            )
            part = jnp.dot(weight2[u], values, preferred_element_type=f32)
            code, high, total = coded(part, high, total)
            rows = pl.ds(pl.multiple_of(16 * i, 16), 16)
            for m in range(4):
                mix_send[m, rows, :] = code[16 * m:16 * m + 16].astype(LINK)
                for at, value in ((m, high), (m + 4, total)):
                    for j in range(2):
                        piece = value[16 * m + 8 * j:16 * m + 8 * j + 8]
                        stats[at] = jnp.where(lane8 == 2 * i + j, piece, stats[at])
        return tuple(stats)

    for h in range(2):
        stats = lax.fori_loop(
            2 * h, 2 * h + 2, mix_pairs,
            tuple([jnp.full((8, 128), NONE, f32)] * 4 + [jnp.zeros((8, 128), f32)] * 4),
        )
        for m in range(4):
            mix_stat_send[h, m, 0:8, :] = stats[m]
            mix_stat_send[h, m, 8:16, :] = stats[4 + m]
        for k in (2, 1, 3):
            for copy in mix_copies(h, k):
                copy.start()
        for copy in mix_own(h):
            copy.start()

    def send_on(h):
        half = pl.ds(64 * h, 64)
        return pltpu.make_async_remote_copy(
            src_ref=done.at[half], dst_ref=out_ref.at[half],
            send_sem=end_sems.at[0, h], recv_sem=end_sems.at[1, h],
            device_id=across, device_id_type=MESH,
        )

    for h in range(2):
        half = pl.ds(64 * h, 64)
        for copy in pre_own(h) + mix_own(h):
            copy.wait()

        def pre_wait(k, carry, h=h, half=half):
            source = lax.rem(p + k, 8)
            landed = pre_part.at[source, half]
            noted = pre_stat.at[h, source]
            pltpu.make_async_copy(landed, landed, pre_sems.at[1, h, 0, source]).wait()
            pltpu.make_async_copy(noted, noted, pre_sems.at[1, h, 1, source]).wait()
            return carry

        lax.fori_loop(1, 8, pre_wait, 0)
        for k in range(1, 4):
            source = lax.rem(n + k, 4)
            landed = mix_part.at[source, half]
            noted = mix_stat.at[h, source]
            pltpu.make_async_copy(landed, landed, mix_sems.at[1, h, 0, source]).wait()
            pltpu.make_async_copy(noted, noted, mix_sems.at[1, h, 1, source]).wait()

        highs = [pre_stat[h, i, 0:8, :] for i in range(8)] + [mix_stat[h, m, 0:8, :] for m in range(4)]
        totals = [pre_stat[h, i, 8:16, :] for i in range(8)] + [mix_stat[h, m, 8:16, :] for m in range(4)]
        highest = functools.reduce(jnp.maximum, highs)
        factors = [jnp.exp2(high - highest) for high in highs]
        total = sum(f * t for f, t in zip(factors, totals))
        inverse = 1.0 / jnp.where(lax.div(lane8, 8) == h, total, 1.0)
        factors = [f * inverse for f in factors]
        for i in range(4 * h, 4 * h + 4):
            rows = slice(16 * i, 16 * i + 16)
            value = jnp.zeros((16, LAT), f32)
            for at, f in enumerate(factors):
                source = pre_part[at, rows, :] if at < 8 else mix_part[at - 8, rows, :]
                scale = jnp.concatenate([f[:, 2 * i:2 * i + 1], f[:, 2 * i + 1:2 * i + 2]], axis=0)
                value = value + source.astype(f32) * scale
            done[rows, :] = value.astype(bf16)

        @pl.when(stays)
        def _(half=half):
            out_ref[half, :] = done[half, :]

        @pl.when(jnp.logical_not(stays))
        def _(h=h):
            send_on(h).start()

    for k in range(1, 8):
        source = lax.rem(z + k, 8)
        pltpu.make_async_copy(spills.at[source], spills.at[source], spill_sems.at[1, source]).wait()
    spill_ref[...] = functools.reduce(jnp.maximum, [spills[i] for i in range(8)])
    for k in range(1, 8):
        spill_copy(k).wait_send()
    for k in range(1, 4):
        q_copy(k).wait_send()
    for h in range(2):
        def pre_sent(k, carry, h=h):
            for copy in pre_copies(h, k):
                copy.wait_send()
            return carry

        lax.fori_loop(1, 8, pre_sent, 0)
        for k in range(1, 4):
            for copy in mix_copies(h, k):
                copy.wait_send()

    @pl.when(jnp.logical_not(stays))
    def _():
        send_on(0).wait()
        send_on(1).wait()


def fused(counts, lens, lists, new_latent, queries, cache, suffix):
    dma = pltpu.SemaphoreType.DMA
    f32, bf16, i32 = jnp.float32, jnp.bfloat16, jnp.int32
    return pl.pallas_call(
        fused_kernel,
        out_shape=(
            jax.ShapeDtypeStruct((128, LAT), bf16),
            jax.ShapeDtypeStruct((8, 128), f32),
        ),
        in_specs=[pl.BlockSpec(memory_space=pl.ANY)] * 7,
        out_specs=(pl.BlockSpec(memory_space=pltpu.VMEM),) * 2,
        scratch_shapes=[
            pltpu.SMEM((16,), i32),
            pltpu.SMEM((16,), i32),
            pltpu.VMEM((16, 64), i32),
            pltpu.VMEM((16, 2, KV), bf16),
            pltpu.VMEM((16, ROWS, KV), bf16),
            pltpu.VMEM((16, ROWS, KV), bf16),
            pltpu.VMEM((8, 128, KV), bf16),
            pltpu.VMEM((4, 128, KV), bf16),
            pltpu.VMEM((64, PAGE, KV), bf16),
            pltpu.VMEM((16, TILE, KV), bf16),
            pltpu.VMEM((8, 16, KV), bf16),
            pltpu.VMEM((24, 256), i32),
            pltpu.SMEM((24, 256), i32),
            pltpu.VMEM((SLOTS + 1, ROWS, LAT), f32),
            pltpu.VMEM((SLOTS + 1, ROWS, 128), f32),
            pltpu.VMEM((SLOTS + 1, ROWS, 128), f32),
            pltpu.VMEM((FUSED, ROWS, TILE), bf16),
            pltpu.VMEM((2, ROWS, SPAN), bf16),
            pltpu.VMEM((ROWS, SPAN), i32),
            pltpu.VMEM((8, 128, LAT), LINK),
            pltpu.VMEM((2, 8, 16, 128), f32),
            pltpu.VMEM((8, 128, LAT), LINK),
            pltpu.VMEM((2, 8, 16, 128), f32),
            pltpu.VMEM((4, 128, LAT), LINK),
            pltpu.VMEM((2, 4, 16, 128), f32),
            pltpu.VMEM((4, 128, LAT), LINK),
            pltpu.VMEM((2, 4, 16, 128), f32),
            pltpu.VMEM((128, LAT), bf16),
            pltpu.VMEM((8, 8, 128), f32),
            dma((7,)),
            dma((10,)),
            dma((2, 4)),
            dma((2, 2, 2, 8)),
            dma((2, 2, 2, 4)),
            dma((2, 2)),
            dma((2, 8)),
        ],
        compiler_params=pltpu.CompilerParams(
            collective_id=1, has_side_effects=True, vmem_limit_bytes=60 << 20
        ),
        name="fused",
    )(counts, lens, lists, new_latent, queries, cache, suffix)


def local(queries, new_latent, prefix_cache, suffix_cache, page_lists, prefix_count, suffix_len):
    rows = queries.reshape(16, ROWS, KV)
    suffix = suffix_cache.reshape(16, TILE, KV)
    out, spill = fused(prefix_count, suffix_len, page_lists, new_latent, rows, prefix_cache, suffix)

    def again():
        part, stat = prefix_part(prefix_count, page_lists, rows, prefix_cache)
        return join(suffix_len, new_latent, rows, suffix, part, stat).reshape(16, 2, 4, LAT)

    return lax.cond(spill[0, 0] > 0, again, lambda: out.reshape(16, 2, 4, LAT))


def solution(mesh):
    return jax.shard_map(
        local,
        mesh=mesh,
        in_specs=(
            P("batch", None, "narrow", None),
            P("batch", None, None),
            P("prefix", None, None),
            P("batch", "narrow", None, None),
            P("batch", None),
            P("batch"),
            P("batch"),
        ),
        out_specs=P("batch", None, ("prefix", "narrow"), None),
        check_vma=False,
    )
```

```python
import functools

import jax
import jax.numpy as jnp
from jax import lax
from jax.experimental import pallas as pl
from jax.experimental.pallas import tpu as pltpu
from jax.sharding import PartitionSpec as P

MESH = pl.DeviceIdType.MESH
LAT = 512
KV = 576
PAGE = 64
ROWS = 64
GROUP = 4
TILE = GROUP * PAGE
UNROLL = 4
NONE = -30000.0
MASKED = -1e30
TO_LOG2 = 192 ** -0.5 * 1.4426950408889634
LINK = jnp.int16
STEPS_OF = 32767.0
SMALL = 1e-28


def by_owner(a):
    width = a.shape[-1]
    first = a[:32].reshape(4, 8, width)
    second = a[32:].reshape(4, 8, width)
    low = lax.broadcasted_iota(jnp.int32, (4, 8, width), 1) < 4
    even = jnp.where(low, first, pltpu.roll(second, 4, 1))
    odd = jnp.where(low, pltpu.roll(first, 4, 1), second)
    return [(even if d % 2 == 0 else odd)[d // 2] for d in range(8)]


def coded(part, high, total):
    largest = jnp.maximum(jnp.max(jnp.abs(part), axis=1, keepdims=True), SMALL)
    code = jnp.round(part * (STEPS_OF / largest)).astype(jnp.int32)
    return code, high + jnp.log2(largest * (1.0 / STEPS_OF)), total * (STEPS_OF / largest)


def wide(a):
    return jnp.concatenate([a] * 4, axis=1)


def owner_of(prefix):
    return 4 * lax.rem(prefix, 2) + lax.div(prefix, 2)


SLOTS_A = 20
SLOTS = 32
SPAN = 2 * TILE
FUSED = 4


def by_lane(column):
    row = lax.broadcasted_iota(jnp.int32, (16, 256), 0)
    lane = lax.broadcasted_iota(jnp.int32, (16, 256), 1)
    return jnp.sum(jnp.where(row == lane, column, 0.0), axis=0, keepdims=True).astype(jnp.int32)


def tile_plan(lists, count_ref, base):
    f32 = jnp.float32
    row = lax.broadcasted_iota(jnp.int32, (16, 64), 0)
    col = lax.broadcasted_iota(jnp.int32, (16, 64), 1)
    counts = jnp.zeros((16, 64), jnp.int32)
    for b in range(16):
        counts = jnp.where(row == b, count_ref[b], counts)
    local = lists - base
    used = (col < counts) & (local >= 0) & (local < 64)
    number = jnp.sum(jnp.where(used, 1.0, 0.0), axis=1, keepdims=True)
    number = jnp.broadcast_to(number, (16, 256))
    tiles = jnp.floor((number + (GROUP - 1)) * (1.0 / GROUP))
    earlier = jnp.where(
        lax.broadcasted_iota(jnp.int32, (16, 16), 1) < lax.broadcasted_iota(jnp.int32, (16, 16), 0), 1.0, 0.0
    ).astype(jnp.bfloat16)
    start = jnp.dot(earlier, tiles.astype(jnp.bfloat16), preferred_element_type=f32)
    room = jnp.where(lax.broadcasted_iota(jnp.int32, (16, 256), 0) < 8, float(SLOTS_A), float(SLOTS))
    kept = jnp.clip(room - start, 0.0, tiles)
    return local, used, number, tiles, start, kept


def pack_pages(meta_v, local, used):
    f32 = jnp.float32
    page_t = jnp.transpose(jnp.where(used, local, -1).astype(f32))
    used_t = jnp.where(page_t >= 0, 1.0, 0.0)
    before = jnp.where(
        lax.broadcasted_iota(jnp.int32, (64, 64), 1) < lax.broadcasted_iota(jnp.int32, (64, 64), 0), 1.0, 0.0
    ).astype(jnp.bfloat16)
    rank = jnp.dot(before, used_t.astype(jnp.bfloat16), preferred_element_type=f32)
    place = jnp.where(used_t > 0, rank, -1.0)
    place_iota = lax.broadcasted_iota(jnp.int32, (64, 128), 1).astype(f32)
    for b in range(16):
        hit = place[:, b:b + 1] == place_iota
        packed = jnp.sum(jnp.where(hit, page_t[:, b:b + 1], 0.0), axis=0, keepdims=True)
        meta_v[b:b + 1, 0:128] = packed.astype(jnp.int32)


def spill_kernel(
    count_any, lists_any, q_any, cache_any, out_any,
    count_ref, lists_ref, q_ref, cache_ref, meta_v, meta_s, acc, stat, sems,
):
    f32 = jnp.float32
    loads = [
        pltpu.make_async_copy(count_any, count_ref, sems.at[0]),
        pltpu.make_async_copy(lists_any, lists_ref, sems.at[1]),
    ]
    for copy in loads:
        copy.start()
    for copy in loads:
        copy.wait()
    local, used, number, tiles, start, kept = tile_plan(
        lists_ref[...], count_ref, lax.axis_index("prefix") * 64
    )

    @pl.when(jnp.max(tiles - kept) > 0.5)
    def _():
        large = [
            pltpu.make_async_copy(q_any, q_ref, sems.at[0]),
            pltpu.make_async_copy(cache_any, cache_ref, sems.at[1]),
        ]
        for copy in large:
            copy.start()
        meta_v[...] = jnp.zeros_like(meta_v)
        pack_pages(meta_v, local, used)
        meta_v[16:17, :] = by_lane(kept)
        meta_v[17:18, :] = by_lane(tiles)
        meta_v[18:19, :] = by_lane(number)
        noted = pltpu.make_async_copy(meta_v, meta_s, sems.at[2])
        noted.start()
        noted.wait()
        for copy in large:
            copy.wait()
        key_iota = lax.broadcasted_iota(jnp.int32, (ROWS, TILE), 1)

        def branch(b, carry):
            acc[b] = jnp.zeros((ROWS, LAT), f32)
            stat[0, b] = jnp.full((ROWS, 128), NONE, f32)
            stat[1, b] = jnp.zeros((ROWS, 128), f32)

            def tile(k, carry):
                at = GROUP * k
                keys = jnp.concatenate([cache_ref[meta_s[b, at + i]] for i in range(GROUP)], axis=0)
                score = lax.dot_general(
                    q_ref[b], keys, (((1,), (1,)), ((), ())), preferred_element_type=f32
                ) * TO_LOG2
                score = jnp.where(key_iota < (meta_s[18, b] - at) * PAGE, score, MASKED)
                high = jnp.maximum(jnp.max(score, axis=1, keepdims=True), NONE)
                expo = jnp.exp2(score - high)
                total = jnp.sum(expo, axis=1, keepdims=True)
                part = jnp.dot(expo.astype(jnp.bfloat16), keys[:, :LAT], preferred_element_type=f32)
                old = stat[0, b]
                new = jnp.maximum(old, high)
                f_old = jnp.exp2(old - new)
                f_new = jnp.exp2(high - new)
                stat[0, b] = new
                stat[1, b] = stat[1, b] * f_old + total * f_new
                acc[b] = acc[b] * wide(f_old) + part * wide(f_new)
                return carry

            lax.fori_loop(meta_s[16, b], meta_s[17, b], tile, 0)
            acc[b] = jnp.concatenate(by_owner(acc[b]), axis=0)
            stat[0, b] = jnp.concatenate(by_owner(stat[0, b]), axis=0)
            stat[1, b] = jnp.concatenate(by_owner(stat[1, b]), axis=0)
            return carry

        lax.fori_loop(0, 16, branch, 0)
        out = [
            pltpu.make_async_copy(acc, out_any.at[:, :, 0:LAT], sems.at[0]),
            pltpu.make_async_copy(stat.at[0], out_any.at[:, :, LAT:LAT + 128], sems.at[1]),
            pltpu.make_async_copy(stat.at[1], out_any.at[:, :, LAT + 128:LAT + 256], sems.at[2]),
        ]
        for copy in out:
            copy.start()
        for copy in out:
            copy.wait()


def spill(counts, lists, queries, cache):
    return pl.pallas_call(
        spill_kernel,
        out_shape=jax.ShapeDtypeStruct((16, ROWS, 2048), jnp.float32),
        in_specs=[pl.BlockSpec(memory_space=pl.ANY)] * 4,
        out_specs=pl.BlockSpec(memory_space=pl.ANY),
        scratch_shapes=[
            pltpu.SMEM((16,), jnp.int32),
            pltpu.VMEM((16, 64), jnp.int32),
            pltpu.VMEM((16, ROWS, KV), jnp.bfloat16),
            pltpu.VMEM((64, PAGE, KV), jnp.bfloat16),
            pltpu.VMEM((24, 256), jnp.int32),
            pltpu.SMEM((24, 256), jnp.int32),
            pltpu.VMEM((16, ROWS, LAT), jnp.float32),
            pltpu.VMEM((2, 16, ROWS, 128), jnp.float32),
            pltpu.SemaphoreType.DMA((3,)),
        ],
        compiler_params=pltpu.CompilerParams(vmem_limit_bytes=60 << 20),
        name="spill",
    )(counts, lists, queries, cache)


def fused_kernel(
    count_any, len_any, lists_any, new_any, q_any, cache_any, suffix_any, spill_any, out_ref,
    count_ref, len_ref, lists_ref, new_ref, q_ref, q_rows, q_send, q_all, cache_ref, suffix_ref,
    meta_v, meta_s, acc, top, tot, weight, weight2, key_rel,
    part_send, stat_send, core_part, core_stat, row_send, row_stat_send, pre_part, pre_stat, mix_send, mix_stat_send, mix_part, mix_stat, done,
    in_sems, own_sems, q_sems, core_sems, pre_sems, mix_sems, end_sems,
):
    f32 = jnp.float32
    bf16 = jnp.bfloat16
    p = lax.axis_index("prefix")
    n = lax.axis_index("narrow")
    x = lax.div(p, 2)
    c = lax.rem(p, 2)
    mine = owner_of(p)
    stays = x == n
    across = {"prefix": 2 * n + c, "narrow": x}

    loads = [
        pltpu.make_async_copy(source, target, in_sems.at[k])
        for k, (source, target) in enumerate([
            (count_any, count_ref), (len_any, len_ref), (lists_any, lists_ref), (new_any, new_ref),
            (q_any, q_ref), (cache_any, cache_ref), (suffix_any, suffix_ref),
            (spill_any.at[:, :, 0:LAT], acc.at[pl.ds(SLOTS + 1, 16)]),
            (spill_any.at[:, :, LAT:LAT + 128], top.at[pl.ds(SLOTS + 1, 16)]),
            (spill_any.at[:, :, LAT + 128:LAT + 256], tot.at[pl.ds(SLOTS + 1, 16)]),
        ])
    ]
    barrier = pltpu.get_barrier_semaphore()

    def greet(**to):
        pl.semaphore_signal(barrier, inc=1, device_id=to, device_id_type=MESH)

    greet(prefix=2 * x + 1 - c)
    for k in range(1, 4):
        greet(prefix=2 * lax.rem(x + k, 4) + c)
        greet(narrow=lax.rem(n + k, 4))

    @pl.when(jnp.logical_not(stays))
    def _():
        greet(**across)

    for k in (0, 2, 4, 5, 1):
        loads[k].start()

    meta_v[...] = jnp.zeros_like(meta_v)
    acc[0] = jnp.zeros((ROWS, LAT), f32)
    top[0] = jnp.full((ROWS, 128), NONE, f32)
    tot[0] = jnp.zeros((ROWS, 128), f32)
    loads[0].wait()
    loads[2].wait()
    local, used, number, tiles, start, kept = tile_plan(lists_ref[...], count_ref, 64 * p)
    pack_pages(meta_v, local, used)
    slot = lax.broadcasted_iota(jnp.int32, (16, 256), 1).astype(f32)
    inside = (slot >= start) & (slot < start + tiles)
    branch = lax.broadcasted_iota(jnp.int32, (16, 256), 0).astype(f32)

    def pick(a):
        return jnp.sum(jnp.where(inside, a, 0.0), axis=0, keepdims=True).astype(jnp.int32)

    meta_v[16:17, :] = pick(branch)
    meta_v[17:18, :] = pick((slot - start) * GROUP)
    meta_v[18:19, :] = pick(jnp.clip(number - (slot - start) * GROUP, 0.0, float(GROUP)) * PAGE)
    meta_v[19:20, :] = pick(jnp.where(slot == start, NONE, -NONE))
    meta_v[20:21, :] = by_lane(jnp.where(kept > 0, start + kept, 0.0))
    meta_v[21:22, :] = by_lane(jnp.where(tiles > kept, branch + (SLOTS + 1.0), 0.0))
    meta_copy = pltpu.make_async_copy(meta_v, meta_s, own_sems.at[0])
    meta_copy.start()

    loads[4].wait()

    def order(i, carry):
        left = by_owner(q_ref[2 * i].astype(f32))
        right = by_owner(q_ref[2 * i + 1].astype(f32))
        q_rows[2 * i] = jnp.concatenate(left, axis=0).astype(bf16)
        q_rows[2 * i + 1] = jnp.concatenate(right, axis=0).astype(bf16)
        for d in range(8):
            q_send[d, pl.ds(pl.multiple_of(16 * i, 16), 16), :] = jnp.concatenate(
                [left[d], right[d]], axis=0
            ).astype(bf16)
        return carry

    def q_own(h):
        half = pl.ds(64 * h, 64)
        return pltpu.make_async_copy(q_send.at[mine, half], q_all.at[n, half], own_sems.at[1 + h])

    def q_copy(h, k):
        half = pl.ds(64 * h, 64)
        return pltpu.make_async_remote_copy(
            src_ref=q_send.at[mine, half], dst_ref=q_all.at[n, half],
            send_sem=q_sems.at[0, h, k], recv_sem=q_sems.at[1, h, n],
            device_id={"narrow": lax.rem(n + k, 4)}, device_id_type=MESH,
        )

    lax.fori_loop(0, 4, order, 0)
    pl.semaphore_wait(barrier, jnp.where(stays, 7, 8))
    for k in (2, 1, 3):
        q_copy(0, k).start()
    lax.fori_loop(4, 8, order, 0)
    for k in (2, 1, 3):
        q_copy(1, k).start()
    for h in range(2):
        q_own(h).start()

    meta_copy.wait()
    loads[5].wait()
    for k in (6, 3, 7, 8, 9):
        loads[k].start()
    key_iota = lax.broadcasted_iota(jnp.int32, (ROWS, TILE), 1)

    def tile_scores(s, u):
        b = jnp.clip(meta_s[16, s], 0, 15)
        k = jnp.clip(meta_s[17, s], 0, 60)
        live = meta_s[18, s]
        pages = [jnp.clip(meta_s[b, k + i], 0, 63) for i in range(GROUP)]
        keys = jnp.concatenate([cache_ref[page] for page in pages], axis=0)
        score = lax.dot_general(
            q_rows[b], keys, (((1,), (1,)), ((), ())), preferred_element_type=f32
        ) * TO_LOG2
        score = jnp.where(key_iota < live, score, MASKED)
        high = jnp.maximum(jnp.max(score, axis=1, keepdims=True), NONE)
        expo = jnp.exp2(score - high)
        weight[u] = expo.astype(bf16)
        return pages, high, jnp.sum(expo, axis=1, keepdims=True)

    def tile_group(i, carry):
        ready = [tile_scores(i * FUSED + u, u) for u in range(FUSED)]
        for u, (pages, high, total) in enumerate(ready):
            s = i * FUSED + u
            values = jnp.concatenate([cache_ref[page, :, :LAT] for page in pages], axis=0)
            part = jnp.dot(weight[u], values, preferred_element_type=f32)
            old = jnp.minimum(top[s], meta_s[19, s].astype(f32))
            new = jnp.maximum(old, high)
            f_old = jnp.exp2(old - new)
            f_new = jnp.exp2(high - new)
            top[s + 1] = new
            tot[s + 1] = tot[s] * f_old + total * f_new
            acc[s + 1] = acc[s] * wide(f_old) + part * wide(f_new)
        return carry

    lane64 = lax.broadcasted_iota(jnp.int32, (ROWS, 128), 1)

    def pack(i, carry):
        high_all, total_all = carry
        pieces = []
        for b in (2 * i, 2 * i + 1):
            at = jnp.clip(meta_s[20, b], 0, SLOTS)
            more = jnp.clip(meta_s[21, b], 0, SLOTS + 16)
            high = jnp.maximum(top[at], top[more])
            f_at = jnp.exp2(top[at] - high)
            f_more = jnp.exp2(top[more] - high)
            part = acc[at] * wide(f_at) + acc[more] * wide(f_more)
            code, high, total = coded(part, high, tot[at] * f_at + tot[more] * f_more)
            high_all = jnp.where(lane64 == b, high, high_all)
            total_all = jnp.where(lane64 == b, total, total_all)
            pieces.append(code)
        left, right = pieces
        for d in range(8):
            rows = slice(8 * d, 8 * d + 8)
            part_send[d, pl.ds(pl.multiple_of(16 * i, 16), 16), :] = jnp.concatenate(
                [left[rows], right[rows]], axis=0
            ).astype(LINK)
        return high_all, total_all

    def core_copies(h):
        other = 4 * (1 - c)
        half = pl.ds(64 * h, 64)
        return [
            pltpu.make_async_remote_copy(
                src_ref=part_send.at[pl.ds(other, 4), half], dst_ref=core_part.at[:, half],
                send_sem=core_sems.at[0, h, 0], recv_sem=core_sems.at[1, h, 0],
                device_id={"prefix": 2 * x + 1 - c}, device_id_type=MESH,
            ),
            pltpu.make_async_remote_copy(
                src_ref=stat_send.at[h, pl.ds(other, 4)], dst_ref=core_stat.at[h],
                send_sem=core_sems.at[0, h, 1], recv_sem=core_sems.at[1, h, 1],
                device_id={"prefix": 2 * x + 1 - c}, device_id_type=MESH,
            ),
        ]

    def pre_copies(h, k):
        other = lax.rem(x + k, 4)
        half = pl.ds(64 * h, 64)
        return [
            pltpu.make_async_remote_copy(
                src_ref=row_send.at[other, half], dst_ref=pre_part.at[x, half],
                send_sem=pre_sems.at[0, h, 0, k], recv_sem=pre_sems.at[1, h, 0, x],
                device_id={"prefix": 2 * other + c}, device_id_type=MESH,
            ),
            pltpu.make_async_remote_copy(
                src_ref=row_stat_send.at[h, other], dst_ref=pre_stat.at[h, x],
                send_sem=pre_sems.at[0, h, 1, k], recv_sem=pre_sems.at[1, h, 1, x],
                device_id={"prefix": 2 * other + c}, device_id_type=MESH,
            ),
        ]

    def pre_own(h):
        half = pl.ds(64 * h, 64)
        return [
            pltpu.make_async_copy(row_send.at[x, half], pre_part.at[x, half], pre_sems.at[0, h, 0, 0]),
            pltpu.make_async_copy(row_stat_send.at[h, x], pre_stat.at[h, x], pre_sems.at[0, h, 1, 0]),
        ]

    def pack_half(h):
        high_all, total_all = lax.fori_loop(
            4 * h, 4 * h + 4, pack, (jnp.full((ROWS, 128), NONE, f32), jnp.zeros((ROWS, 128), f32))
        )
        for d in range(8):
            stat_send[h, d, 0:8, :] = high_all[8 * d:8 * d + 8]
            stat_send[h, d, 8:16, :] = total_all[8 * d:8 * d + 8]
        for copy in core_copies(h):
            copy.start()

    def join_cores(h):
        for copy in core_copies(h):
            copy.wait_recv()

        def one_owner(to, carry):
            d = 4 * c + to
            high_a, high_b = stat_send[h, d, 0:8, :], core_stat[h, to, 0:8, :]
            high = jnp.maximum(high_a, high_b)
            f_a, f_b = jnp.exp2(high_a - high) * 0.5, jnp.exp2(high_b - high) * 0.5
            row_stat_send[h, to, 0:8, :] = high + 1.0
            row_stat_send[h, to, 8:16, :] = f_a * stat_send[h, d, 8:16, :] + f_b * core_stat[h, to, 8:16, :]
            for i in range(4 * h, 4 * h + 4):
                rows = slice(16 * i, 16 * i + 16)

                def column(a):
                    return jnp.concatenate([a[:, 2 * i + j:2 * i + j + 1] for j in range(2)], axis=0)

                value = (
                    part_send[d, rows, :].astype(f32) * column(f_a)
                    + core_part[to, rows, :].astype(f32) * column(f_b)
                )
                row_send[to, rows, :] = jnp.round(value).astype(jnp.int32).astype(LINK)
            return carry

        lax.fori_loop(0, 4, one_owner, 0)
        for k in (2, 1, 3):
            for copy in pre_copies(h, k):
                copy.start()
        for copy in pre_own(h):
            copy.start()

    lane8 = lax.broadcasted_iota(jnp.int32, (8, 128), 1)
    lax.fori_loop(0, SLOTS_A // FUSED, tile_group, 0)
    for k in (7, 8, 9):
        loads[k].wait()
    pack_half(0)
    lax.fori_loop(SLOTS_A // FUSED, SLOTS // FUSED - 1, tile_group, 0)
    join_cores(0)
    lax.fori_loop(SLOTS // FUSED - 1, SLOTS // FUSED, tile_group, 0)
    pack_half(1)

    key_at = lax.broadcasted_iota(jnp.int32, (ROWS, SPAN), 1)
    side = lax.rem(lax.div(lax.broadcasted_iota(jnp.int32, (ROWS, SPAN), 0), 8), 2)
    key_rel[...] = jnp.where(lax.div(key_at, TILE) == side, lax.rem(key_at, TILE), 1 << 20)
    loads[1].wait()
    loads[6].wait()

    def q_arrived(h):
        q_own(h).wait()
        half = pl.ds(64 * h, 64)
        for k in range(1, 4):
            source = lax.rem(n + k, 4)
            landed = q_all.at[source, half]
            pltpu.make_async_copy(landed, landed, q_sems.at[1, h, source]).wait()


    def quarter(g):
        return pl.ds(pl.multiple_of(32 * g, 32), 32)

    def mix_copies(g, k):
        other = lax.rem(n + k, 4)
        return [
            pltpu.make_async_remote_copy(
                src_ref=mix_send.at[other, quarter(g)], dst_ref=mix_part.at[n, quarter(g)],
                send_sem=mix_sems.at[0, g, 0, k], recv_sem=mix_sems.at[1, g, 0, n],
                device_id={"narrow": other}, device_id_type=MESH,
            ),
            pltpu.make_async_remote_copy(
                src_ref=mix_stat_send.at[g, other], dst_ref=mix_stat.at[g, n],
                send_sem=mix_sems.at[0, g, 1, k], recv_sem=mix_sems.at[1, g, 1, n],
                device_id={"narrow": other}, device_id_type=MESH,
            ),
        ]

    def mix_own(g):
        return [
            pltpu.make_async_copy(mix_send.at[n, quarter(g)], mix_part.at[n, quarter(g)], mix_sems.at[0, g, 0, 0]),
            pltpu.make_async_copy(mix_stat_send.at[g, n], mix_stat.at[g, n], mix_sems.at[0, g, 1, 0]),
        ]

    def mix_scores(i, u):
        rows = pl.ds(pl.multiple_of(16 * i, 16), 16)
        queries = jnp.concatenate([q_all[m, rows, :] for m in range(4)], axis=0)
        keys = jnp.concatenate([suffix_ref[2 * i], suffix_ref[2 * i + 1]], axis=0)
        score = lax.dot_general(
            queries, keys, (((1,), (1,)), ((), ())), preferred_element_type=f32
        ) * TO_LOG2
        limit = jnp.where(side == 0, len_ref[2 * i] - n * TILE, len_ref[2 * i + 1] - n * TILE)
        score = jnp.where(key_rel[...] < limit, score, MASKED)
        high = jnp.maximum(jnp.max(score, axis=1, keepdims=True), NONE)
        expo = jnp.exp2(score - high)
        weight2[u] = expo.astype(bf16)
        return high, jnp.sum(expo, axis=1, keepdims=True)

    def mix_pairs(g, carry):
        stats = [jnp.full((8, 128), NONE, f32)] * 4 + [jnp.zeros((8, 128), f32)] * 4
        ready = [mix_scores(2 * g + u, u) for u in range(2)]
        for u, (high, total) in enumerate(ready):
            i = 2 * g + u
            values = jnp.concatenate([suffix_ref[2 * i, :, :LAT], suffix_ref[2 * i + 1, :, :LAT]], axis=0)
            part = jnp.dot(weight2[u], values, preferred_element_type=f32)
            code, high, total = coded(part, high, total)
            rows = pl.ds(pl.multiple_of(16 * i, 16), 16)
            for m in range(4):
                mix_send[m, rows, :] = code[16 * m:16 * m + 16].astype(LINK)
                for at, value in ((m, high), (m + 4, total)):
                    for j in range(2):
                        piece = value[16 * m + 8 * j:16 * m + 8 * j + 8]
                        stats[at] = jnp.where(lane8 == 2 * i + j, piece, stats[at])
        for m in range(4):
            mix_stat_send[g, m, 0:8, :] = stats[m]
            mix_stat_send[g, m, 8:16, :] = stats[4 + m]
        for k in (2, 1, 3):
            for copy in mix_copies(g, k):
                copy.start()
        for copy in mix_own(g):
            copy.start()
        return carry

    q_arrived(0)
    lax.fori_loop(0, 2, mix_pairs, 0)
    join_cores(1)
    q_arrived(1)
    lax.fori_loop(2, 4, mix_pairs, 0)

    loads[3].wait()
    step8 = lax.broadcasted_iota(jnp.int32, (8, 1), 0) >= 4

    def new_scores(i, carry):
        queries = q_send[mine, pl.ds(pl.multiple_of(16 * i, 16), 16), :].astype(f32)
        out = list(carry)
        for j in range(2):
            keys = new_ref[2 * i + j].astype(f32)
            for u in range(2):
                score = jnp.sum(queries[8 * j:8 * j + 8] * keys[u:u + 1], axis=1, keepdims=True) * TO_LOG2
                if u == 1:
                    score = jnp.where(step8, score, NONE)
                out[u] = jnp.where(lane8 == 2 * i + j, score, out[u])
        return tuple(out)

    new_highs = lax.fori_loop(0, 8, new_scores, tuple([jnp.full((8, 128), NONE, f32)] * 2))

    def send_on(g):
        return pltpu.make_async_remote_copy(
            src_ref=done.at[pl.ds(4 * g, 4)], dst_ref=out_ref.at[pl.ds(4 * g, 4)],
            send_sem=end_sems.at[0, g], recv_sem=end_sems.at[1, g],
            device_id=across, device_id_type=MESH,
        )

    for g in range(4):
        h = g // 2
        if g % 2 == 0:
            half = pl.ds(64 * h, 64)
            for copy in pre_own(h):
                copy.wait()

            for k in range(1, 4):
                source = lax.rem(x + k, 4)
                landed = pre_part.at[source, half]
                noted = pre_stat.at[h, source]
                pltpu.make_async_copy(landed, landed, pre_sems.at[1, h, 0, source]).wait()
                pltpu.make_async_copy(noted, noted, pre_sems.at[1, h, 1, source]).wait()
        for copy in mix_own(g):
            copy.wait()
        for k in range(1, 4):
            source = lax.rem(n + k, 4)
            landed = mix_part.at[source, quarter(g)]
            noted = mix_stat.at[g, source]
            pltpu.make_async_copy(landed, landed, mix_sems.at[1, g, 0, source]).wait()
            pltpu.make_async_copy(noted, noted, mix_sems.at[1, g, 1, source]).wait()

        highs = [pre_stat[h, i, 0:8, :] for i in range(4)] + [mix_stat[g, m, 0:8, :] for m in range(4)]
        totals = [pre_stat[h, i, 8:16, :] for i in range(4)] + [mix_stat[g, m, 8:16, :] for m in range(4)]
        highs += list(new_highs)
        totals += [1.0, 1.0]
        highest = functools.reduce(jnp.maximum, highs)
        factors = [jnp.exp2(high - highest) for high in highs]
        total = sum(f * t for f, t in zip(factors, totals))
        inverse = 1.0 / jnp.where(lax.div(lane8, 4) == g, total, 1.0)
        factors = [f * inverse for f in factors]
        for i in range(2 * g, 2 * g + 2):
            rows = slice(16 * i, 16 * i + 16)
            value = jnp.zeros((16, LAT), f32)
            for at, f in enumerate(factors):
                columns = [f[:, 2 * i + j:2 * i + j + 1] for j in range(2)]
                if at < 8:
                    source = pre_part[at, rows, :] if at < 4 else mix_part[at - 4, rows, :]
                    value = value + source.astype(f32) * jnp.concatenate(columns, axis=0)
                else:
                    u = at - 8
                    new = [new_ref[2 * i + j].astype(f32)[u:u + 1, :LAT] for j in range(2)]
                    value = value + jnp.concatenate([a * b for a, b in zip(columns, new)], axis=0)
            for j in range(2):
                for t in range(2):
                    at = 8 * j + 4 * t
                    done[2 * i + j, t] = value[at:at + 4].astype(bf16)

        @pl.when(stays)
        def _(g=g):
            out_ref[4 * g:4 * g + 4] = done[4 * g:4 * g + 4]

        @pl.when(jnp.logical_not(stays))
        def _(g=g):
            send_on(g).start()

    for h in range(2):
        for k in range(1, 4):
            q_copy(h, k).wait_send()
    for h in range(2):
        for copy in core_copies(h):
            copy.wait_send()
        for k in range(1, 4):
            for copy in pre_copies(h, k):
                copy.wait_send()
    for g in range(4):
        for k in range(1, 4):
            for copy in mix_copies(g, k):
                copy.wait_send()

    @pl.when(jnp.logical_not(stays))
    def _():
        for g in range(4):
            send_on(g).wait()


def fused(counts, lens, lists, new_latent, queries, cache, suffix, spilled):
    dma = pltpu.SemaphoreType.DMA
    f32, bf16, i32 = jnp.float32, jnp.bfloat16, jnp.int32
    return pl.pallas_call(
        fused_kernel,
        out_shape=jax.ShapeDtypeStruct((16, 2, 4, LAT), bf16),
        in_specs=[pl.BlockSpec(memory_space=pl.ANY)] * 8,
        out_specs=pl.BlockSpec(memory_space=pltpu.VMEM),
        scratch_shapes=[
            pltpu.SMEM((16,), i32),
            pltpu.SMEM((16,), i32),
            pltpu.VMEM((16, 64), i32),
            pltpu.VMEM((16, 2, KV), bf16),
            pltpu.VMEM((16, ROWS, KV), bf16),
            pltpu.VMEM((16, ROWS, KV), bf16),
            pltpu.VMEM((8, 128, KV), bf16),
            pltpu.VMEM((4, 128, KV), bf16),
            pltpu.VMEM((64, PAGE, KV), bf16),
            pltpu.VMEM((16, TILE, KV), bf16),
            pltpu.VMEM((24, 256), i32),
            pltpu.SMEM((24, 256), i32),
            pltpu.VMEM((SLOTS + 17, ROWS, LAT), f32),
            pltpu.VMEM((SLOTS + 17, ROWS, 128), f32),
            pltpu.VMEM((SLOTS + 17, ROWS, 128), f32),
            pltpu.VMEM((FUSED, ROWS, TILE), bf16),
            pltpu.VMEM((2, ROWS, SPAN), bf16),
            pltpu.VMEM((ROWS, SPAN), i32),
            pltpu.VMEM((8, 128, LAT), LINK),
            pltpu.VMEM((2, 8, 16, 128), f32),
            pltpu.VMEM((4, 128, LAT), LINK),
            pltpu.VMEM((2, 4, 16, 128), f32),
            pltpu.VMEM((4, 128, LAT), LINK),
            pltpu.VMEM((2, 4, 16, 128), f32),
            pltpu.VMEM((4, 128, LAT), LINK),
            pltpu.VMEM((2, 4, 16, 128), f32),
            pltpu.VMEM((4, 128, LAT), LINK),
            pltpu.VMEM((4, 4, 16, 128), f32),
            pltpu.VMEM((4, 128, LAT), LINK),
            pltpu.VMEM((4, 4, 16, 128), f32),
            pltpu.VMEM((16, 2, 4, LAT), bf16),
            dma((10,)),
            dma((3,)),
            dma((2, 2, 4)),
            dma((2, 2, 2)),
            dma((2, 2, 2, 4)),
            dma((2, 4, 2, 4)),
            dma((2, 4)),
        ],
        compiler_params=pltpu.CompilerParams(
            collective_id=1, has_side_effects=True, vmem_limit_bytes=52 << 20
        ),
        name="fused",
    )(counts, lens, lists, new_latent, queries, cache, suffix, spilled)


def local(queries, new_latent, prefix_cache, suffix_cache, page_lists, prefix_count, suffix_len):
    rows = queries.reshape(16, ROWS, KV)
    suffix = suffix_cache.reshape(16, TILE, KV)
    spilled = spill(prefix_count, page_lists, rows, prefix_cache)
    return fused(
        prefix_count, suffix_len, page_lists, new_latent, rows, prefix_cache, suffix, spilled
    )


def solution(mesh):
    return jax.shard_map(
        local,
        mesh=mesh,
        in_specs=(
            P("batch", None, "narrow", None),
            P("batch", None, None),
            P("prefix", None, None),
            P("batch", "narrow", None, None),
            P("batch", None),
            P("batch"),
            P("batch"),
        ),
        out_specs=P("batch", None, ("prefix", "narrow"), None),
        check_vma=False,
    )
```

```python
import functools

import jax
import jax.numpy as jnp
from jax import lax
from jax.experimental import pallas as pl
from jax.experimental.pallas import tpu as pltpu
from jax.sharding import PartitionSpec as P

MESH = pl.DeviceIdType.MESH
LAT = 512
KV = 576
PAGE = 64
ROWS = 64
GROUP = 4
TILE = GROUP * PAGE
UNROLL = 4
NONE = -30000.0
MASKED = -1e30
TO_LOG2 = 192 ** -0.5 * 1.4426950408889634
LINK = jnp.int16
STEPS_OF = 32767.0
SMALL = 1e-28


def by_owner(a):
    width = a.shape[-1]
    first = a[:32].reshape(4, 8, width)
    second = a[32:].reshape(4, 8, width)
    low = lax.broadcasted_iota(jnp.int32, (4, 8, width), 1) < 4
    even = jnp.where(low, first, pltpu.roll(second, 4, 1))
    odd = jnp.where(low, pltpu.roll(first, 4, 1), second)
    return [(even if d % 2 == 0 else odd)[d // 2] for d in range(8)]


def coded(part, high, total):
    largest = jnp.maximum(jnp.max(jnp.abs(part), axis=1, keepdims=True), SMALL)
    code = jnp.round(part * (STEPS_OF / largest)).astype(jnp.int32)
    return code, high + jnp.log2(largest * (1.0 / STEPS_OF)), total * (STEPS_OF / largest)


def wide(a):
    return jnp.concatenate([a] * 4, axis=1)


def owner_of(prefix):
    return 4 * lax.rem(prefix, 2) + lax.div(prefix, 2)


SLOTS_A = 24
SLOTS = 32
SPAN = 2 * TILE
FUSED = 8


def by_lane(column):
    row = lax.broadcasted_iota(jnp.int32, (16, 256), 0)
    lane = lax.broadcasted_iota(jnp.int32, (16, 256), 1)
    return jnp.sum(jnp.where(row == lane, column, 0.0), axis=0, keepdims=True).astype(jnp.int32)


def tile_plan(lists, count_ref, base):
    f32 = jnp.float32
    row = lax.broadcasted_iota(jnp.int32, (16, 64), 0)
    col = lax.broadcasted_iota(jnp.int32, (16, 64), 1)
    counts = jnp.zeros((16, 64), jnp.int32)
    for b in range(16):
        counts = jnp.where(row == b, count_ref[b], counts)
    local = lists - base
    used = (col < counts) & (local >= 0) & (local < 64)
    number = jnp.sum(jnp.where(used, 1.0, 0.0), axis=1, keepdims=True)
    number = jnp.broadcast_to(number, (16, 256))
    tiles = jnp.floor((number + (GROUP - 1)) * (1.0 / GROUP))
    earlier = jnp.where(
        lax.broadcasted_iota(jnp.int32, (16, 16), 1) < lax.broadcasted_iota(jnp.int32, (16, 16), 0), 1.0, 0.0
    ).astype(jnp.bfloat16)
    start = jnp.dot(earlier, tiles.astype(jnp.bfloat16), preferred_element_type=f32)
    room = jnp.where(lax.broadcasted_iota(jnp.int32, (16, 256), 0) < 8, float(SLOTS_A), float(SLOTS))
    kept = jnp.clip(room - start, 0.0, tiles)
    return local, used, number, tiles, start, kept


def pack_pages(meta_v, local, used):
    f32 = jnp.float32
    page_t = jnp.transpose(jnp.where(used, local, -1).astype(f32))
    used_t = jnp.where(page_t >= 0, 1.0, 0.0)
    before = jnp.where(
        lax.broadcasted_iota(jnp.int32, (64, 64), 1) < lax.broadcasted_iota(jnp.int32, (64, 64), 0), 1.0, 0.0
    ).astype(jnp.bfloat16)
    rank = jnp.dot(before, used_t.astype(jnp.bfloat16), preferred_element_type=f32)
    place = jnp.where(used_t > 0, rank, -1.0)
    place_iota = lax.broadcasted_iota(jnp.int32, (64, 128), 1).astype(f32)
    for b in range(16):
        hit = place[:, b:b + 1] == place_iota
        packed = jnp.sum(jnp.where(hit, page_t[:, b:b + 1], 0.0), axis=0, keepdims=True)
        meta_v[b:b + 1, 0:128] = packed.astype(jnp.int32)


def spill_kernel(
    count_any, lists_any, q_any, cache_any, out_any,
    count_ref, lists_ref, q_ref, cache_ref, meta_v, meta_s, acc, stat, sems,
):
    f32 = jnp.float32
    loads = [
        pltpu.make_async_copy(count_any, count_ref, sems.at[0]),
        pltpu.make_async_copy(lists_any, lists_ref, sems.at[1]),
    ]
    for copy in loads:
        copy.start()
    for copy in loads:
        copy.wait()
    local, used, number, tiles, start, kept = tile_plan(
        lists_ref[...], count_ref, lax.axis_index("prefix") * 64
    )

    @pl.when(jnp.max(tiles - kept) > 0.5)
    def _():
        large = [
            pltpu.make_async_copy(q_any, q_ref, sems.at[0]),
            pltpu.make_async_copy(cache_any, cache_ref, sems.at[1]),
        ]
        for copy in large:
            copy.start()
        meta_v[...] = jnp.zeros_like(meta_v)
        pack_pages(meta_v, local, used)
        meta_v[16:17, :] = by_lane(kept)
        meta_v[17:18, :] = by_lane(tiles)
        meta_v[18:19, :] = by_lane(number)
        noted = pltpu.make_async_copy(meta_v, meta_s, sems.at[2])
        noted.start()
        noted.wait()
        for copy in large:
            copy.wait()
        key_iota = lax.broadcasted_iota(jnp.int32, (ROWS, TILE), 1)

        def branch(b, carry):
            acc[b] = jnp.zeros((ROWS, LAT), f32)
            stat[0, b] = jnp.full((ROWS, 128), NONE, f32)
            stat[1, b] = jnp.zeros((ROWS, 128), f32)

            def tile(k, carry):
                at = GROUP * k
                keys = jnp.concatenate([cache_ref[meta_s[b, at + i]] for i in range(GROUP)], axis=0)
                score = lax.dot_general(
                    q_ref[b], keys, (((1,), (1,)), ((), ())), preferred_element_type=f32
                ) * TO_LOG2
                score = jnp.where(key_iota < (meta_s[18, b] - at) * PAGE, score, MASKED)
                high = jnp.maximum(jnp.max(score, axis=1, keepdims=True), NONE)
                expo = jnp.exp2(score - high)
                total = jnp.sum(expo, axis=1, keepdims=True)
                part = jnp.dot(expo.astype(jnp.bfloat16), keys[:, :LAT], preferred_element_type=f32)
                old = stat[0, b]
                new = jnp.maximum(old, high)
                f_old = jnp.exp2(old - new)
                f_new = jnp.exp2(high - new)
                stat[0, b] = new
                stat[1, b] = stat[1, b] * f_old + total * f_new
                acc[b] = acc[b] * wide(f_old) + part * wide(f_new)
                return carry

            lax.fori_loop(meta_s[16, b], meta_s[17, b], tile, 0)
            acc[b] = jnp.concatenate(by_owner(acc[b]), axis=0)
            stat[0, b] = jnp.concatenate(by_owner(stat[0, b]), axis=0)
            stat[1, b] = jnp.concatenate(by_owner(stat[1, b]), axis=0)
            return carry

        lax.fori_loop(0, 16, branch, 0)
        out = [
            pltpu.make_async_copy(acc, out_any.at[:, :, 0:LAT], sems.at[0]),
            pltpu.make_async_copy(stat.at[0], out_any.at[:, :, LAT:LAT + 128], sems.at[1]),
            pltpu.make_async_copy(stat.at[1], out_any.at[:, :, LAT + 128:LAT + 256], sems.at[2]),
        ]
        for copy in out:
            copy.start()
        for copy in out:
            copy.wait()


def spill(counts, lists, queries, cache):
    return pl.pallas_call(
        spill_kernel,
        out_shape=jax.ShapeDtypeStruct((16, ROWS, 2048), jnp.float32),
        in_specs=[pl.BlockSpec(memory_space=pl.ANY)] * 4,
        out_specs=pl.BlockSpec(memory_space=pl.ANY),
        scratch_shapes=[
            pltpu.SMEM((16,), jnp.int32),
            pltpu.VMEM((16, 64), jnp.int32),
            pltpu.VMEM((16, ROWS, KV), jnp.bfloat16),
            pltpu.VMEM((64, PAGE, KV), jnp.bfloat16),
            pltpu.VMEM((24, 256), jnp.int32),
            pltpu.SMEM((24, 256), jnp.int32),
            pltpu.VMEM((16, ROWS, LAT), jnp.float32),
            pltpu.VMEM((2, 16, ROWS, 128), jnp.float32),
            pltpu.SemaphoreType.DMA((3,)),
        ],
        compiler_params=pltpu.CompilerParams(vmem_limit_bytes=60 << 20),
        name="spill",
    )(counts, lists, queries, cache)


def fused_kernel(
    count_any, len_any, lists_any, new_any, q_any, cache_any, suffix_any, spill_any, out_ref,
    count_ref, len_ref, lists_ref, new_ref, q_ref, q_rows, q_send, q_all, cache_ref, suffix_ref,
    meta_v, meta_s, acc, top, tot, weight, weight2, key_rel,
    part_send, stat_send, core_part, core_stat, row_send, row_stat_send, pre_part, pre_stat, mix_send, mix_stat_send, mix_part, mix_stat, done,
    in_sems, own_sems, q_sems, core_sems, pre_sems, mix_sems, end_sems,
):
    f32 = jnp.float32
    bf16 = jnp.bfloat16
    p = lax.axis_index("prefix")
    n = lax.axis_index("narrow")
    x = lax.div(p, 2)
    c = lax.rem(p, 2)
    mine = owner_of(p)
    stays = x == n
    across = {"prefix": 2 * n + c, "narrow": x}

    loads = [
        pltpu.make_async_copy(source, target, in_sems.at[k])
        for k, (source, target) in enumerate([
            (count_any, count_ref), (len_any, len_ref), (lists_any, lists_ref), (new_any, new_ref),
            (q_any, q_ref), (cache_any, cache_ref), (suffix_any, suffix_ref),
            (spill_any.at[:, :, 0:LAT], acc.at[pl.ds(SLOTS + 1, 16)]),
            (spill_any.at[:, :, LAT:LAT + 128], top.at[pl.ds(SLOTS + 1, 16)]),
            (spill_any.at[:, :, LAT + 128:LAT + 256], tot.at[pl.ds(SLOTS + 1, 16)]),
        ])
    ]
    barrier = pltpu.get_barrier_semaphore()

    def greet(**to):
        pl.semaphore_signal(barrier, inc=1, device_id=to, device_id_type=MESH)

    greet(prefix=2 * x + 1 - c)
    for k in range(1, 4):
        greet(prefix=2 * lax.rem(x + k, 4) + c)
        greet(narrow=lax.rem(n + k, 4))

    @pl.when(jnp.logical_not(stays))
    def _():
        greet(**across)

    for k in (0, 2, 4, 5, 1):
        loads[k].start()

    meta_v[...] = jnp.zeros_like(meta_v)
    acc[0] = jnp.zeros((ROWS, LAT), f32)
    top[0] = jnp.full((ROWS, 128), NONE, f32)
    tot[0] = jnp.zeros((ROWS, 128), f32)
    loads[0].wait()
    loads[2].wait()
    local, used, number, tiles, start, kept = tile_plan(lists_ref[...], count_ref, 64 * p)
    pack_pages(meta_v, local, used)
    slot = lax.broadcasted_iota(jnp.int32, (16, 256), 1).astype(f32)
    inside = (slot >= start) & (slot < start + tiles)
    branch = lax.broadcasted_iota(jnp.int32, (16, 256), 0).astype(f32)

    def pick(a):
        return jnp.sum(jnp.where(inside, a, 0.0), axis=0, keepdims=True).astype(jnp.int32)

    meta_v[16:17, :] = pick(branch)
    meta_v[17:18, :] = pick((slot - start) * GROUP)
    meta_v[18:19, :] = pick(jnp.clip(number - (slot - start) * GROUP, 0.0, float(GROUP)) * PAGE)
    meta_v[19:20, :] = pick(jnp.where(slot == start, NONE, -NONE))
    meta_v[20:21, :] = by_lane(jnp.where(kept > 0, start + kept, 0.0))
    meta_v[21:22, :] = by_lane(jnp.where(tiles > kept, branch + (SLOTS + 1.0), 0.0))
    meta_copy = pltpu.make_async_copy(meta_v, meta_s, own_sems.at[0])
    meta_copy.start()

    loads[4].wait()

    def order(i, carry):
        left = by_owner(q_ref[2 * i].astype(f32))
        right = by_owner(q_ref[2 * i + 1].astype(f32))
        q_rows[2 * i] = jnp.concatenate(left, axis=0).astype(bf16)
        q_rows[2 * i + 1] = jnp.concatenate(right, axis=0).astype(bf16)
        for d in range(8):
            q_send[d, pl.ds(pl.multiple_of(16 * i, 16), 16), :] = jnp.concatenate(
                [left[d], right[d]], axis=0
            ).astype(bf16)
        return carry

    def q_own(h):
        half = pl.ds(64 * h, 64)
        return pltpu.make_async_copy(q_send.at[mine, half], q_all.at[n, half], own_sems.at[1 + h])

    def q_copy(h, k):
        half = pl.ds(64 * h, 64)
        return pltpu.make_async_remote_copy(
            src_ref=q_send.at[mine, half], dst_ref=q_all.at[n, half],
            send_sem=q_sems.at[0, h, k], recv_sem=q_sems.at[1, h, n],
            device_id={"narrow": lax.rem(n + k, 4)}, device_id_type=MESH,
        )

    lax.fori_loop(0, 4, order, 0)
    pl.semaphore_wait(barrier, jnp.where(stays, 7, 8))
    for k in (2, 1, 3):
        q_copy(0, k).start()
    lax.fori_loop(4, 8, order, 0)
    for k in (2, 1, 3):
        q_copy(1, k).start()
    for h in range(2):
        q_own(h).start()

    meta_copy.wait()
    loads[5].wait()
    for k in (6, 3, 7, 8, 9):
        loads[k].start()
    key_iota = lax.broadcasted_iota(jnp.int32, (ROWS, TILE), 1)

    def tile_scores(s, u):
        b = jnp.clip(meta_s[16, s], 0, 15)
        k = jnp.clip(meta_s[17, s], 0, 60)
        live = meta_s[18, s]
        pages = [jnp.clip(meta_s[b, k + i], 0, 63) for i in range(GROUP)]
        keys = jnp.concatenate([cache_ref[page] for page in pages], axis=0)
        score = lax.dot_general(
            q_rows[b], keys, (((1,), (1,)), ((), ())), preferred_element_type=f32
        ) * TO_LOG2
        score = jnp.where(key_iota < live, score, MASKED)
        high = jnp.maximum(jnp.max(score, axis=1, keepdims=True), NONE)
        expo = jnp.exp2(score - high)
        weight[u] = expo.astype(bf16)
        return pages, high, jnp.sum(expo, axis=1, keepdims=True)

    def tile_group(i, carry):
        ready = [tile_scores(i * FUSED + u, u) for u in range(FUSED)]
        for u, (pages, high, total) in enumerate(ready):
            s = i * FUSED + u
            values = jnp.concatenate([cache_ref[page, :, :LAT] for page in pages], axis=0)
            part = jnp.dot(weight[u], values, preferred_element_type=f32)
            old = jnp.minimum(top[s], meta_s[19, s].astype(f32))
            new = jnp.maximum(old, high)
            f_old = jnp.exp2(old - new)
            f_new = jnp.exp2(high - new)
            top[s + 1] = new
            tot[s + 1] = tot[s] * f_old + total * f_new
            acc[s + 1] = acc[s] * wide(f_old) + part * wide(f_new)
        return carry

    lane64 = lax.broadcasted_iota(jnp.int32, (ROWS, 128), 1)

    def pack(i, carry):
        high_all, total_all = carry
        pieces = []
        for b in (2 * i, 2 * i + 1):
            at = jnp.clip(meta_s[20, b], 0, SLOTS)
            more = jnp.clip(meta_s[21, b], 0, SLOTS + 16)
            high = jnp.maximum(top[at], top[more])
            f_at = jnp.exp2(top[at] - high)
            f_more = jnp.exp2(top[more] - high)
            part = acc[at] * wide(f_at) + acc[more] * wide(f_more)
            code, high, total = coded(part, high, tot[at] * f_at + tot[more] * f_more)
            high_all = jnp.where(lane64 == b, high, high_all)
            total_all = jnp.where(lane64 == b, total, total_all)
            pieces.append(code)
        left, right = pieces
        for d in range(8):
            rows = slice(8 * d, 8 * d + 8)
            part_send[d, pl.ds(pl.multiple_of(16 * i, 16), 16), :] = jnp.concatenate(
                [left[rows], right[rows]], axis=0
            ).astype(LINK)
        return high_all, total_all

    def core_copies(h):
        other = 4 * (1 - c)
        half = pl.ds(64 * h, 64)
        return [
            pltpu.make_async_remote_copy(
                src_ref=part_send.at[pl.ds(other, 4), half], dst_ref=core_part.at[:, half],
                send_sem=core_sems.at[0, h, 0], recv_sem=core_sems.at[1, h, 0],
                device_id={"prefix": 2 * x + 1 - c}, device_id_type=MESH,
            ),
            pltpu.make_async_remote_copy(
                src_ref=stat_send.at[h, pl.ds(other, 4)], dst_ref=core_stat.at[h],
                send_sem=core_sems.at[0, h, 1], recv_sem=core_sems.at[1, h, 1],
                device_id={"prefix": 2 * x + 1 - c}, device_id_type=MESH,
            ),
        ]

    def pre_copies(h, k):
        other = lax.rem(x + k, 4)
        half = pl.ds(64 * h, 64)
        return [
            pltpu.make_async_remote_copy(
                src_ref=row_send.at[other, half], dst_ref=pre_part.at[x, half],
                send_sem=pre_sems.at[0, h, 0, k], recv_sem=pre_sems.at[1, h, 0, x],
                device_id={"prefix": 2 * other + c}, device_id_type=MESH,
            ),
            pltpu.make_async_remote_copy(
                src_ref=row_stat_send.at[h, other], dst_ref=pre_stat.at[h, x],
                send_sem=pre_sems.at[0, h, 1, k], recv_sem=pre_sems.at[1, h, 1, x],
                device_id={"prefix": 2 * other + c}, device_id_type=MESH,
            ),
        ]

    def pre_own(h):
        half = pl.ds(64 * h, 64)
        return [
            pltpu.make_async_copy(row_send.at[x, half], pre_part.at[x, half], pre_sems.at[0, h, 0, 0]),
            pltpu.make_async_copy(row_stat_send.at[h, x], pre_stat.at[h, x], pre_sems.at[0, h, 1, 0]),
        ]

    def pack_half(h):
        high_all, total_all = lax.fori_loop(
            4 * h, 4 * h + 4, pack, (jnp.full((ROWS, 128), NONE, f32), jnp.zeros((ROWS, 128), f32))
        )
        for d in range(8):
            stat_send[h, d, 0:8, :] = high_all[8 * d:8 * d + 8]
            stat_send[h, d, 8:16, :] = total_all[8 * d:8 * d + 8]
        for copy in core_copies(h):
            copy.start()

    def join_cores(h):
        for copy in core_copies(h):
            copy.wait_recv()

        def one_owner(to, carry):
            d = 4 * c + to
            high_a, high_b = stat_send[h, d, 0:8, :], core_stat[h, to, 0:8, :]
            high = jnp.maximum(high_a, high_b)
            f_a, f_b = jnp.exp2(high_a - high) * 0.5, jnp.exp2(high_b - high) * 0.5
            row_stat_send[h, to, 0:8, :] = high + 1.0
            row_stat_send[h, to, 8:16, :] = f_a * stat_send[h, d, 8:16, :] + f_b * core_stat[h, to, 8:16, :]
            for i in range(4 * h, 4 * h + 4):
                rows = slice(16 * i, 16 * i + 16)

                def column(a):
                    return jnp.concatenate([a[:, 2 * i + j:2 * i + j + 1] for j in range(2)], axis=0)

                value = (
                    part_send[d, rows, :].astype(f32) * column(f_a)
                    + core_part[to, rows, :].astype(f32) * column(f_b)
                )
                row_send[to, rows, :] = jnp.round(value).astype(jnp.int32).astype(LINK)
            return carry

        lax.fori_loop(0, 4, one_owner, 0)
        for k in (2, 1, 3):
            for copy in pre_copies(h, k):
                copy.start()
        for copy in pre_own(h):
            copy.start()

    lane8 = lax.broadcasted_iota(jnp.int32, (8, 128), 1)
    key_at = lax.broadcasted_iota(jnp.int32, (ROWS, SPAN), 1)
    side = lax.rem(lax.div(lax.broadcasted_iota(jnp.int32, (ROWS, SPAN), 0), 8), 2)
    key_rel[...] = jnp.where(lax.div(key_at, TILE) == side, lax.rem(key_at, TILE), 1 << 20)
    def q_arrived(h):
        q_own(h).wait()
        half = pl.ds(64 * h, 64)
        for k in range(1, 4):
            source = lax.rem(n + k, 4)
            landed = q_all.at[source, half]
            pltpu.make_async_copy(landed, landed, q_sems.at[1, h, source]).wait()


    def quarter(g):
        return pl.ds(pl.multiple_of(32 * g, 32), 32)

    def mix_copies(g, k):
        other = lax.rem(n + k, 4)
        return [
            pltpu.make_async_remote_copy(
                src_ref=mix_send.at[other, quarter(g)], dst_ref=mix_part.at[n, quarter(g)],
                send_sem=mix_sems.at[0, g, 0, k], recv_sem=mix_sems.at[1, g, 0, n],
                device_id={"narrow": other}, device_id_type=MESH,
            ),
            pltpu.make_async_remote_copy(
                src_ref=mix_stat_send.at[g, other], dst_ref=mix_stat.at[g, n],
                send_sem=mix_sems.at[0, g, 1, k], recv_sem=mix_sems.at[1, g, 1, n],
                device_id={"narrow": other}, device_id_type=MESH,
            ),
        ]

    def mix_own(g):
        return [
            pltpu.make_async_copy(mix_send.at[n, quarter(g)], mix_part.at[n, quarter(g)], mix_sems.at[0, g, 0, 0]),
            pltpu.make_async_copy(mix_stat_send.at[g, n], mix_stat.at[g, n], mix_sems.at[0, g, 1, 0]),
        ]

    def mix_scores(i, u):
        rows = pl.ds(pl.multiple_of(16 * i, 16), 16)
        queries = jnp.concatenate([q_all[m, rows, :] for m in range(4)], axis=0)
        keys = jnp.concatenate([suffix_ref[2 * i], suffix_ref[2 * i + 1]], axis=0)
        score = lax.dot_general(
            queries, keys, (((1,), (1,)), ((), ())), preferred_element_type=f32
        ) * TO_LOG2
        limit = jnp.where(side == 0, len_ref[2 * i] - n * TILE, len_ref[2 * i + 1] - n * TILE)
        score = jnp.where(key_rel[...] < limit, score, MASKED)
        high = jnp.maximum(jnp.max(score, axis=1, keepdims=True), NONE)
        expo = jnp.exp2(score - high)
        weight2[u] = expo.astype(bf16)
        return high, jnp.sum(expo, axis=1, keepdims=True)

    def mix_pairs(g, carry):
        stats = [jnp.full((8, 128), NONE, f32)] * 4 + [jnp.zeros((8, 128), f32)] * 4
        ready = [mix_scores(2 * g + u, u) for u in range(2)]
        for u, (high, total) in enumerate(ready):
            i = 2 * g + u
            values = jnp.concatenate([suffix_ref[2 * i, :, :LAT], suffix_ref[2 * i + 1, :, :LAT]], axis=0)
            part = jnp.dot(weight2[u], values, preferred_element_type=f32)
            code, high, total = coded(part, high, total)
            rows = pl.ds(pl.multiple_of(16 * i, 16), 16)
            for m in range(4):
                mix_send[m, rows, :] = code[16 * m:16 * m + 16].astype(LINK)
                for at, value in ((m, high), (m + 4, total)):
                    for j in range(2):
                        piece = value[16 * m + 8 * j:16 * m + 8 * j + 8]
                        stats[at] = jnp.where(lane8 == 2 * i + j, piece, stats[at])
        for m in range(4):
            mix_stat_send[g, m, 0:8, :] = stats[m]
            mix_stat_send[g, m, 8:16, :] = stats[4 + m]
        for k in (2, 1, 3):
            for copy in mix_copies(g, k):
                copy.start()
        for copy in mix_own(g):
            copy.start()
        return carry

    def send_on(g):
        return pltpu.make_async_remote_copy(
            src_ref=done.at[pl.ds(4 * g, 4)], dst_ref=out_ref.at[pl.ds(4 * g, 4)],
            send_sem=end_sems.at[0, g], recv_sem=end_sems.at[1, g],
            device_id=across, device_id_type=MESH,
        )

    def finish(g):
        h = g // 2
        if g % 2 == 0:
            half = pl.ds(64 * h, 64)
            for copy in pre_own(h):
                copy.wait()

            for k in range(1, 4):
                source = lax.rem(x + k, 4)
                landed = pre_part.at[source, half]
                noted = pre_stat.at[h, source]
                pltpu.make_async_copy(landed, landed, pre_sems.at[1, h, 0, source]).wait()
                pltpu.make_async_copy(noted, noted, pre_sems.at[1, h, 1, source]).wait()
        for copy in mix_own(g):
            copy.wait()
        for k in range(1, 4):
            source = lax.rem(n + k, 4)
            landed = mix_part.at[source, quarter(g)]
            noted = mix_stat.at[g, source]
            pltpu.make_async_copy(landed, landed, mix_sems.at[1, g, 0, source]).wait()
            pltpu.make_async_copy(noted, noted, mix_sems.at[1, g, 1, source]).wait()

        highs = [pre_stat[h, i, 0:8, :] for i in range(4)] + [mix_stat[g, m, 0:8, :] for m in range(4)]
        totals = [pre_stat[h, i, 8:16, :] for i in range(4)] + [mix_stat[g, m, 8:16, :] for m in range(4)]
        highs += list(new_highs)
        totals += [1.0, 1.0]
        highest = functools.reduce(jnp.maximum, highs)
        factors = [jnp.exp2(high - highest) for high in highs]
        total = sum(f * t for f, t in zip(factors, totals))
        inverse = 1.0 / jnp.where(lax.div(lane8, 4) == g, total, 1.0)
        factors = [f * inverse for f in factors]
        for i in range(2 * g, 2 * g + 2):
            rows = slice(16 * i, 16 * i + 16)
            value = jnp.zeros((16, LAT), f32)
            for at, f in enumerate(factors):
                columns = [f[:, 2 * i + j:2 * i + j + 1] for j in range(2)]
                if at < 8:
                    source = pre_part[at, rows, :] if at < 4 else mix_part[at - 4, rows, :]
                    value = value + source.astype(f32) * jnp.concatenate(columns, axis=0)
                else:
                    u = at - 8
                    new = [new_ref[2 * i + j].astype(f32)[u:u + 1, :LAT] for j in range(2)]
                    value = value + jnp.concatenate([a * b for a, b in zip(columns, new)], axis=0)
            for j in range(2):
                for t in range(2):
                    at = 8 * j + 4 * t
                    done[2 * i + j, t] = value[at:at + 4].astype(bf16)

        @pl.when(stays)
        def _():
            out_ref[4 * g:4 * g + 4] = done[4 * g:4 * g + 4]

        @pl.when(jnp.logical_not(stays))
        def _():
            send_on(g).start()

    lax.fori_loop(0, SLOTS_A // FUSED, tile_group, 0)
    for k in (7, 8, 9):
        loads[k].wait()
    pack_half(0)
    lax.fori_loop(SLOTS_A // FUSED + 0, SLOTS_A // FUSED + 1, tile_group, 0)
    join_cores(0)
    loads[1].wait()
    loads[6].wait()
    q_arrived(0)
    lax.fori_loop(0, 2, mix_pairs, 0)
    pack_half(1)
    q_arrived(1)
    lax.fori_loop(2, 3, mix_pairs, 0)
    join_cores(1)
    lax.fori_loop(3, 4, mix_pairs, 0)
    loads[3].wait()
    step8 = lax.broadcasted_iota(jnp.int32, (8, 1), 0) >= 4

    def new_scores(i, carry):
        queries = q_send[mine, pl.ds(pl.multiple_of(16 * i, 16), 16), :].astype(f32)
        out = list(carry)
        for j in range(2):
            keys = new_ref[2 * i + j].astype(f32)
            for u in range(2):
                score = jnp.sum(queries[8 * j:8 * j + 8] * keys[u:u + 1], axis=1, keepdims=True) * TO_LOG2
                if u == 1:
                    score = jnp.where(step8, score, NONE)
                out[u] = jnp.where(lane8 == 2 * i + j, score, out[u])
        return tuple(out)

    new_highs = lax.fori_loop(0, 8, new_scores, tuple([jnp.full((8, 128), NONE, f32)] * 2))

    finish(0)
    finish(1)
    finish(2)
    finish(3)


    for h in range(2):
        for k in range(1, 4):
            q_copy(h, k).wait_send()
    for h in range(2):
        for copy in core_copies(h):
            copy.wait_send()
        for k in range(1, 4):
            for copy in pre_copies(h, k):
                copy.wait_send()
    for g in range(4):
        for k in range(1, 4):
            for copy in mix_copies(g, k):
                copy.wait_send()

    @pl.when(jnp.logical_not(stays))
    def _():
        for g in range(4):
            send_on(g).wait()


def fused(counts, lens, lists, new_latent, queries, cache, suffix, spilled):
    dma = pltpu.SemaphoreType.DMA
    f32, bf16, i32 = jnp.float32, jnp.bfloat16, jnp.int32
    return pl.pallas_call(
        fused_kernel,
        out_shape=jax.ShapeDtypeStruct((16, 2, 4, LAT), bf16),
        in_specs=[pl.BlockSpec(memory_space=pl.ANY)] * 8,
        out_specs=pl.BlockSpec(memory_space=pltpu.VMEM),
        scratch_shapes=[
            pltpu.SMEM((16,), i32),
            pltpu.SMEM((16,), i32),
            pltpu.VMEM((16, 64), i32),
            pltpu.VMEM((16, 2, KV), bf16),
            pltpu.VMEM((16, ROWS, KV), bf16),
            pltpu.VMEM((16, ROWS, KV), bf16),
            pltpu.VMEM((8, 128, KV), bf16),
            pltpu.VMEM((4, 128, KV), bf16),
            pltpu.VMEM((64, PAGE, KV), bf16),
            pltpu.VMEM((16, TILE, KV), bf16),
            pltpu.VMEM((24, 256), i32),
            pltpu.SMEM((24, 256), i32),
            pltpu.VMEM((SLOTS + 17, ROWS, LAT), f32),
            pltpu.VMEM((SLOTS + 17, ROWS, 128), f32),
            pltpu.VMEM((SLOTS + 17, ROWS, 128), f32),
            pltpu.VMEM((FUSED, ROWS, TILE), bf16),
            pltpu.VMEM((2, ROWS, SPAN), bf16),
            pltpu.VMEM((ROWS, SPAN), i32),
            pltpu.VMEM((8, 128, LAT), LINK),
            pltpu.VMEM((2, 8, 16, 128), f32),
            pltpu.VMEM((4, 128, LAT), LINK),
            pltpu.VMEM((2, 4, 16, 128), f32),
            pltpu.VMEM((4, 128, LAT), LINK),
            pltpu.VMEM((2, 4, 16, 128), f32),
            pltpu.VMEM((4, 128, LAT), LINK),
            pltpu.VMEM((2, 4, 16, 128), f32),
            pltpu.VMEM((4, 128, LAT), LINK),
            pltpu.VMEM((4, 4, 16, 128), f32),
            pltpu.VMEM((4, 128, LAT), LINK),
            pltpu.VMEM((4, 4, 16, 128), f32),
            pltpu.VMEM((16, 2, 4, LAT), bf16),
            dma((10,)),
            dma((3,)),
            dma((2, 2, 4)),
            dma((2, 2, 2)),
            dma((2, 2, 2, 4)),
            dma((2, 4, 2, 4)),
            dma((2, 4)),
        ],
        compiler_params=pltpu.CompilerParams(
            collective_id=1, has_side_effects=True, vmem_limit_bytes=52 << 20
        ),
        name="fused",
    )(counts, lens, lists, new_latent, queries, cache, suffix, spilled)


def local(queries, new_latent, prefix_cache, suffix_cache, page_lists, prefix_count, suffix_len):
    rows = queries.reshape(16, ROWS, KV)
    suffix = suffix_cache.reshape(16, TILE, KV)
    spilled = spill(prefix_count, page_lists, rows, prefix_cache)
    return fused(
        prefix_count, suffix_len, page_lists, new_latent, rows, prefix_cache, suffix, spilled
    )


def solution(mesh):
    return jax.shard_map(
        local,
        mesh=mesh,
        in_specs=(
            P("batch", None, "narrow", None),
            P("batch", None, None),
            P("prefix", None, None),
            P("batch", "narrow", None, None),
            P("batch", None),
            P("batch"),
            P("batch"),
        ),
        out_specs=P("batch", None, ("prefix", "narrow"), None),
        check_vma=False,
    )
```

```python
import functools

import jax
import jax.numpy as jnp
from jax import lax
from jax.experimental import pallas as pl
from jax.experimental.pallas import tpu as pltpu
from jax.sharding import PartitionSpec as P

MESH = pl.DeviceIdType.MESH
LAT = 512
KV = 576
PAGE = 64
ROWS = 64
GROUP = 4
TILE = GROUP * PAGE
UNROLL = 4
NONE = -30000.0
MASKED = -1e30
TO_LOG2 = 192 ** -0.5 * 1.4426950408889634
LINK = jnp.int16
STEPS_OF = 32767.0
SMALL = 1e-28


def by_owner(a):
    width = a.shape[-1]
    first = a[:32].reshape(4, 8, width)
    second = a[32:].reshape(4, 8, width)
    low = lax.broadcasted_iota(jnp.int32, (4, 8, width), 1) < 4
    even = jnp.where(low, first, pltpu.roll(second, 4, 1))
    odd = jnp.where(low, pltpu.roll(first, 4, 1), second)
    return [(even if d % 2 == 0 else odd)[d // 2] for d in range(8)]


def coded(part, high, total):
    largest = jnp.maximum(jnp.max(jnp.abs(part), axis=1, keepdims=True), SMALL)
    code = jnp.round(part * (STEPS_OF / largest)).astype(jnp.int32)
    return code, high + jnp.log2(largest * (1.0 / STEPS_OF)), total * (STEPS_OF / largest)


def wide(a):
    return jnp.concatenate([a] * 4, axis=1)


def owner_of(prefix):
    return 4 * lax.rem(prefix, 2) + lax.div(prefix, 2)


SLOTS_A = 24
SLOTS = 36
FUSED = 12
ROUND = 2


def by_lane(column):
    row = lax.broadcasted_iota(jnp.int32, (16, 256), 0)
    lane = lax.broadcasted_iota(jnp.int32, (16, 256), 1)
    return jnp.sum(jnp.where(row == lane, column, 0.0), axis=0, keepdims=True).astype(jnp.int32)


def tile_plan(lists, count_ref, base):
    f32 = jnp.float32
    row = lax.broadcasted_iota(jnp.int32, (16, 64), 0)
    col = lax.broadcasted_iota(jnp.int32, (16, 64), 1)
    counts = jnp.zeros((16, 64), jnp.int32)
    for b in range(16):
        counts = jnp.where(row == b, count_ref[b], counts)
    local = lists - base
    used = (col < counts) & (local >= 0) & (local < 64)
    number = jnp.sum(jnp.where(used, 1.0, 0.0), axis=1, keepdims=True)
    number = jnp.broadcast_to(number, (16, 256))
    tiles = jnp.floor((number + (GROUP - 1)) * (1.0 / GROUP))
    earlier = jnp.where(
        lax.broadcasted_iota(jnp.int32, (16, 16), 1) < lax.broadcasted_iota(jnp.int32, (16, 16), 0), 1.0, 0.0
    ).astype(jnp.bfloat16)
    start = jnp.dot(earlier, tiles.astype(jnp.bfloat16), preferred_element_type=f32)
    room = jnp.where(lax.broadcasted_iota(jnp.int32, (16, 256), 0) < 8, float(SLOTS_A), float(SLOTS))
    kept = jnp.clip(room - start, 0.0, tiles)
    return local, used, number, tiles, start, kept


def pack_pages(meta_v, local, used):
    f32 = jnp.float32
    page_t = jnp.transpose(jnp.where(used, local, -1).astype(f32))
    used_t = jnp.where(page_t >= 0, 1.0, 0.0)
    before = jnp.where(
        lax.broadcasted_iota(jnp.int32, (64, 64), 1) < lax.broadcasted_iota(jnp.int32, (64, 64), 0), 1.0, 0.0
    ).astype(jnp.bfloat16)
    rank = jnp.dot(before, used_t.astype(jnp.bfloat16), preferred_element_type=f32)
    place = jnp.where(used_t > 0, rank, -1.0)
    place_iota = lax.broadcasted_iota(jnp.int32, (64, 128), 1).astype(f32)
    for b in range(16):
        hit = place[:, b:b + 1] == place_iota
        packed = jnp.sum(jnp.where(hit, page_t[:, b:b + 1], 0.0), axis=0, keepdims=True)
        meta_v[b:b + 1, 0:128] = packed.astype(jnp.int32)


def spill_kernel(
    count_any, lists_any, q_any, cache_any, out_any,
    count_ref, lists_ref, q_ref, cache_ref, meta_v, meta_s, acc, stat, sems,
):
    f32 = jnp.float32
    loads = [
        pltpu.make_async_copy(count_any, count_ref, sems.at[0]),
        pltpu.make_async_copy(lists_any, lists_ref, sems.at[1]),
    ]
    for copy in loads:
        copy.start()
    for copy in loads:
        copy.wait()
    local, used, number, tiles, start, kept = tile_plan(
        lists_ref[...], count_ref, lax.axis_index("prefix") * 64
    )

    @pl.when(jnp.max(tiles - kept) > 0.5)
    def _():
        large = [
            pltpu.make_async_copy(q_any, q_ref, sems.at[0]),
            pltpu.make_async_copy(cache_any, cache_ref, sems.at[1]),
        ]
        for copy in large:
            copy.start()
        meta_v[...] = jnp.zeros_like(meta_v)
        pack_pages(meta_v, local, used)
        meta_v[16:17, :] = by_lane(kept)
        meta_v[17:18, :] = by_lane(tiles)
        meta_v[18:19, :] = by_lane(number)
        noted = pltpu.make_async_copy(meta_v, meta_s, sems.at[2])
        noted.start()
        noted.wait()
        for copy in large:
            copy.wait()
        key_iota = lax.broadcasted_iota(jnp.int32, (ROWS, TILE), 1)

        def branch(b, carry):
            acc[b] = jnp.zeros((ROWS, LAT), f32)
            stat[0, b] = jnp.full((ROWS, 128), NONE, f32)
            stat[1, b] = jnp.zeros((ROWS, 128), f32)

            def tile(k, carry):
                at = GROUP * k
                keys = jnp.concatenate([cache_ref[meta_s[b, at + i]] for i in range(GROUP)], axis=0)
                score = lax.dot_general(
                    q_ref[b], keys, (((1,), (1,)), ((), ())), preferred_element_type=f32
                ) * TO_LOG2
                score = jnp.where(key_iota < (meta_s[18, b] - at) * PAGE, score, MASKED)
                high = jnp.maximum(jnp.max(score, axis=1, keepdims=True), NONE)
                expo = jnp.exp2(score - high)
                total = jnp.sum(expo, axis=1, keepdims=True)
                part = jnp.dot(expo.astype(jnp.bfloat16), keys[:, :LAT], preferred_element_type=f32)
                old = stat[0, b]
                new = jnp.maximum(old, high)
                f_old = jnp.exp2(old - new)
                f_new = jnp.exp2(high - new)
                stat[0, b] = new
                stat[1, b] = stat[1, b] * f_old + total * f_new
                acc[b] = acc[b] * wide(f_old) + part * wide(f_new)
                return carry

            lax.fori_loop(meta_s[16, b], meta_s[17, b], tile, 0)
            acc[b] = jnp.concatenate(by_owner(acc[b]), axis=0)
            stat[0, b] = jnp.concatenate(by_owner(stat[0, b]), axis=0)
            stat[1, b] = jnp.concatenate(by_owner(stat[1, b]), axis=0)
            return carry

        lax.fori_loop(0, 16, branch, 0)
        out = [
            pltpu.make_async_copy(acc, out_any.at[:, :, 0:LAT], sems.at[0]),
            pltpu.make_async_copy(stat.at[0], out_any.at[:, :, LAT:LAT + 128], sems.at[1]),
            pltpu.make_async_copy(stat.at[1], out_any.at[:, :, LAT + 128:LAT + 256], sems.at[2]),
        ]
        for copy in out:
            copy.start()
        for copy in out:
            copy.wait()


def spill(counts, lists, queries, cache):
    return pl.pallas_call(
        spill_kernel,
        out_shape=jax.ShapeDtypeStruct((16, ROWS, 2048), jnp.float32),
        in_specs=[pl.BlockSpec(memory_space=pl.ANY)] * 4,
        out_specs=pl.BlockSpec(memory_space=pl.ANY),
        scratch_shapes=[
            pltpu.SMEM((16,), jnp.int32),
            pltpu.VMEM((16, 64), jnp.int32),
            pltpu.VMEM((16, ROWS, KV), jnp.bfloat16),
            pltpu.VMEM((64, PAGE, KV), jnp.bfloat16),
            pltpu.VMEM((24, 256), jnp.int32),
            pltpu.SMEM((24, 256), jnp.int32),
            pltpu.VMEM((16, ROWS, LAT), jnp.float32),
            pltpu.VMEM((2, 16, ROWS, 128), jnp.float32),
            pltpu.SemaphoreType.DMA((3,)),
        ],
        compiler_params=pltpu.CompilerParams(vmem_limit_bytes=60 << 20),
        name="spill",
    )(counts, lists, queries, cache)


def fused_kernel(
    count_any, len_any, lists_any, new_any, q_any, cache_any, suffix_any, spill_any, out_ref,
    count_ref, len_ref, lists_ref, new_ref, q_ref, q_rows, q_send, q_all, cache_ref, suffix_ref,
    meta_v, meta_s, acc, top, tot, weight, weight2,
    part_send, stat_send, core_part, core_stat, row_send, row_stat_send, pre_part, pre_stat, mix_send, mix_stat_send, mix_part, mix_stat, done, passing,
    in_sems, own_sems, q_sems, core_sems, pre_sems, note_sems, mix_sems, end_sems, pass_sems,
):
    f32 = jnp.float32
    bf16 = jnp.bfloat16
    p = lax.axis_index("prefix")
    n = lax.axis_index("narrow")
    x = lax.div(p, 2)
    c = lax.rem(p, 2)
    mine = owner_of(p)
    stays = x == n
    across = {"prefix": 2 * n + c, "narrow": x}

    loads = [
        pltpu.make_async_copy(source, target, in_sems.at[k])
        for k, (source, target) in enumerate([
            (count_any, count_ref), (len_any, len_ref), (lists_any, lists_ref), (new_any, new_ref),
            (q_any, q_ref), (cache_any, cache_ref), (suffix_any, suffix_ref),
            (spill_any.at[:, :, 0:LAT], acc.at[pl.ds(SLOTS + 1, 16)]),
            (spill_any.at[:, :, LAT:LAT + 128], top.at[pl.ds(SLOTS + 1, 16)]),
            (spill_any.at[:, :, LAT + 128:LAT + 256], tot.at[pl.ds(SLOTS + 1, 16)]),
        ])
    ]
    barrier = pltpu.get_barrier_semaphore()

    def greet(**to):
        pl.semaphore_signal(barrier, inc=1, device_id=to, device_id_type=MESH)

    greet(prefix=2 * x + 1 - c)
    for k in range(1, 4):
        greet(prefix=2 * lax.rem(x + k, 4) + c)
        greet(narrow=lax.rem(n + k, 4))

    @pl.when(jnp.logical_not(stays))
    def _():
        greet(**across)

    for k in (0, 2, 4, 5, 1):
        loads[k].start()

    meta_v[...] = jnp.zeros_like(meta_v)
    acc[0] = jnp.zeros((ROWS, LAT), f32)
    top[0] = jnp.full((ROWS, 128), NONE, f32)
    tot[0] = jnp.zeros((ROWS, 128), f32)
    loads[0].wait()
    loads[2].wait()
    local, used, number, tiles, start, kept = tile_plan(lists_ref[...], count_ref, 64 * p)
    pack_pages(meta_v, local, used)
    slot = lax.broadcasted_iota(jnp.int32, (16, 256), 1).astype(f32)
    inside = (slot >= start) & (slot < start + tiles)
    branch = lax.broadcasted_iota(jnp.int32, (16, 256), 0).astype(f32)

    def pick(a):
        return jnp.sum(jnp.where(inside, a, 0.0), axis=0, keepdims=True).astype(jnp.int32)

    meta_v[16:17, :] = pick(branch)
    meta_v[17:18, :] = pick((slot - start) * GROUP)
    meta_v[18:19, :] = pick(jnp.clip(number - (slot - start) * GROUP, 0.0, float(GROUP)) * PAGE)
    meta_v[19:20, :] = pick(jnp.where(slot == start, NONE, -NONE))
    meta_v[20:21, :] = by_lane(jnp.where(kept > 0, start + kept, 0.0))
    meta_v[21:22, :] = by_lane(jnp.where(tiles > kept, branch + (SLOTS + 1.0), 0.0))
    meta_copy = pltpu.make_async_copy(meta_v, meta_s, own_sems.at[0])
    meta_copy.start()

    loads[4].wait()

    def order(i, carry):
        left = by_owner(q_ref[2 * i].astype(f32))
        right = by_owner(q_ref[2 * i + 1].astype(f32))
        q_rows[2 * i] = jnp.concatenate(left, axis=0).astype(bf16)
        q_rows[2 * i + 1] = jnp.concatenate(right, axis=0).astype(bf16)
        for d in range(8):
            q_send[d, pl.ds(pl.multiple_of(16 * i, 16), 16), :] = jnp.concatenate(
                [left[d], right[d]], axis=0
            ).astype(bf16)
        return carry

    def q_own(h):
        half = pl.ds(64 * h, 64)
        return pltpu.make_async_copy(q_send.at[mine, half], q_all.at[n, half], own_sems.at[1 + h])

    def q_copy(h, k):
        half = pl.ds(64 * h, 64)
        return pltpu.make_async_remote_copy(
            src_ref=q_send.at[mine, half], dst_ref=q_all.at[n, half],
            send_sem=q_sems.at[0, h, k], recv_sem=q_sems.at[1, h, n],
            device_id={"narrow": lax.rem(n + k, 4)}, device_id_type=MESH,
        )

    lax.fori_loop(0, 4, order, 0)
    pl.semaphore_wait(barrier, jnp.where(stays, 7, 8))
    for k in (2, 1, 3):
        q_copy(0, k).start()
    lax.fori_loop(4, 8, order, 0)
    for k in (2, 1, 3):
        q_copy(1, k).start()
    for h in range(2):
        q_own(h).start()

    meta_copy.wait()
    loads[5].wait()
    for k in (6, 3, 7, 8, 9):
        loads[k].start()
    key_iota = lax.broadcasted_iota(jnp.int32, (ROWS, TILE), 1)

    def tile_scores(s, u):
        b = jnp.clip(meta_s[16, s], 0, 15)
        k = jnp.clip(meta_s[17, s], 0, 60)
        live = meta_s[18, s]
        pages = [jnp.clip(meta_s[b, k + i], 0, 63) for i in range(GROUP)]
        keys = jnp.concatenate([cache_ref[page] for page in pages], axis=0)
        score = lax.dot_general(
            q_rows[b], keys, (((1,), (1,)), ((), ())), preferred_element_type=f32
        ) * TO_LOG2
        score = jnp.where(key_iota < live, score, MASKED)
        high = jnp.maximum(jnp.max(score, axis=1, keepdims=True), NONE)
        expo = jnp.exp2(score - high)
        weight[u] = expo.astype(bf16)
        return pages, high, jnp.sum(expo, axis=1, keepdims=True)

    def tile_group(i, carry):
        ready = [tile_scores(i * FUSED + u, u) for u in range(FUSED)]
        for u, (pages, high, total) in enumerate(ready):
            s = i * FUSED + u
            values = jnp.concatenate([cache_ref[page, :, :LAT] for page in pages], axis=0)
            part = jnp.dot(weight[u], values, preferred_element_type=f32)
            old = jnp.minimum(top[s], meta_s[19, s].astype(f32))
            new = jnp.maximum(old, high)
            f_old = jnp.exp2(old - new)
            f_new = jnp.exp2(high - new)
            top[s + 1] = new
            tot[s + 1] = tot[s] * f_old + total * f_new
            acc[s + 1] = acc[s] * wide(f_old) + part * wide(f_new)
        return carry

    lane64 = lax.broadcasted_iota(jnp.int32, (ROWS, 128), 1)

    def pack(i, carry):
        high_all, total_all = carry
        pieces = []
        for b in (2 * i, 2 * i + 1):
            at = jnp.clip(meta_s[20, b], 0, SLOTS)
            more = jnp.clip(meta_s[21, b], 0, SLOTS + 16)
            high = jnp.maximum(top[at], top[more])
            f_at = jnp.exp2(top[at] - high)
            f_more = jnp.exp2(top[more] - high)
            part = acc[at] * wide(f_at) + acc[more] * wide(f_more)
            code, high, total = coded(part, high, tot[at] * f_at + tot[more] * f_more)
            high_all = jnp.where(lane64 == b, high, high_all)
            total_all = jnp.where(lane64 == b, total, total_all)
            pieces.append(code)
        left, right = pieces
        for d in range(8):
            rows = slice(8 * d, 8 * d + 8)
            part_send[d, pl.ds(pl.multiple_of(16 * i, 16), 16), :] = jnp.concatenate(
                [left[rows], right[rows]], axis=0
            ).astype(LINK)
        return high_all, total_all

    def core_copies(h):
        other = 4 * (1 - c)
        half = pl.ds(64 * h, 64)
        return [
            pltpu.make_async_remote_copy(
                src_ref=part_send.at[pl.ds(other, 4), half], dst_ref=core_part.at[:, half],
                send_sem=core_sems.at[0, h, 0], recv_sem=core_sems.at[1, h, 0],
                device_id={"prefix": 2 * x + 1 - c}, device_id_type=MESH,
            ),
            pltpu.make_async_remote_copy(
                src_ref=stat_send.at[h, pl.ds(other, 4)], dst_ref=core_stat.at[h],
                send_sem=core_sems.at[0, h, 1], recv_sem=core_sems.at[1, h, 1],
                device_id={"prefix": 2 * x + 1 - c}, device_id_type=MESH,
            ),
        ]

    def pre_copy(g, k):
        other = lax.rem(x + k, 4)
        return pltpu.make_async_remote_copy(
            src_ref=row_send.at[other, quarter(g)], dst_ref=pre_part.at[x, quarter(g)],
            send_sem=pre_sems.at[0, g, k], recv_sem=pre_sems.at[1, g, x],
            device_id={"prefix": 2 * other + c}, device_id_type=MESH,
        )

    def pre_note(h, k):
        other = lax.rem(x + k, 4)
        return pltpu.make_async_remote_copy(
            src_ref=row_stat_send.at[h, other], dst_ref=pre_stat.at[h, x],
            send_sem=note_sems.at[0, h, k], recv_sem=note_sems.at[1, h, x],
            device_id={"prefix": 2 * other + c}, device_id_type=MESH,
        )

    def pre_own(g):
        return pltpu.make_async_copy(row_send.at[x, quarter(g)], pre_part.at[x, quarter(g)], pre_sems.at[0, g, 0])

    def note_own(h):
        return pltpu.make_async_copy(row_stat_send.at[h, x], pre_stat.at[h, x], note_sems.at[0, h, 0])

    def quarter(g):
        return pl.ds(pl.multiple_of(32 * g, 32), 32)

    def pack_half(h):
        high_all, total_all = lax.fori_loop(
            4 * h, 4 * h + 4, pack, (jnp.full((ROWS, 128), NONE, f32), jnp.zeros((ROWS, 128), f32))
        )
        for d in range(8):
            stat_send[h, d, 0:8, :] = high_all[8 * d:8 * d + 8]
            stat_send[h, d, 8:16, :] = total_all[8 * d:8 * d + 8]
        for copy in core_copies(h):
            copy.start()

    def join_cores(h):
        for copy in core_copies(h):
            copy.wait_recv()

        def scales(to):
            d = 4 * c + to
            high_a, high_b = stat_send[h, d, 0:8, :], core_stat[h, to, 0:8, :]
            high = jnp.maximum(high_a, high_b)
            f_a, f_b = jnp.exp2(high_a - high) * 0.5, jnp.exp2(high_b - high) * 0.5
            row_stat_send[h, to, 0:8, :] = high + 1.0
            row_stat_send[h, to, 8:16, :] = f_a * stat_send[h, d, 8:16, :] + f_b * core_stat[h, to, 8:16, :]
            return f_a, f_b

        factors = [scales(to) for to in range(4)]
        for g in (2 * h, 2 * h + 1):
            for to, (f_a, f_b) in enumerate(factors):
                for i in (2 * g, 2 * g + 1):
                    rows = slice(16 * i, 16 * i + 16)

                    def column(a):
                        return jnp.concatenate([a[:, 2 * i + j:2 * i + j + 1] for j in range(2)], axis=0)

                    value = (
                        part_send[4 * c + to, rows, :].astype(f32) * column(f_a)
                        + core_part[to, rows, :].astype(f32) * column(f_b)
                    )
                    row_send[to, rows, :] = jnp.round(value).astype(jnp.int32).astype(LINK)
            for k in (2, 1, 3):
                if g == 2 * h:
                    pre_note(h, k).start()
                pre_copy(g, k).start()
            if g == 2 * h:
                note_own(h).start()
            pre_own(g).start()

    lane8 = lax.broadcasted_iota(jnp.int32, (8, 128), 1)
    def q_arrived(h):
        q_own(h).wait()
        half = pl.ds(64 * h, 64)
        for k in range(1, 4):
            source = lax.rem(n + k, 4)
            landed = q_all.at[source, half]
            pltpu.make_async_copy(landed, landed, q_sems.at[1, h, source]).wait()


    def mix_copies(g, k):
        other = lax.rem(n + k, 4)
        return [
            pltpu.make_async_remote_copy(
                src_ref=mix_send.at[other, quarter(g)], dst_ref=mix_part.at[n, quarter(g)],
                send_sem=mix_sems.at[0, g, 0, k], recv_sem=mix_sems.at[1, g, 0, n],
                device_id={"narrow": other}, device_id_type=MESH,
            ),
            pltpu.make_async_remote_copy(
                src_ref=mix_stat_send.at[g, other], dst_ref=mix_stat.at[g, n],
                send_sem=mix_sems.at[0, g, 1, k], recv_sem=mix_sems.at[1, g, 1, n],
                device_id={"narrow": other}, device_id_type=MESH,
            ),
        ]

    def mix_own(g):
        return [
            pltpu.make_async_copy(mix_send.at[n, quarter(g)], mix_part.at[n, quarter(g)], mix_sems.at[0, g, 0, 0]),
            pltpu.make_async_copy(mix_stat_send.at[g, n], mix_stat.at[g, n], mix_sems.at[0, g, 1, 0]),
        ]

    mix_iota = lax.broadcasted_iota(jnp.int32, (32, TILE), 1)

    def mix_scores(i, u):
        rows = pl.ds(pl.multiple_of(16 * i, 16), 16)
        queries = jnp.concatenate([q_all[m, rows, :] for m in range(4)], axis=0)
        found = []
        for j in range(2):
            score = lax.dot_general(
                queries, suffix_ref[2 * i + j], (((1,), (1,)), ((), ())), preferred_element_type=f32
            )
            score = jnp.concatenate([score[16 * m + 8 * j:16 * m + 8 * j + 8] for m in range(4)], axis=0) * TO_LOG2
            score = jnp.where(mix_iota < len_ref[2 * i + j] - n * TILE, score, MASKED)
            high = jnp.maximum(jnp.max(score, axis=1, keepdims=True), NONE)
            expo = jnp.exp2(score - high)
            weight2[2 * u + j] = expo.astype(bf16)
            found.append((high, jnp.sum(expo, axis=1, keepdims=True)))
        return found

    def mix_pairs(g, carry):
        stats = [jnp.full((8, 128), NONE, f32)] * 4 + [jnp.zeros((8, 128), f32)] * 4
        ready = [mix_scores(2 * g + u, u) for u in range(2)]
        for u, found in enumerate(ready):
            i = 2 * g + u
            codes = []
            for j, (high, total) in enumerate(found):
                part = jnp.dot(
                    weight2[2 * u + j], suffix_ref[2 * i + j, :, :LAT], preferred_element_type=f32
                )
                code, high, total = coded(part, high, total)
                codes.append(code)
                for m in range(4):
                    rows = slice(8 * m, 8 * m + 8)
                    stats[m] = jnp.where(lane8 == 2 * i + j, high[rows], stats[m])
                    stats[4 + m] = jnp.where(lane8 == 2 * i + j, total[rows], stats[4 + m])
            for m in range(4):
                rows = slice(8 * m, 8 * m + 8)
                mix_send[m, pl.ds(pl.multiple_of(16 * i, 16), 16), :] = jnp.concatenate(
                    [codes[0][rows], codes[1][rows]], axis=0
                ).astype(LINK)
        for m in range(4):
            mix_stat_send[g, m, 0:8, :] = stats[m]
            mix_stat_send[g, m, 8:16, :] = stats[4 + m]
        for k in (2, 1, 3):
            for copy in mix_copies(g, k):
                copy.start()
        for copy in mix_own(g):
            copy.start()
        return carry

    def send_on(g):
        return pltpu.make_async_remote_copy(
            src_ref=done.at[pl.ds(4 * g, 4)], dst_ref=out_ref.at[pl.ds(4 * g, 4)],
            send_sem=end_sems.at[0, g], recv_sem=end_sems.at[1, g],
            device_id=across, device_id_type=MESH,
        )

    far = lax.rem(x + 2, 4) == n

    def send_round(g):
        return pltpu.make_async_remote_copy(
            src_ref=done.at[pl.ds(4 * g, 4)], dst_ref=passing.at[pl.ds(4 * g, 4)],
            send_sem=end_sems.at[0, g], recv_sem=pass_sems.at[1, g],
            device_id={"narrow": x}, device_id_type=MESH,
        )

    def pass_on(g):
        return pltpu.make_async_remote_copy(
            src_ref=passing.at[pl.ds(4 * g, 4)], dst_ref=out_ref.at[pl.ds(4 * g, 4)],
            send_sem=pass_sems.at[0, g], recv_sem=end_sems.at[1, g],
            device_id={"prefix": 2 * lax.rem(x + 2, 4) + c}, device_id_type=MESH,
        )

    def finish(g):
        h = g // 2
        if g % 2 == 0:
            note_own(h).wait()
            for k in range(1, 4):
                noted = pre_stat.at[h, lax.rem(x + k, 4)]
                pltpu.make_async_copy(noted, noted, note_sems.at[1, h, lax.rem(x + k, 4)]).wait()
        pre_own(g).wait()
        for k in range(1, 4):
            landed = pre_part.at[lax.rem(x + k, 4), quarter(g)]
            pltpu.make_async_copy(landed, landed, pre_sems.at[1, g, lax.rem(x + k, 4)]).wait()
        for copy in mix_own(g):
            copy.wait()
        for k in range(1, 4):
            source = lax.rem(n + k, 4)
            landed = mix_part.at[source, quarter(g)]
            noted = mix_stat.at[g, source]
            pltpu.make_async_copy(landed, landed, mix_sems.at[1, g, 0, source]).wait()
            pltpu.make_async_copy(noted, noted, mix_sems.at[1, g, 1, source]).wait()

        highs = [pre_stat[h, i, 0:8, :] for i in range(4)] + [mix_stat[g, m, 0:8, :] for m in range(4)]
        totals = [pre_stat[h, i, 8:16, :] for i in range(4)] + [mix_stat[g, m, 8:16, :] for m in range(4)]
        highs += list(new_highs)
        totals += [1.0, 1.0]
        highest = functools.reduce(jnp.maximum, highs)
        factors = [jnp.exp2(high - highest) for high in highs]
        total = sum(f * t for f, t in zip(factors, totals))
        inverse = 1.0 / jnp.where(lax.div(lane8, 4) == g, total, 1.0)
        factors = [f * inverse for f in factors]
        for i in range(2 * g, 2 * g + 2):
            rows = slice(16 * i, 16 * i + 16)
            value = jnp.zeros((16, LAT), f32)
            for at, f in enumerate(factors):
                columns = [f[:, 2 * i + j:2 * i + j + 1] for j in range(2)]
                if at < 8:
                    source = pre_part[at, rows, :] if at < 4 else mix_part[at - 4, rows, :]
                    value = value + source.astype(f32) * jnp.concatenate(columns, axis=0)
                else:
                    u = at - 8
                    new = [new_ref[2 * i + j].astype(f32)[u:u + 1, :LAT] for j in range(2)]
                    value = value + jnp.concatenate([a * b for a, b in zip(columns, new)], axis=0)
            for j in range(2):
                for t in range(2):
                    at = 8 * j + 4 * t
                    done[2 * i + j, t] = value[at:at + 4].astype(bf16)

        @pl.when(stays)
        def _():
            out_ref[4 * g:4 * g + 4] = done[4 * g:4 * g + 4]

        if g < ROUND:
            @pl.when(far)
            def _():
                send_round(g).start()

        @pl.when(jnp.logical_not(stays | far) if g < ROUND else jnp.logical_not(stays))
        def _():
            send_on(g).start()

    lax.fori_loop(0, SLOTS_A // FUSED, tile_group, 0)
    for k in (7, 8, 9):
        loads[k].wait()
    pack_half(0)
    lax.fori_loop(SLOTS_A // FUSED + 0, SLOTS_A // FUSED + 1, tile_group, 0)
    join_cores(0)
    loads[1].wait()
    loads[6].wait()
    q_arrived(0)
    lax.fori_loop(0, 2, mix_pairs, 0)
    pack_half(1)
    q_arrived(1)
    lax.fori_loop(2, 3, mix_pairs, 0)
    join_cores(1)
    lax.fori_loop(3, 4, mix_pairs, 0)
    loads[3].wait()
    step8 = lax.broadcasted_iota(jnp.int32, (8, 1), 0) >= 4

    def new_scores(i, carry):
        queries = q_send[mine, pl.ds(pl.multiple_of(16 * i, 16), 16), :].astype(f32)
        out = list(carry)
        for j in range(2):
            keys = new_ref[2 * i + j].astype(f32)
            for u in range(2):
                score = jnp.sum(queries[8 * j:8 * j + 8] * keys[u:u + 1], axis=1, keepdims=True) * TO_LOG2
                if u == 1:
                    score = jnp.where(step8, score, NONE)
                out[u] = jnp.where(lane8 == 2 * i + j, score, out[u])
        return tuple(out)

    new_highs = lax.fori_loop(0, 8, new_scores, tuple([jnp.full((8, 128), NONE, f32)] * 2))

    finish(0)
    finish(1)
    finish(2)
    finish(3)

    @pl.when(stays)
    def _():
        for g in range(ROUND):
            landed = passing.at[pl.ds(4 * g, 4)]
            pltpu.make_async_copy(landed, landed, pass_sems.at[1, g]).wait()
            pass_on(g).start()
        for g in range(ROUND):
            pass_on(g).wait_send()


    for h in range(2):
        for k in range(1, 4):
            q_copy(h, k).wait_send()
    for h in range(2):
        for copy in core_copies(h):
            copy.wait_send()
        for k in range(1, 4):
            pre_note(h, k).wait_send()
            pre_copy(2 * h, k).wait_send()
            pre_copy(2 * h + 1, k).wait_send()
    for g in range(4):
        for k in range(1, 4):
            for copy in mix_copies(g, k):
                copy.wait_send()

    @pl.when(jnp.logical_not(stays))
    def _():
        for g in range(4):
            send_on(g).wait()


def fused(counts, lens, lists, new_latent, queries, cache, suffix, spilled):
    dma = pltpu.SemaphoreType.DMA
    f32, bf16, i32 = jnp.float32, jnp.bfloat16, jnp.int32
    return pl.pallas_call(
        fused_kernel,
        out_shape=jax.ShapeDtypeStruct((16, 2, 4, LAT), bf16),
        in_specs=[pl.BlockSpec(memory_space=pl.ANY)] * 8,
        out_specs=pl.BlockSpec(memory_space=pltpu.VMEM),
        scratch_shapes=[
            pltpu.SMEM((16,), i32),
            pltpu.SMEM((16,), i32),
            pltpu.VMEM((16, 64), i32),
            pltpu.VMEM((16, 2, KV), bf16),
            pltpu.VMEM((16, ROWS, KV), bf16),
            pltpu.VMEM((16, ROWS, KV), bf16),
            pltpu.VMEM((8, 128, KV), bf16),
            pltpu.VMEM((4, 128, KV), bf16),
            pltpu.VMEM((64, PAGE, KV), bf16),
            pltpu.VMEM((16, TILE, KV), bf16),
            pltpu.VMEM((24, 256), i32),
            pltpu.SMEM((24, 256), i32),
            pltpu.VMEM((SLOTS + 17, ROWS, LAT), f32),
            pltpu.VMEM((SLOTS + 17, ROWS, 128), f32),
            pltpu.VMEM((SLOTS + 17, ROWS, 128), f32),
            pltpu.VMEM((FUSED, ROWS, TILE), bf16),
            pltpu.VMEM((4, 32, TILE), bf16),
            pltpu.VMEM((8, 128, LAT), LINK),
            pltpu.VMEM((2, 8, 16, 128), f32),
            pltpu.VMEM((4, 128, LAT), LINK),
            pltpu.VMEM((2, 4, 16, 128), f32),
            pltpu.VMEM((4, 128, LAT), LINK),
            pltpu.VMEM((2, 4, 16, 128), f32),
            pltpu.VMEM((4, 128, LAT), LINK),
            pltpu.VMEM((2, 4, 16, 128), f32),
            pltpu.VMEM((4, 128, LAT), LINK),
            pltpu.VMEM((4, 4, 16, 128), f32),
            pltpu.VMEM((4, 128, LAT), LINK),
            pltpu.VMEM((4, 4, 16, 128), f32),
            pltpu.VMEM((16, 2, 4, LAT), bf16),
            pltpu.VMEM((4 * ROUND, 2, 4, LAT), bf16),
            dma((10,)),
            dma((3,)),
            dma((2, 2, 4)),
            dma((2, 2, 2)),
            dma((2, 4, 4)),
            dma((2, 2, 4)),
            dma((2, 4, 2, 4)),
            dma((2, 4)),
            dma((2, ROUND)),
        ],
        compiler_params=pltpu.CompilerParams(
            collective_id=1, has_side_effects=True, vmem_limit_bytes=52 << 20
        ),
        name="fused",
    )(counts, lens, lists, new_latent, queries, cache, suffix, spilled)


def local(queries, new_latent, prefix_cache, suffix_cache, page_lists, prefix_count, suffix_len):
    rows = queries.reshape(16, ROWS, KV)
    suffix = suffix_cache.reshape(16, TILE, KV)
    spilled = spill(prefix_count, page_lists, rows, prefix_cache)
    return fused(
        prefix_count, suffix_len, page_lists, new_latent, rows, prefix_cache, suffix, spilled
    )


def solution(mesh):
    return jax.shard_map(
        local,
        mesh=mesh,
        in_specs=(
            P("batch", None, "narrow", None),
            P("batch", None, None),
            P("prefix", None, None),
            P("batch", "narrow", None, None),
            P("batch", None),
            P("batch"),
            P("batch"),
        ),
        out_specs=P("batch", None, ("prefix", "narrow"), None),
        check_vma=False,
    )
```

```python
import functools

import jax
import jax.numpy as jnp
from jax import lax
from jax.experimental import pallas as pl
from jax.experimental.pallas import tpu as pltpu
from jax.sharding import PartitionSpec as P

MESH = pl.DeviceIdType.MESH
LAT = 512
KV = 576
PAGE = 64
ROWS = 64
GROUP = 4
TILE = GROUP * PAGE
UNROLL = 4
NONE = -30000.0
MASKED = -1e30
TO_LOG2 = 192 ** -0.5 * 1.4426950408889634
LINK = jnp.int16
STEPS_OF = 32767.0
SMALL = 1e-28


def by_owner(a):
    width = a.shape[-1]
    first = a[:32].reshape(4, 8, width)
    second = a[32:].reshape(4, 8, width)
    low = lax.broadcasted_iota(jnp.int32, (4, 8, width), 1) < 4
    even = jnp.where(low, first, pltpu.roll(second, 4, 1))
    odd = jnp.where(low, pltpu.roll(first, 4, 1), second)
    return [(even if d % 2 == 0 else odd)[d // 2] for d in range(8)]


def coded(part, high, total):
    largest = jnp.maximum(jnp.max(jnp.abs(part), axis=1, keepdims=True), SMALL)
    code = jnp.round(part * (STEPS_OF / largest)).astype(jnp.int32)
    return code, high + jnp.log2(largest * (1.0 / STEPS_OF)), total * (STEPS_OF / largest)


def wide(a):
    return jnp.concatenate([a] * 4, axis=1)


def owner_of(prefix):
    return 4 * lax.rem(prefix, 2) + lax.div(prefix, 2)


SLOTS_A = 24
SLOTS = 36
FUSED = 12
ROUND = 2


def by_lane(column):
    row = lax.broadcasted_iota(jnp.int32, (16, 256), 0)
    lane = lax.broadcasted_iota(jnp.int32, (16, 256), 1)
    return jnp.sum(jnp.where(row == lane, column, 0.0), axis=0, keepdims=True).astype(jnp.int32)


def tile_plan(lists, count_ref, base):
    f32 = jnp.float32
    row = lax.broadcasted_iota(jnp.int32, (16, 64), 0)
    col = lax.broadcasted_iota(jnp.int32, (16, 64), 1)
    counts = jnp.zeros((16, 64), jnp.int32)
    for b in range(16):
        counts = jnp.where(row == b, count_ref[b], counts)
    local = lists - base
    used = (col < counts) & (local >= 0) & (local < 64)
    number = jnp.sum(jnp.where(used, 1.0, 0.0), axis=1, keepdims=True)
    number = jnp.broadcast_to(number, (16, 256))
    tiles = jnp.floor((number + (GROUP - 1)) * (1.0 / GROUP))
    earlier = jnp.where(
        lax.broadcasted_iota(jnp.int32, (16, 16), 1) < lax.broadcasted_iota(jnp.int32, (16, 16), 0), 1.0, 0.0
    ).astype(jnp.bfloat16)
    start = jnp.dot(earlier, tiles.astype(jnp.bfloat16), preferred_element_type=f32)
    room = jnp.where(lax.broadcasted_iota(jnp.int32, (16, 256), 0) < 8, float(SLOTS_A), float(SLOTS))
    kept = jnp.clip(room - start, 0.0, tiles)
    return local, used, number, tiles, start, kept


def pack_pages(meta_v, local, used):
    f32 = jnp.float32
    page_t = jnp.transpose(jnp.where(used, local, -1).astype(f32))
    used_t = jnp.where(page_t >= 0, 1.0, 0.0)
    before = jnp.where(
        lax.broadcasted_iota(jnp.int32, (64, 64), 1) < lax.broadcasted_iota(jnp.int32, (64, 64), 0), 1.0, 0.0
    ).astype(jnp.bfloat16)
    rank = jnp.dot(before, used_t.astype(jnp.bfloat16), preferred_element_type=f32)
    place = jnp.where(used_t > 0, rank, -1.0)
    place_iota = lax.broadcasted_iota(jnp.int32, (64, 128), 1).astype(f32)
    for b in range(16):
        hit = place[:, b:b + 1] == place_iota
        packed = jnp.sum(jnp.where(hit, page_t[:, b:b + 1], 0.0), axis=0, keepdims=True)
        meta_v[b:b + 1, 0:128] = packed.astype(jnp.int32)


def spill_kernel(
    count_any, lists_any, q_any, cache_any, out_any,
    count_ref, lists_ref, q_ref, cache_ref, meta_v, meta_s, acc, stat, sems,
):
    f32 = jnp.float32
    loads = [
        pltpu.make_async_copy(count_any, count_ref, sems.at[0]),
        pltpu.make_async_copy(lists_any, lists_ref, sems.at[1]),
    ]
    for copy in loads:
        copy.start()
    for copy in loads:
        copy.wait()
    local, used, number, tiles, start, kept = tile_plan(
        lists_ref[...], count_ref, lax.axis_index("prefix") * 64
    )

    @pl.when(jnp.max(tiles - kept) > 0.5)
    def _():
        large = [
            pltpu.make_async_copy(q_any, q_ref, sems.at[0]),
            pltpu.make_async_copy(cache_any, cache_ref, sems.at[1]),
        ]
        for copy in large:
            copy.start()
        meta_v[...] = jnp.zeros_like(meta_v)
        pack_pages(meta_v, local, used)
        meta_v[16:17, :] = by_lane(kept)
        meta_v[17:18, :] = by_lane(tiles)
        meta_v[18:19, :] = by_lane(number)
        noted = pltpu.make_async_copy(meta_v, meta_s, sems.at[2])
        noted.start()
        noted.wait()
        for copy in large:
            copy.wait()
        key_iota = lax.broadcasted_iota(jnp.int32, (ROWS, TILE), 1)

        def branch(b, carry):
            acc[b] = jnp.zeros((ROWS, LAT), f32)
            stat[0, b] = jnp.full((ROWS, 128), NONE, f32)
            stat[1, b] = jnp.zeros((ROWS, 128), f32)

            def tile(k, carry):
                at = GROUP * k
                keys = jnp.concatenate([cache_ref[meta_s[b, at + i]] for i in range(GROUP)], axis=0)
                score = lax.dot_general(
                    q_ref[b], keys, (((1,), (1,)), ((), ())), preferred_element_type=f32
                ) * TO_LOG2
                score = jnp.where(key_iota < (meta_s[18, b] - at) * PAGE, score, MASKED)
                high = jnp.maximum(jnp.max(score, axis=1, keepdims=True), NONE)
                expo = jnp.exp2(score - high)
                total = jnp.sum(expo, axis=1, keepdims=True)
                part = jnp.dot(expo.astype(jnp.bfloat16), keys[:, :LAT], preferred_element_type=f32)
                old = stat[0, b]
                new = jnp.maximum(old, high)
                f_old = jnp.exp2(old - new)
                f_new = jnp.exp2(high - new)
                stat[0, b] = new
                stat[1, b] = stat[1, b] * f_old + total * f_new
                acc[b] = acc[b] * wide(f_old) + part * wide(f_new)
                return carry

            lax.fori_loop(meta_s[16, b], meta_s[17, b], tile, 0)
            acc[b] = jnp.concatenate(by_owner(acc[b]), axis=0)
            stat[0, b] = jnp.concatenate(by_owner(stat[0, b]), axis=0)
            stat[1, b] = jnp.concatenate(by_owner(stat[1, b]), axis=0)
            return carry

        lax.fori_loop(0, 16, branch, 0)
        out = [
            pltpu.make_async_copy(acc, out_any.at[:, :, 0:LAT], sems.at[0]),
            pltpu.make_async_copy(stat.at[0], out_any.at[:, :, LAT:LAT + 128], sems.at[1]),
            pltpu.make_async_copy(stat.at[1], out_any.at[:, :, LAT + 128:LAT + 256], sems.at[2]),
        ]
        for copy in out:
            copy.start()
        for copy in out:
            copy.wait()


def spill(counts, lists, queries, cache):
    return pl.pallas_call(
        spill_kernel,
        out_shape=jax.ShapeDtypeStruct((16, ROWS, 2048), jnp.float32),
        in_specs=[pl.BlockSpec(memory_space=pl.ANY)] * 4,
        out_specs=pl.BlockSpec(memory_space=pl.ANY),
        scratch_shapes=[
            pltpu.SMEM((16,), jnp.int32),
            pltpu.VMEM((16, 64), jnp.int32),
            pltpu.VMEM((16, ROWS, KV), jnp.bfloat16),
            pltpu.VMEM((64, PAGE, KV), jnp.bfloat16),
            pltpu.VMEM((24, 256), jnp.int32),
            pltpu.SMEM((24, 256), jnp.int32),
            pltpu.VMEM((16, ROWS, LAT), jnp.float32),
            pltpu.VMEM((2, 16, ROWS, 128), jnp.float32),
            pltpu.SemaphoreType.DMA((3,)),
        ],
        compiler_params=pltpu.CompilerParams(vmem_limit_bytes=60 << 20),
        name="spill",
    )(counts, lists, queries, cache)


def fused_kernel(
    count_any, len_any, lists_any, new_any, q_any, cache_any, suffix_any, spill_any, out_ref,
    count_ref, len_ref, lists_ref, new_ref, q_ref, q_rows, q_send, q_all, cache_ref, suffix_ref,
    meta_v, meta_s, acc, top, tot, weight, weight2,
    part_send, stat_send, core_part, core_stat, row_send, row_stat_send, pre_part, pre_stat, mix_send, mix_stat_send, mix_part, mix_stat, done, passing,
    in_sems, own_sems, q_sems, core_sems, pre_sems, note_sems, mix_sems, end_sems, pass_sems,
):
    f32 = jnp.float32
    bf16 = jnp.bfloat16
    p = lax.axis_index("prefix")
    n = lax.axis_index("narrow")
    x = lax.div(p, 2)
    c = lax.rem(p, 2)
    mine = owner_of(p)
    stays = x == n
    across = {"prefix": 2 * n + c, "narrow": x}

    loads = [
        pltpu.make_async_copy(source, target, in_sems.at[k])
        for k, (source, target) in enumerate([
            (count_any, count_ref), (len_any, len_ref), (lists_any, lists_ref), (new_any, new_ref),
            (q_any, q_ref), (cache_any, cache_ref), (suffix_any, suffix_ref),
            (spill_any.at[:, :, 0:LAT], acc.at[pl.ds(SLOTS + 1, 16)]),
            (spill_any.at[:, :, LAT:LAT + 128], top.at[pl.ds(SLOTS + 1, 16)]),
            (spill_any.at[:, :, LAT + 128:LAT + 256], tot.at[pl.ds(SLOTS + 1, 16)]),
        ])
    ]
    barrier = pltpu.get_barrier_semaphore()

    def greet(**to):
        pl.semaphore_signal(barrier, inc=1, device_id=to, device_id_type=MESH)

    greet(prefix=2 * x + 1 - c)
    for k in range(1, 4):
        greet(prefix=2 * lax.rem(x + k, 4) + c)
        greet(narrow=lax.rem(n + k, 4))

    @pl.when(jnp.logical_not(stays))
    def _():
        greet(**across)

    for k in (0, 2, 4, 5, 1):
        loads[k].start()

    meta_v[...] = jnp.zeros_like(meta_v)
    acc[0] = jnp.zeros((ROWS, LAT), f32)
    top[0] = jnp.full((ROWS, 128), NONE, f32)
    tot[0] = jnp.zeros((ROWS, 128), f32)
    loads[0].wait()
    loads[2].wait()
    local, used, number, tiles, start, kept = tile_plan(lists_ref[...], count_ref, 64 * p)
    pack_pages(meta_v, local, used)
    slot = lax.broadcasted_iota(jnp.int32, (16, 256), 1).astype(f32)
    inside = (slot >= start) & (slot < start + tiles)
    branch = lax.broadcasted_iota(jnp.int32, (16, 256), 0).astype(f32)

    def pick(a):
        return jnp.sum(jnp.where(inside, a, 0.0), axis=0, keepdims=True).astype(jnp.int32)

    meta_v[16:17, :] = pick(branch)
    meta_v[17:18, :] = pick((slot - start) * GROUP)
    meta_v[18:19, :] = pick(jnp.clip(number - (slot - start) * GROUP, 0.0, float(GROUP)) * PAGE)
    meta_v[19:20, :] = pick(jnp.where(slot == start, NONE, -NONE))
    meta_v[20:21, :] = by_lane(jnp.where(kept > 0, start + kept, 0.0))
    meta_v[21:22, :] = by_lane(jnp.where(tiles > kept, branch + (SLOTS + 1.0), 0.0))
    meta_copy = pltpu.make_async_copy(meta_v, meta_s, own_sems.at[0])
    meta_copy.start()

    loads[4].wait()

    def order(i, carry):
        left = by_owner(q_ref[2 * i].astype(f32))
        right = by_owner(q_ref[2 * i + 1].astype(f32))
        q_rows[2 * i] = jnp.concatenate(left, axis=0).astype(bf16)
        q_rows[2 * i + 1] = jnp.concatenate(right, axis=0).astype(bf16)
        for d in range(8):
            q_send[d, pl.ds(pl.multiple_of(16 * i, 16), 16), :] = jnp.concatenate(
                [left[d], right[d]], axis=0
            ).astype(bf16)
        return carry

    def q_own(h):
        half = pl.ds(64 * h, 64)
        return pltpu.make_async_copy(q_send.at[mine, half], q_all.at[n, half], own_sems.at[1 + h])

    def q_copy(h, k):
        half = pl.ds(64 * h, 64)
        return pltpu.make_async_remote_copy(
            src_ref=q_send.at[mine, half], dst_ref=q_all.at[n, half],
            send_sem=q_sems.at[0, h, k], recv_sem=q_sems.at[1, h, n],
            device_id={"narrow": lax.rem(n + k, 4)}, device_id_type=MESH,
        )

    lax.fori_loop(0, 4, order, 0)
    pl.semaphore_wait(barrier, jnp.where(stays, 7, 8))
    for k in (2, 1, 3):
        q_copy(0, k).start()
    lax.fori_loop(4, 8, order, 0)
    for k in (2, 1, 3):
        q_copy(1, k).start()
    for h in range(2):
        q_own(h).start()

    meta_copy.wait()
    loads[5].wait()
    for k in (6, 3, 7, 8, 9):
        loads[k].start()
    key_iota = lax.broadcasted_iota(jnp.int32, (ROWS, TILE), 1)

    def tile_scores(s, u):
        b = jnp.clip(meta_s[16, s], 0, 15)
        k = jnp.clip(meta_s[17, s], 0, 60)
        live = meta_s[18, s]
        pages = [jnp.clip(meta_s[b, k + i], 0, 63) for i in range(GROUP)]
        keys = jnp.concatenate([cache_ref[page] for page in pages], axis=0)
        score = lax.dot_general(
            q_rows[b], keys, (((1,), (1,)), ((), ())), preferred_element_type=f32
        ) * TO_LOG2
        score = jnp.where(key_iota < live, score, MASKED)
        high = jnp.maximum(jnp.max(score, axis=1, keepdims=True), NONE)
        expo = jnp.exp2(score - high)
        weight[u] = expo.astype(bf16)
        return pages, high, jnp.sum(expo, axis=1, keepdims=True)

    def tile_group(i, carry):
        ready = [tile_scores(i * FUSED + u, u) for u in range(FUSED)]
        for u, (pages, high, total) in enumerate(ready):
            s = i * FUSED + u
            values = jnp.concatenate([cache_ref[page, :, :LAT] for page in pages], axis=0)
            part = jnp.dot(weight[u], values, preferred_element_type=f32)
            old = jnp.minimum(top[s], meta_s[19, s].astype(f32))
            new = jnp.maximum(old, high)
            f_old = jnp.exp2(old - new)
            f_new = jnp.exp2(high - new)
            top[s + 1] = new
            tot[s + 1] = tot[s] * f_old + total * f_new
            acc[s + 1] = acc[s] * wide(f_old) + part * wide(f_new)
        return carry

    lane64 = lax.broadcasted_iota(jnp.int32, (ROWS, 128), 1)

    def pack(i, carry):
        high_all, total_all = carry
        pieces = []
        for b in (2 * i, 2 * i + 1):
            at = jnp.clip(meta_s[20, b], 0, SLOTS)
            more = jnp.clip(meta_s[21, b], 0, SLOTS + 16)
            high = jnp.maximum(top[at], top[more])
            f_at = jnp.exp2(top[at] - high)
            f_more = jnp.exp2(top[more] - high)
            part = acc[at] * wide(f_at) + acc[more] * wide(f_more)
            code, high, total = coded(part, high, tot[at] * f_at + tot[more] * f_more)
            high_all = jnp.where(lane64 == b, high, high_all)
            total_all = jnp.where(lane64 == b, total, total_all)
            pieces.append(code)
        left, right = pieces
        for d in range(8):
            rows = slice(8 * d, 8 * d + 8)
            part_send[d, pl.ds(pl.multiple_of(16 * i, 16), 16), :] = jnp.concatenate(
                [left[rows], right[rows]], axis=0
            ).astype(LINK)
        return high_all, total_all

    def core_copies(h):
        other = 4 * (1 - c)
        half = pl.ds(64 * h, 64)
        return [
            pltpu.make_async_remote_copy(
                src_ref=part_send.at[pl.ds(other, 4), half], dst_ref=core_part.at[:, half],
                send_sem=core_sems.at[0, h, 0], recv_sem=core_sems.at[1, h, 0],
                device_id={"prefix": 2 * x + 1 - c}, device_id_type=MESH,
            ),
            pltpu.make_async_remote_copy(
                src_ref=stat_send.at[h, pl.ds(other, 4)], dst_ref=core_stat.at[h],
                send_sem=core_sems.at[0, h, 1], recv_sem=core_sems.at[1, h, 1],
                device_id={"prefix": 2 * x + 1 - c}, device_id_type=MESH,
            ),
        ]

    def pre_copy(g, k):
        other = lax.rem(x + k, 4)
        return pltpu.make_async_remote_copy(
            src_ref=row_send.at[other, quarter(g)], dst_ref=pre_part.at[x, quarter(g)],
            send_sem=pre_sems.at[0, g, k], recv_sem=pre_sems.at[1, g, x],
            device_id={"prefix": 2 * other + c}, device_id_type=MESH,
        )

    def pre_note(h, k):
        other = lax.rem(x + k, 4)
        return pltpu.make_async_remote_copy(
            src_ref=row_stat_send.at[h, other], dst_ref=pre_stat.at[h, x],
            send_sem=note_sems.at[0, h, k], recv_sem=note_sems.at[1, h, x],
            device_id={"prefix": 2 * other + c}, device_id_type=MESH,
        )

    def pre_own(g):
        return pltpu.make_async_copy(row_send.at[x, quarter(g)], pre_part.at[x, quarter(g)], pre_sems.at[0, g, 0])

    def note_own(h):
        return pltpu.make_async_copy(row_stat_send.at[h, x], pre_stat.at[h, x], note_sems.at[0, h, 0])

    def quarter(g):
        return pl.ds(pl.multiple_of(32 * g, 32), 32)

    def pack_half(h):
        high_all, total_all = lax.fori_loop(
            4 * h, 4 * h + 4, pack, (jnp.full((ROWS, 128), NONE, f32), jnp.zeros((ROWS, 128), f32))
        )
        for d in range(8):
            stat_send[h, d, 0:8, :] = high_all[8 * d:8 * d + 8]
            stat_send[h, d, 8:16, :] = total_all[8 * d:8 * d + 8]
        for copy in core_copies(h):
            copy.start()

    def join_cores(h):
        for copy in core_copies(h):
            copy.wait_recv()

        def scales(to):
            d = 4 * c + to
            high_a, high_b = stat_send[h, d, 0:8, :], core_stat[h, to, 0:8, :]
            high = jnp.maximum(high_a, high_b)
            f_a, f_b = jnp.exp2(high_a - high) * 0.5, jnp.exp2(high_b - high) * 0.5
            row_stat_send[h, to, 0:8, :] = high + 1.0
            row_stat_send[h, to, 8:16, :] = f_a * stat_send[h, d, 8:16, :] + f_b * core_stat[h, to, 8:16, :]
            return f_a, f_b

        factors = [scales(to) for to in range(4)]
        for g in (2 * h, 2 * h + 1):
            for to, (f_a, f_b) in enumerate(factors):
                for i in (2 * g, 2 * g + 1):
                    rows = slice(16 * i, 16 * i + 16)

                    def column(a):
                        return jnp.concatenate([a[:, 2 * i + j:2 * i + j + 1] for j in range(2)], axis=0)

                    value = (
                        part_send[4 * c + to, rows, :].astype(f32) * column(f_a)
                        + core_part[to, rows, :].astype(f32) * column(f_b)
                    )
                    row_send[to, rows, :] = jnp.round(value).astype(jnp.int32).astype(LINK)
            for k in (2, 1, 3):
                if g == 2 * h:
                    pre_note(h, k).start()
                pre_copy(g, k).start()
            if g == 2 * h:
                note_own(h).start()
            pre_own(g).start()

    lane8 = lax.broadcasted_iota(jnp.int32, (8, 128), 1)
    def q_arrived(h):
        q_own(h).wait()
        half = pl.ds(64 * h, 64)
        for k in range(1, 4):
            source = lax.rem(n + k, 4)
            landed = q_all.at[source, half]
            pltpu.make_async_copy(landed, landed, q_sems.at[1, h, source]).wait()


    def mix_copies(g, k):
        other = lax.rem(n + k, 4)
        return [
            pltpu.make_async_remote_copy(
                src_ref=mix_send.at[other, quarter(g)], dst_ref=mix_part.at[n, quarter(g)],
                send_sem=mix_sems.at[0, g, 0, k], recv_sem=mix_sems.at[1, g, 0, n],
                device_id={"narrow": other}, device_id_type=MESH,
            ),
            pltpu.make_async_remote_copy(
                src_ref=mix_stat_send.at[g, other], dst_ref=mix_stat.at[g, n],
                send_sem=mix_sems.at[0, g, 1, k], recv_sem=mix_sems.at[1, g, 1, n],
                device_id={"narrow": other}, device_id_type=MESH,
            ),
        ]

    def mix_own(g):
        return [
            pltpu.make_async_copy(mix_send.at[n, quarter(g)], mix_part.at[n, quarter(g)], mix_sems.at[0, g, 0, 0]),
            pltpu.make_async_copy(mix_stat_send.at[g, n], mix_stat.at[g, n], mix_sems.at[0, g, 1, 0]),
        ]

    mix_iota = lax.broadcasted_iota(jnp.int32, (32, TILE), 1)

    def mix_scores(i, u):
        rows = pl.ds(pl.multiple_of(16 * i, 16), 16)
        queries = jnp.concatenate([q_all[m, rows, :] for m in range(4)], axis=0)
        found = []
        for j in range(2):
            score = lax.dot_general(
                queries, suffix_ref[2 * i + j], (((1,), (1,)), ((), ())), preferred_element_type=f32
            )
            score = jnp.concatenate([score[16 * m + 8 * j:16 * m + 8 * j + 8] for m in range(4)], axis=0) * TO_LOG2
            score = jnp.where(mix_iota < len_ref[2 * i + j] - n * TILE, score, MASKED)
            high = jnp.maximum(jnp.max(score, axis=1, keepdims=True), NONE)
            expo = jnp.exp2(score - high)
            weight2[2 * u + j] = expo.astype(bf16)
            found.append((high, jnp.sum(expo, axis=1, keepdims=True)))
        return found

    def mix_pairs(g, carry):
        stats = [jnp.full((8, 128), NONE, f32)] * 4 + [jnp.zeros((8, 128), f32)] * 4
        ready = [mix_scores(2 * g + u, u) for u in range(2)]
        for u, found in enumerate(ready):
            i = 2 * g + u
            codes = []
            for j, (high, total) in enumerate(found):
                part = jnp.dot(
                    weight2[2 * u + j], suffix_ref[2 * i + j, :, :LAT], preferred_element_type=f32
                )
                code, high, total = coded(part, high, total)
                codes.append(code)
                for m in range(4):
                    rows = slice(8 * m, 8 * m + 8)
                    stats[m] = jnp.where(lane8 == 2 * i + j, high[rows], stats[m])
                    stats[4 + m] = jnp.where(lane8 == 2 * i + j, total[rows], stats[4 + m])
            for m in range(4):
                rows = slice(8 * m, 8 * m + 8)
                mix_send[m, pl.ds(pl.multiple_of(16 * i, 16), 16), :] = jnp.concatenate(
                    [codes[0][rows], codes[1][rows]], axis=0
                ).astype(LINK)
        for m in range(4):
            mix_stat_send[g, m, 0:8, :] = stats[m]
            mix_stat_send[g, m, 8:16, :] = stats[4 + m]
        for k in (2, 1, 3):
            for copy in mix_copies(g, k):
                copy.start()
        for copy in mix_own(g):
            copy.start()
        return carry

    def send_on(g):
        return pltpu.make_async_remote_copy(
            src_ref=done.at[pl.ds(4 * g, 4)], dst_ref=out_ref.at[pl.ds(4 * g, 4)],
            send_sem=end_sems.at[0, g], recv_sem=end_sems.at[1, g],
            device_id=across, device_id_type=MESH,
        )

    far = lax.rem(x + 2, 4) == n

    def send_round(g):
        return pltpu.make_async_remote_copy(
            src_ref=done.at[pl.ds(4 * g, 4)], dst_ref=passing.at[pl.ds(4 * g, 4)],
            send_sem=end_sems.at[0, g], recv_sem=pass_sems.at[1, g],
            device_id={"narrow": x}, device_id_type=MESH,
        )

    def pass_on(g):
        return pltpu.make_async_remote_copy(
            src_ref=passing.at[pl.ds(4 * g, 4)], dst_ref=out_ref.at[pl.ds(4 * g, 4)],
            send_sem=pass_sems.at[0, g], recv_sem=end_sems.at[1, g],
            device_id={"prefix": 2 * lax.rem(x + 2, 4) + c}, device_id_type=MESH,
        )

    def finish(g):
        h = g // 2
        if g % 2 == 0:
            note_own(h).wait()
            for k in range(1, 4):
                noted = pre_stat.at[h, lax.rem(x + k, 4)]
                pltpu.make_async_copy(noted, noted, note_sems.at[1, h, lax.rem(x + k, 4)]).wait()
        pre_own(g).wait()
        for k in range(1, 4):
            landed = pre_part.at[lax.rem(x + k, 4), quarter(g)]
            pltpu.make_async_copy(landed, landed, pre_sems.at[1, g, lax.rem(x + k, 4)]).wait()
        for copy in mix_own(g):
            copy.wait()
        for k in range(1, 4):
            source = lax.rem(n + k, 4)
            landed = mix_part.at[source, quarter(g)]
            noted = mix_stat.at[g, source]
            pltpu.make_async_copy(landed, landed, mix_sems.at[1, g, 0, source]).wait()
            pltpu.make_async_copy(noted, noted, mix_sems.at[1, g, 1, source]).wait()

        highs = [pre_stat[h, i, 0:8, :] for i in range(4)] + [mix_stat[g, m, 0:8, :] for m in range(4)]
        totals = [pre_stat[h, i, 8:16, :] for i in range(4)] + [mix_stat[g, m, 8:16, :] for m in range(4)]
        highs += list(new_highs)
        totals += [1.0, 1.0]
        highest = functools.reduce(jnp.maximum, highs)
        factors = [jnp.exp2(high - highest) for high in highs]
        total = sum(f * t for f, t in zip(factors, totals))
        inverse = 1.0 / jnp.where(lax.div(lane8, 4) == g, total, 1.0)
        factors = [f * inverse for f in factors]
        for i in range(2 * g, 2 * g + 2):
            rows = slice(16 * i, 16 * i + 16)
            value = jnp.zeros((16, LAT), f32)
            for at, f in enumerate(factors):
                columns = [f[:, 2 * i + j:2 * i + j + 1] for j in range(2)]
                if at < 8:
                    source = pre_part[at, rows, :] if at < 4 else mix_part[at - 4, rows, :]
                    value = value + source.astype(f32) * jnp.concatenate(columns, axis=0)
                else:
                    u = at - 8
                    new = [new_ref[2 * i + j].astype(f32)[u:u + 1, :LAT] for j in range(2)]
                    value = value + jnp.concatenate([a * b for a, b in zip(columns, new)], axis=0)
            for j in range(2):
                for t in range(2):
                    at = 8 * j + 4 * t
                    done[2 * i + j, t] = value[at:at + 4].astype(bf16)

        @pl.when(stays)
        def _():
            out_ref[4 * g:4 * g + 4] = done[4 * g:4 * g + 4]

        if g < ROUND:
            @pl.when(far)
            def _():
                send_round(g).start()

        @pl.when(jnp.logical_not(stays | far) if g < ROUND else jnp.logical_not(stays))
        def _():
            send_on(g).start()

    lax.fori_loop(0, SLOTS_A // FUSED, tile_group, 0)
    for k in (7, 8, 9):
        loads[k].wait()
    pack_half(0)
    lax.fori_loop(SLOTS_A // FUSED + 0, SLOTS_A // FUSED + 1, tile_group, 0)
    loads[1].wait()
    loads[6].wait()
    q_arrived(0)
    lax.fori_loop(0, 1, mix_pairs, 0)
    join_cores(0)
    lax.fori_loop(1, 2, mix_pairs, 0)
    pack_half(1)
    q_arrived(1)
    lax.fori_loop(2, 3, mix_pairs, 0)
    join_cores(1)
    lax.fori_loop(3, 4, mix_pairs, 0)
    loads[3].wait()
    step8 = lax.broadcasted_iota(jnp.int32, (8, 1), 0) >= 4

    def new_scores(i, carry):
        queries = q_send[mine, pl.ds(pl.multiple_of(16 * i, 16), 16), :].astype(f32)
        out = list(carry)
        for j in range(2):
            keys = new_ref[2 * i + j].astype(f32)
            for u in range(2):
                score = jnp.sum(queries[8 * j:8 * j + 8] * keys[u:u + 1], axis=1, keepdims=True) * TO_LOG2
                if u == 1:
                    score = jnp.where(step8, score, NONE)
                out[u] = jnp.where(lane8 == 2 * i + j, score, out[u])
        return tuple(out)

    new_highs = lax.fori_loop(0, 8, new_scores, tuple([jnp.full((8, 128), NONE, f32)] * 2))

    finish(0)
    finish(1)
    finish(2)
    finish(3)

    @pl.when(stays)
    def _():
        for g in range(ROUND):
            landed = passing.at[pl.ds(4 * g, 4)]
            pltpu.make_async_copy(landed, landed, pass_sems.at[1, g]).wait()
            pass_on(g).start()
        for g in range(ROUND):
            pass_on(g).wait_send()


    for h in range(2):
        for k in range(1, 4):
            q_copy(h, k).wait_send()
    for h in range(2):
        for copy in core_copies(h):
            copy.wait_send()
        for k in range(1, 4):
            pre_note(h, k).wait_send()
            pre_copy(2 * h, k).wait_send()
            pre_copy(2 * h + 1, k).wait_send()
    for g in range(4):
        for k in range(1, 4):
            for copy in mix_copies(g, k):
                copy.wait_send()

    @pl.when(jnp.logical_not(stays))
    def _():
        for g in range(4):
            send_on(g).wait()


def fused(counts, lens, lists, new_latent, queries, cache, suffix, spilled):
    dma = pltpu.SemaphoreType.DMA
    f32, bf16, i32 = jnp.float32, jnp.bfloat16, jnp.int32
    return pl.pallas_call(
        fused_kernel,
        out_shape=jax.ShapeDtypeStruct((16, 2, 4, LAT), bf16),
        in_specs=[pl.BlockSpec(memory_space=pl.ANY)] * 8,
        out_specs=pl.BlockSpec(memory_space=pltpu.VMEM),
        scratch_shapes=[
            pltpu.SMEM((16,), i32),
            pltpu.SMEM((16,), i32),
            pltpu.VMEM((16, 64), i32),
            pltpu.VMEM((16, 2, KV), bf16),
            pltpu.VMEM((16, ROWS, KV), bf16),
            pltpu.VMEM((16, ROWS, KV), bf16),
            pltpu.VMEM((8, 128, KV), bf16),
            pltpu.VMEM((4, 128, KV), bf16),
            pltpu.VMEM((64, PAGE, KV), bf16),
            pltpu.VMEM((16, TILE, KV), bf16),
            pltpu.VMEM((24, 256), i32),
            pltpu.SMEM((24, 256), i32),
            pltpu.VMEM((SLOTS + 17, ROWS, LAT), f32),
            pltpu.VMEM((SLOTS + 17, ROWS, 128), f32),
            pltpu.VMEM((SLOTS + 17, ROWS, 128), f32),
            pltpu.VMEM((FUSED, ROWS, TILE), bf16),
            pltpu.VMEM((4, 32, TILE), bf16),
            pltpu.VMEM((8, 128, LAT), LINK),
            pltpu.VMEM((2, 8, 16, 128), f32),
            pltpu.VMEM((4, 128, LAT), LINK),
            pltpu.VMEM((2, 4, 16, 128), f32),
            pltpu.VMEM((4, 128, LAT), LINK),
            pltpu.VMEM((2, 4, 16, 128), f32),
            pltpu.VMEM((4, 128, LAT), LINK),
            pltpu.VMEM((2, 4, 16, 128), f32),
            pltpu.VMEM((4, 128, LAT), LINK),
            pltpu.VMEM((4, 4, 16, 128), f32),
            pltpu.VMEM((4, 128, LAT), LINK),
            pltpu.VMEM((4, 4, 16, 128), f32),
            pltpu.VMEM((16, 2, 4, LAT), bf16),
            pltpu.VMEM((4 * ROUND, 2, 4, LAT), bf16),
            dma((10,)),
            dma((3,)),
            dma((2, 2, 4)),
            dma((2, 2, 2)),
            dma((2, 4, 4)),
            dma((2, 2, 4)),
            dma((2, 4, 2, 4)),
            dma((2, 4)),
            dma((2, ROUND)),
        ],
        compiler_params=pltpu.CompilerParams(
            collective_id=1, has_side_effects=True, vmem_limit_bytes=52 << 20
        ),
        name="fused",
    )(counts, lens, lists, new_latent, queries, cache, suffix, spilled)


def local(queries, new_latent, prefix_cache, suffix_cache, page_lists, prefix_count, suffix_len):
    rows = queries.reshape(16, ROWS, KV)
    suffix = suffix_cache.reshape(16, TILE, KV)
    spilled = spill(prefix_count, page_lists, rows, prefix_cache)
    return fused(
        prefix_count, suffix_len, page_lists, new_latent, rows, prefix_cache, suffix, spilled
    )


def solution(mesh):
    return jax.shard_map(
        local,
        mesh=mesh,
        in_specs=(
            P("batch", None, "narrow", None),
            P("batch", None, None),
            P("prefix", None, None),
            P("batch", "narrow", None, None),
            P("batch", None),
            P("batch"),
            P("batch"),
        ),
        out_specs=P("batch", None, ("prefix", "narrow"), None),
        check_vma=False,
    )
```

```python
import functools

import jax
import jax.numpy as jnp
from jax import lax
from jax.experimental import pallas as pl
from jax.experimental.pallas import tpu as pltpu
from jax.sharding import PartitionSpec as P

MESH = pl.DeviceIdType.MESH
LAT = 512
KV = 576
PAGE = 64
ROWS = 64
GROUP = 4
TILE = GROUP * PAGE
UNROLL = 4
NONE = -30000.0
MASKED = -1e30
TO_LOG2 = 192 ** -0.5 * 1.4426950408889634
LINK = jnp.int16
STEPS_OF = 32767.0
SMALL = 1e-28


def by_owner(a):
    width = a.shape[-1]
    first = a[:32].reshape(4, 8, width)
    second = a[32:].reshape(4, 8, width)
    low = lax.broadcasted_iota(jnp.int32, (4, 8, width), 1) < 4
    even = jnp.where(low, first, pltpu.roll(second, 4, 1))
    odd = jnp.where(low, pltpu.roll(first, 4, 1), second)
    return [(even if d % 2 == 0 else odd)[d // 2] for d in range(8)]


def coded(part, high, total):
    largest = jnp.maximum(jnp.max(jnp.abs(part), axis=1, keepdims=True), SMALL)
    code = jnp.round(part * (STEPS_OF / largest)).astype(jnp.int32)
    return code, high + jnp.log2(largest * (1.0 / STEPS_OF)), total * (STEPS_OF / largest)


def wide(a):
    return jnp.concatenate([a] * 4, axis=1)


def owner_of(prefix):
    return 4 * lax.rem(prefix, 2) + lax.div(prefix, 2)


SLOTS_A = 24
SLOTS = 36
FUSED = 12
ROUND = 2


def by_lane(column):
    row = lax.broadcasted_iota(jnp.int32, (16, 256), 0)
    lane = lax.broadcasted_iota(jnp.int32, (16, 256), 1)
    return jnp.sum(jnp.where(row == lane, column, 0.0), axis=0, keepdims=True).astype(jnp.int32)


def tile_plan(lists, count_ref, base):
    f32 = jnp.float32
    row = lax.broadcasted_iota(jnp.int32, (16, 64), 0)
    col = lax.broadcasted_iota(jnp.int32, (16, 64), 1)
    counts = jnp.zeros((16, 64), jnp.int32)
    for b in range(16):
        counts = jnp.where(row == b, count_ref[b], counts)
    local = lists - base
    used = (col < counts) & (local >= 0) & (local < 64)
    number = jnp.sum(jnp.where(used, 1.0, 0.0), axis=1, keepdims=True)
    number = jnp.broadcast_to(number, (16, 256))
    tiles = jnp.floor((number + (GROUP - 1)) * (1.0 / GROUP))
    earlier = jnp.where(
        lax.broadcasted_iota(jnp.int32, (16, 16), 1) < lax.broadcasted_iota(jnp.int32, (16, 16), 0), 1.0, 0.0
    ).astype(jnp.bfloat16)
    start = jnp.dot(earlier, tiles.astype(jnp.bfloat16), preferred_element_type=f32)
    room = jnp.where(lax.broadcasted_iota(jnp.int32, (16, 256), 0) < 8, float(SLOTS_A), float(SLOTS))
    kept = jnp.clip(room - start, 0.0, tiles)
    return local, used, number, tiles, start, kept


def pack_pages(meta_v, local, used):
    f32 = jnp.float32
    page_t = jnp.transpose(jnp.where(used, local, -1).astype(f32))
    used_t = jnp.where(page_t >= 0, 1.0, 0.0)
    before = jnp.where(
        lax.broadcasted_iota(jnp.int32, (64, 64), 1) < lax.broadcasted_iota(jnp.int32, (64, 64), 0), 1.0, 0.0
    ).astype(jnp.bfloat16)
    rank = jnp.dot(before, used_t.astype(jnp.bfloat16), preferred_element_type=f32)
    place = jnp.where(used_t > 0, rank, -1.0)
    place_iota = lax.broadcasted_iota(jnp.int32, (64, 128), 1).astype(f32)
    for b in range(16):
        hit = place[:, b:b + 1] == place_iota
        packed = jnp.sum(jnp.where(hit, page_t[:, b:b + 1], 0.0), axis=0, keepdims=True)
        meta_v[b:b + 1, 0:128] = packed.astype(jnp.int32)


def spill_kernel(
    count_any, lists_any, q_any, cache_any, out_any,
    count_ref, lists_ref, q_ref, cache_ref, meta_v, meta_s, acc, stat, sems,
):
    f32 = jnp.float32
    loads = [
        pltpu.make_async_copy(count_any, count_ref, sems.at[0]),
        pltpu.make_async_copy(lists_any, lists_ref, sems.at[1]),
    ]
    for copy in loads:
        copy.start()
    for copy in loads:
        copy.wait()
    local, used, number, tiles, start, kept = tile_plan(
        lists_ref[...], count_ref, lax.axis_index("prefix") * 64
    )

    @pl.when(jnp.max(tiles - kept) > 0.5)
    def _():
        large = [
            pltpu.make_async_copy(q_any, q_ref, sems.at[0]),
            pltpu.make_async_copy(cache_any, cache_ref, sems.at[1]),
        ]
        for copy in large:
            copy.start()
        meta_v[...] = jnp.zeros_like(meta_v)
        pack_pages(meta_v, local, used)
        meta_v[16:17, :] = by_lane(kept)
        meta_v[17:18, :] = by_lane(tiles)
        meta_v[18:19, :] = by_lane(number)
        noted = pltpu.make_async_copy(meta_v, meta_s, sems.at[2])
        noted.start()
        noted.wait()
        for copy in large:
            copy.wait()
        key_iota = lax.broadcasted_iota(jnp.int32, (ROWS, TILE), 1)

        def branch(b, carry):
            acc[b] = jnp.zeros((ROWS, LAT), f32)
            stat[0, b] = jnp.full((ROWS, 128), NONE, f32)
            stat[1, b] = jnp.zeros((ROWS, 128), f32)

            def tile(k, carry):
                at = GROUP * k
                keys = jnp.concatenate([cache_ref[meta_s[b, at + i]] for i in range(GROUP)], axis=0)
                score = lax.dot_general(
                    q_ref[b], keys, (((1,), (1,)), ((), ())), preferred_element_type=f32
                ) * TO_LOG2
                score = jnp.where(key_iota < (meta_s[18, b] - at) * PAGE, score, MASKED)
                high = jnp.maximum(jnp.max(score, axis=1, keepdims=True), NONE)
                expo = jnp.exp2(score - high)
                total = jnp.sum(expo, axis=1, keepdims=True)
                part = jnp.dot(expo.astype(jnp.bfloat16), keys[:, :LAT], preferred_element_type=f32)
                old = stat[0, b]
                new = jnp.maximum(old, high)
                f_old = jnp.exp2(old - new)
                f_new = jnp.exp2(high - new)
                stat[0, b] = new
                stat[1, b] = stat[1, b] * f_old + total * f_new
                acc[b] = acc[b] * wide(f_old) + part * wide(f_new)
                return carry

            lax.fori_loop(meta_s[16, b], meta_s[17, b], tile, 0)
            acc[b] = jnp.concatenate(by_owner(acc[b]), axis=0)
            stat[0, b] = jnp.concatenate(by_owner(stat[0, b]), axis=0)
            stat[1, b] = jnp.concatenate(by_owner(stat[1, b]), axis=0)
            return carry

        lax.fori_loop(0, 16, branch, 0)
        out = [
            pltpu.make_async_copy(acc, out_any.at[:, :, 0:LAT], sems.at[0]),
            pltpu.make_async_copy(stat.at[0], out_any.at[:, :, LAT:LAT + 128], sems.at[1]),
            pltpu.make_async_copy(stat.at[1], out_any.at[:, :, LAT + 128:LAT + 256], sems.at[2]),
        ]
        for copy in out:
            copy.start()
        for copy in out:
            copy.wait()


def spill(counts, lists, queries, cache):
    return pl.pallas_call(
        spill_kernel,
        out_shape=jax.ShapeDtypeStruct((16, ROWS, 2048), jnp.float32),
        in_specs=[pl.BlockSpec(memory_space=pl.ANY)] * 4,
        out_specs=pl.BlockSpec(memory_space=pl.ANY),
        scratch_shapes=[
            pltpu.SMEM((16,), jnp.int32),
            pltpu.VMEM((16, 64), jnp.int32),
            pltpu.VMEM((16, ROWS, KV), jnp.bfloat16),
            pltpu.VMEM((64, PAGE, KV), jnp.bfloat16),
            pltpu.VMEM((24, 256), jnp.int32),
            pltpu.SMEM((24, 256), jnp.int32),
            pltpu.VMEM((16, ROWS, LAT), jnp.float32),
            pltpu.VMEM((2, 16, ROWS, 128), jnp.float32),
            pltpu.SemaphoreType.DMA((3,)),
        ],
        compiler_params=pltpu.CompilerParams(vmem_limit_bytes=60 << 20),
        name="spill",
    )(counts, lists, queries, cache)


def fused_kernel(
    count_any, len_any, lists_any, new_any, q_any, cache_any, suffix_any, spill_any, out_ref,
    count_ref, len_ref, lists_ref, new_ref, q_ref, q_rows, q_send, q_all, cache_ref, suffix_ref,
    meta_v, meta_s, acc, top, tot, weight, weight2,
    part_send, stat_send, core_part, core_stat, row_send, row_stat_send, pre_part, pre_stat, mix_send, mix_stat_send, mix_part, mix_stat, done, passing,
    in_sems, own_sems, q_sems, core_sems, pre_sems, note_sems, mix_sems, end_sems, pass_sems,
):
    f32 = jnp.float32
    bf16 = jnp.bfloat16
    p = lax.axis_index("prefix")
    n = lax.axis_index("narrow")
    x = lax.div(p, 2)
    c = lax.rem(p, 2)
    mine = owner_of(p)
    stays = x == n
    across = {"prefix": 2 * n + c, "narrow": x}

    loads = [
        pltpu.make_async_copy(source, target, in_sems.at[k])
        for k, (source, target) in enumerate([
            (count_any, count_ref), (len_any, len_ref), (lists_any, lists_ref), (new_any, new_ref),
            (q_any, q_ref), (cache_any, cache_ref), (suffix_any, suffix_ref),
            (spill_any.at[:, :, 0:LAT], acc.at[pl.ds(SLOTS + 1, 16)]),
            (spill_any.at[:, :, LAT:LAT + 128], top.at[pl.ds(SLOTS + 1, 16)]),
            (spill_any.at[:, :, LAT + 128:LAT + 256], tot.at[pl.ds(SLOTS + 1, 16)]),
        ])
    ]
    barrier = pltpu.get_barrier_semaphore()

    def greet(**to):
        pl.semaphore_signal(barrier, inc=1, device_id=to, device_id_type=MESH)

    greet(prefix=2 * x + 1 - c)
    for k in range(1, 4):
        greet(prefix=2 * lax.rem(x + k, 4) + c)
        greet(narrow=lax.rem(n + k, 4))

    @pl.when(jnp.logical_not(stays))
    def _():
        greet(**across)

    for k in (0, 2, 4, 5, 1):
        loads[k].start()

    meta_v[...] = jnp.zeros_like(meta_v)
    acc[0] = jnp.zeros((ROWS, LAT), f32)
    top[0] = jnp.full((ROWS, 128), NONE, f32)
    tot[0] = jnp.zeros((ROWS, 128), f32)
    loads[0].wait()
    loads[2].wait()
    local, used, number, tiles, start, kept = tile_plan(lists_ref[...], count_ref, 64 * p)
    pack_pages(meta_v, local, used)
    slot = lax.broadcasted_iota(jnp.int32, (16, 256), 1).astype(f32)
    inside = (slot >= start) & (slot < start + tiles)
    branch = lax.broadcasted_iota(jnp.int32, (16, 256), 0).astype(f32)

    def pick(a):
        return jnp.sum(jnp.where(inside, a, 0.0), axis=0, keepdims=True).astype(jnp.int32)

    meta_v[16:17, :] = pick(branch)
    meta_v[17:18, :] = pick((slot - start) * GROUP)
    meta_v[18:19, :] = pick(jnp.clip(number - (slot - start) * GROUP, 0.0, float(GROUP)) * PAGE)
    meta_v[19:20, :] = pick(jnp.where(slot == start, NONE, -NONE))
    meta_v[20:21, :] = by_lane(jnp.where(kept > 0, start + kept, 0.0))
    meta_v[21:22, :] = by_lane(jnp.where(tiles > kept, branch + (SLOTS + 1.0), 0.0))
    meta_copy = pltpu.make_async_copy(meta_v, meta_s, own_sems.at[0])
    meta_copy.start()

    loads[4].wait()

    def order(i, carry):
        left = by_owner(q_ref[2 * i].astype(f32))
        right = by_owner(q_ref[2 * i + 1].astype(f32))
        q_rows[2 * i] = jnp.concatenate(left, axis=0).astype(bf16)
        q_rows[2 * i + 1] = jnp.concatenate(right, axis=0).astype(bf16)
        for d in range(8):
            q_send[d, pl.ds(pl.multiple_of(16 * i, 16), 16), :] = jnp.concatenate(
                [left[d], right[d]], axis=0
            ).astype(bf16)
        return carry

    def q_own(h):
        half = pl.ds(64 * h, 64)
        return pltpu.make_async_copy(q_send.at[mine, half], q_all.at[n, half], own_sems.at[1 + h])

    def q_copy(h, k):
        half = pl.ds(64 * h, 64)
        return pltpu.make_async_remote_copy(
            src_ref=q_send.at[mine, half], dst_ref=q_all.at[n, half],
            send_sem=q_sems.at[0, h, k], recv_sem=q_sems.at[1, h, n],
            device_id={"narrow": lax.rem(n + k, 4)}, device_id_type=MESH,
        )

    lax.fori_loop(0, 4, order, 0)
    pl.semaphore_wait(barrier, jnp.where(stays, 7, 8))
    for k in (2, 1, 3):
        q_copy(0, k).start()
    lax.fori_loop(4, 8, order, 0)
    for k in (2, 1, 3):
        q_copy(1, k).start()
    for h in range(2):
        q_own(h).start()

    meta_copy.wait()
    loads[5].wait()
    for k in (6, 3, 7, 8, 9):
        loads[k].start()
    key_iota = lax.broadcasted_iota(jnp.int32, (ROWS, TILE), 1)

    def tile_scores(s, u):
        b = jnp.clip(meta_s[16, s], 0, 15)
        k = jnp.clip(meta_s[17, s], 0, 60)
        live = meta_s[18, s]
        pages = [jnp.clip(meta_s[b, k + i], 0, 63) for i in range(GROUP)]
        keys = jnp.concatenate([cache_ref[page] for page in pages], axis=0)
        score = lax.dot_general(
            q_rows[b], keys, (((1,), (1,)), ((), ())), preferred_element_type=f32
        ) * TO_LOG2
        score = jnp.where(key_iota < live, score, MASKED)
        high = jnp.maximum(jnp.max(score, axis=1, keepdims=True), NONE)
        expo = jnp.exp2(score - high)
        weight[u] = expo.astype(bf16)
        return pages, high, jnp.sum(expo, axis=1, keepdims=True)

    def tile_group(i, carry):
        ready = [tile_scores(i * FUSED + u, u) for u in range(FUSED)]
        for u, (pages, high, total) in enumerate(ready):
            s = i * FUSED + u
            values = jnp.concatenate([cache_ref[page, :, :LAT] for page in pages], axis=0)
            part = jnp.dot(weight[u], values, preferred_element_type=f32)
            old = jnp.minimum(top[s], meta_s[19, s].astype(f32))
            new = jnp.maximum(old, high)
            f_old = jnp.exp2(old - new)
            f_new = jnp.exp2(high - new)
            top[s + 1] = new
            tot[s + 1] = tot[s] * f_old + total * f_new
            acc[s + 1] = acc[s] * wide(f_old) + part * wide(f_new)
        return carry

    lane64 = lax.broadcasted_iota(jnp.int32, (ROWS, 128), 1)

    def pack(i, carry):
        high_all, total_all = carry
        pieces = []
        for b in (2 * i, 2 * i + 1):
            at = jnp.clip(meta_s[20, b], 0, SLOTS)
            more = jnp.clip(meta_s[21, b], 0, SLOTS + 16)
            high = jnp.maximum(top[at], top[more])
            f_at = jnp.exp2(top[at] - high)
            f_more = jnp.exp2(top[more] - high)
            part = acc[at] * wide(f_at) + acc[more] * wide(f_more)
            code, high, total = coded(part, high, tot[at] * f_at + tot[more] * f_more)
            high_all = jnp.where(lane64 == b, high, high_all)
            total_all = jnp.where(lane64 == b, total, total_all)
            pieces.append(code)
        left, right = pieces
        for d in range(8):
            rows = slice(8 * d, 8 * d + 8)
            part_send[d, pl.ds(pl.multiple_of(16 * i, 16), 16), :] = jnp.concatenate(
                [left[rows], right[rows]], axis=0
            ).astype(LINK)
        return high_all, total_all

    def core_copies(h):
        other = 4 * (1 - c)
        half = pl.ds(64 * h, 64)
        return [
            pltpu.make_async_remote_copy(
                src_ref=part_send.at[pl.ds(other, 4), half], dst_ref=core_part.at[:, half],
                send_sem=core_sems.at[0, h, 0], recv_sem=core_sems.at[1, h, 0],
                device_id={"prefix": 2 * x + 1 - c}, device_id_type=MESH,
            ),
            pltpu.make_async_remote_copy(
                src_ref=stat_send.at[h, pl.ds(other, 4)], dst_ref=core_stat.at[h],
                send_sem=core_sems.at[0, h, 1], recv_sem=core_sems.at[1, h, 1],
                device_id={"prefix": 2 * x + 1 - c}, device_id_type=MESH,
            ),
        ]

    def pre_copy(g, k):
        other = lax.rem(x + k, 4)
        return pltpu.make_async_remote_copy(
            src_ref=row_send.at[other, quarter(g)], dst_ref=pre_part.at[x, quarter(g)],
            send_sem=pre_sems.at[0, g, k], recv_sem=pre_sems.at[1, g, x],
            device_id={"prefix": 2 * other + c}, device_id_type=MESH,
        )

    def pre_note(h, k):
        other = lax.rem(x + k, 4)
        return pltpu.make_async_remote_copy(
            src_ref=row_stat_send.at[h, other], dst_ref=pre_stat.at[h, x],
            send_sem=note_sems.at[0, h, k], recv_sem=note_sems.at[1, h, x],
            device_id={"prefix": 2 * other + c}, device_id_type=MESH,
        )

    def pre_own(g):
        return pltpu.make_async_copy(row_send.at[x, quarter(g)], pre_part.at[x, quarter(g)], pre_sems.at[0, g, 0])

    def note_own(h):
        return pltpu.make_async_copy(row_stat_send.at[h, x], pre_stat.at[h, x], note_sems.at[0, h, 0])

    def quarter(g):
        return pl.ds(pl.multiple_of(32 * g, 32), 32)

    def pack_half(h):
        high_all, total_all = lax.fori_loop(
            4 * h, 4 * h + 4, pack, (jnp.full((ROWS, 128), NONE, f32), jnp.zeros((ROWS, 128), f32))
        )
        for d in range(8):
            stat_send[h, d, 0:8, :] = high_all[8 * d:8 * d + 8]
            stat_send[h, d, 8:16, :] = total_all[8 * d:8 * d + 8]
        for copy in core_copies(h):
            copy.start()

    def join_cores(h):
        for copy in core_copies(h):
            copy.wait_recv()

        def scales(to):
            d = 4 * c + to
            high_a, high_b = stat_send[h, d, 0:8, :], core_stat[h, to, 0:8, :]
            high = jnp.maximum(high_a, high_b)
            f_a, f_b = jnp.exp2(high_a - high) * 0.5, jnp.exp2(high_b - high) * 0.5
            row_stat_send[h, to, 0:8, :] = high + 1.0
            row_stat_send[h, to, 8:16, :] = f_a * stat_send[h, d, 8:16, :] + f_b * core_stat[h, to, 8:16, :]
            return f_a, f_b

        factors = [scales(to) for to in range(4)]
        for g in (2 * h, 2 * h + 1):
            for to, (f_a, f_b) in enumerate(factors):
                for i in (2 * g, 2 * g + 1):
                    rows = slice(16 * i, 16 * i + 16)

                    def column(a):
                        return jnp.concatenate([a[:, 2 * i + j:2 * i + j + 1] for j in range(2)], axis=0)

                    value = (
                        part_send[4 * c + to, rows, :].astype(f32) * column(f_a)
                        + core_part[to, rows, :].astype(f32) * column(f_b)
                    )
                    row_send[to, rows, :] = jnp.round(value).astype(jnp.int32).astype(LINK)
            for k in (2, 1, 3):
                if g == 2 * h:
                    pre_note(h, k).start()
                pre_copy(g, k).start()
            if g == 2 * h:
                note_own(h).start()
            pre_own(g).start()

    lane8 = lax.broadcasted_iota(jnp.int32, (8, 128), 1)
    def q_arrived(h):
        q_own(h).wait()
        half = pl.ds(64 * h, 64)
        for k in range(1, 4):
            source = lax.rem(n + k, 4)
            landed = q_all.at[source, half]
            pltpu.make_async_copy(landed, landed, q_sems.at[1, h, source]).wait()


    def mix_copies(g, k):
        other = lax.rem(n + k, 4)
        return [
            pltpu.make_async_remote_copy(
                src_ref=mix_send.at[other, quarter(g)], dst_ref=mix_part.at[n, quarter(g)],
                send_sem=mix_sems.at[0, g, 0, k], recv_sem=mix_sems.at[1, g, 0, n],
                device_id={"narrow": other}, device_id_type=MESH,
            ),
            pltpu.make_async_remote_copy(
                src_ref=mix_stat_send.at[g, other], dst_ref=mix_stat.at[g, n],
                send_sem=mix_sems.at[0, g, 1, k], recv_sem=mix_sems.at[1, g, 1, n],
                device_id={"narrow": other}, device_id_type=MESH,
            ),
        ]

    def mix_own(g):
        return [
            pltpu.make_async_copy(mix_send.at[n, quarter(g)], mix_part.at[n, quarter(g)], mix_sems.at[0, g, 0, 0]),
            pltpu.make_async_copy(mix_stat_send.at[g, n], mix_stat.at[g, n], mix_sems.at[0, g, 1, 0]),
        ]

    mix_iota = lax.broadcasted_iota(jnp.int32, (32, TILE), 1)

    def mix_scores(i, u):
        rows = pl.ds(pl.multiple_of(16 * i, 16), 16)
        queries = jnp.concatenate([q_all[m, rows, :] for m in range(4)], axis=0)
        found = []
        for j in range(2):
            score = lax.dot_general(
                queries, suffix_ref[2 * i + j], (((1,), (1,)), ((), ())), preferred_element_type=f32
            )
            score = jnp.concatenate([score[16 * m + 8 * j:16 * m + 8 * j + 8] for m in range(4)], axis=0) * TO_LOG2
            score = jnp.where(mix_iota < len_ref[2 * i + j] - n * TILE, score, MASKED)
            high = jnp.maximum(jnp.max(score, axis=1, keepdims=True), NONE)
            expo = jnp.exp2(score - high)
            weight2[2 * u + j] = expo.astype(bf16)
            found.append((high, jnp.sum(expo, axis=1, keepdims=True)))
        return found

    def mix_pairs(g, carry):
        stats = [jnp.where(lane8 < 64, NONE, 0.0)] * 4
        ready = [mix_scores(2 * g + u, u) for u in range(2)]
        for u, found in enumerate(ready):
            i = 2 * g + u
            codes = []
            for j, (high, total) in enumerate(found):
                part = jnp.dot(
                    weight2[2 * u + j], suffix_ref[2 * i + j, :, :LAT], preferred_element_type=f32
                )
                code, high, total = coded(part, high, total)
                codes.append(code)
                for m in range(4):
                    rows = slice(8 * m, 8 * m + 8)
                    stats[m] = jnp.where(lane8 == 2 * i + j, high[rows], stats[m])
                    stats[m] = jnp.where(lane8 == 64 + 2 * i + j, total[rows], stats[m])
            for m in range(4):
                rows = slice(8 * m, 8 * m + 8)
                mix_send[m, pl.ds(pl.multiple_of(16 * i, 16), 16), :] = jnp.concatenate(
                    [codes[0][rows], codes[1][rows]], axis=0
                ).astype(LINK)
        for m in range(4):
            mix_stat_send[g, m] = stats[m]
        for k in (2, 1, 3):
            for copy in mix_copies(g, k):
                copy.start()
        for copy in mix_own(g):
            copy.start()
        return carry

    def send_on(g):
        return pltpu.make_async_remote_copy(
            src_ref=done.at[pl.ds(4 * g, 4)], dst_ref=out_ref.at[pl.ds(4 * g, 4)],
            send_sem=end_sems.at[0, g], recv_sem=end_sems.at[1, g],
            device_id=across, device_id_type=MESH,
        )

    far = lax.rem(x + 2, 4) == n

    def send_round(g):
        return pltpu.make_async_remote_copy(
            src_ref=done.at[pl.ds(4 * g, 4)], dst_ref=passing.at[pl.ds(4 * g, 4)],
            send_sem=end_sems.at[0, g], recv_sem=pass_sems.at[1, g],
            device_id={"narrow": x}, device_id_type=MESH,
        )

    def pass_on(g):
        return pltpu.make_async_remote_copy(
            src_ref=passing.at[pl.ds(4 * g, 4)], dst_ref=out_ref.at[pl.ds(4 * g, 4)],
            send_sem=pass_sems.at[0, g], recv_sem=end_sems.at[1, g],
            device_id={"prefix": 2 * lax.rem(x + 2, 4) + c}, device_id_type=MESH,
        )

    def finish(g):
        h = g // 2
        if g % 2 == 0:
            note_own(h).wait()
            for k in range(1, 4):
                noted = pre_stat.at[h, lax.rem(x + k, 4)]
                pltpu.make_async_copy(noted, noted, note_sems.at[1, h, lax.rem(x + k, 4)]).wait()
        pre_own(g).wait()
        for k in range(1, 4):
            landed = pre_part.at[lax.rem(x + k, 4), quarter(g)]
            pltpu.make_async_copy(landed, landed, pre_sems.at[1, g, lax.rem(x + k, 4)]).wait()
        for copy in mix_own(g):
            copy.wait()
        for k in range(1, 4):
            source = lax.rem(n + k, 4)
            landed = mix_part.at[source, quarter(g)]
            noted = mix_stat.at[g, source]
            pltpu.make_async_copy(landed, landed, mix_sems.at[1, g, 0, source]).wait()
            pltpu.make_async_copy(noted, noted, mix_sems.at[1, g, 1, source]).wait()

        highs = [pre_stat[h, i, 0:8, :] for i in range(4)] + [mix_stat[g, m] for m in range(4)]
        totals = [pre_stat[h, i, 8:16, :] for i in range(4)] + [pltpu.roll(mix_stat[g, m], 64, 1) for m in range(4)]
        highs += list(new_highs)
        totals += [1.0, 1.0]
        highest = functools.reduce(jnp.maximum, highs)
        factors = [jnp.exp2(high - highest) for high in highs]
        total = sum(f * t for f, t in zip(factors, totals))
        inverse = 1.0 / jnp.where(lax.div(lane8, 4) == g, total, 1.0)
        factors = [f * inverse for f in factors]
        for i in range(2 * g, 2 * g + 2):
            rows = slice(16 * i, 16 * i + 16)
            value = jnp.zeros((16, LAT), f32)
            for at, f in enumerate(factors):
                columns = [f[:, 2 * i + j:2 * i + j + 1] for j in range(2)]
                if at < 8:
                    source = pre_part[at, rows, :] if at < 4 else mix_part[at - 4, rows, :]
                    value = value + source.astype(f32) * jnp.concatenate(columns, axis=0)
                else:
                    u = at - 8
                    new = [new_ref[2 * i + j].astype(f32)[u:u + 1, :LAT] for j in range(2)]
                    value = value + jnp.concatenate([a * b for a, b in zip(columns, new)], axis=0)
            for j in range(2):
                for t in range(2):
                    at = 8 * j + 4 * t
                    done[2 * i + j, t] = value[at:at + 4].astype(bf16)

        @pl.when(stays)
        def _():
            out_ref[4 * g:4 * g + 4] = done[4 * g:4 * g + 4]

        if g < ROUND:
            @pl.when(far)
            def _():
                send_round(g).start()

        @pl.when(jnp.logical_not(stays | far) if g < ROUND else jnp.logical_not(stays))
        def _():
            send_on(g).start()

    lax.fori_loop(0, SLOTS_A // FUSED, tile_group, 0)
    for k in (7, 8, 9):
        loads[k].wait()
    pack_half(0)
    lax.fori_loop(SLOTS_A // FUSED + 0, SLOTS_A // FUSED + 1, tile_group, 0)
    loads[1].wait()
    loads[6].wait()
    q_arrived(0)
    lax.fori_loop(0, 1, mix_pairs, 0)
    join_cores(0)
    lax.fori_loop(1, 2, mix_pairs, 0)
    pack_half(1)
    q_arrived(1)
    lax.fori_loop(2, 3, mix_pairs, 0)
    join_cores(1)
    lax.fori_loop(3, 4, mix_pairs, 0)
    loads[3].wait()
    step8 = lax.broadcasted_iota(jnp.int32, (8, 1), 0) >= 4

    def new_scores(i, carry):
        queries = q_send[mine, pl.ds(pl.multiple_of(16 * i, 16), 16), :].astype(f32)
        out = list(carry)
        for j in range(2):
            keys = new_ref[2 * i + j].astype(f32)
            for u in range(2):
                score = jnp.sum(queries[8 * j:8 * j + 8] * keys[u:u + 1], axis=1, keepdims=True) * TO_LOG2
                if u == 1:
                    score = jnp.where(step8, score, NONE)
                out[u] = jnp.where(lane8 == 2 * i + j, score, out[u])
        return tuple(out)

    new_highs = lax.fori_loop(0, 8, new_scores, tuple([jnp.full((8, 128), NONE, f32)] * 2))

    finish(0)
    finish(1)
    finish(2)
    finish(3)

    @pl.when(stays)
    def _():
        for g in range(ROUND):
            landed = passing.at[pl.ds(4 * g, 4)]
            pltpu.make_async_copy(landed, landed, pass_sems.at[1, g]).wait()
            pass_on(g).start()
        for g in range(ROUND):
            pass_on(g).wait_send()


    for h in range(2):
        for k in range(1, 4):
            q_copy(h, k).wait_send()
    for h in range(2):
        for copy in core_copies(h):
            copy.wait_send()
        for k in range(1, 4):
            pre_note(h, k).wait_send()
            pre_copy(2 * h, k).wait_send()
            pre_copy(2 * h + 1, k).wait_send()
    for g in range(4):
        for k in range(1, 4):
            for copy in mix_copies(g, k):
                copy.wait_send()

    @pl.when(jnp.logical_not(stays))
    def _():
        for g in range(4):
            send_on(g).wait()


def fused(counts, lens, lists, new_latent, queries, cache, suffix, spilled):
    dma = pltpu.SemaphoreType.DMA
    f32, bf16, i32 = jnp.float32, jnp.bfloat16, jnp.int32
    return pl.pallas_call(
        fused_kernel,
        out_shape=jax.ShapeDtypeStruct((16, 2, 4, LAT), bf16),
        in_specs=[pl.BlockSpec(memory_space=pl.ANY)] * 8,
        out_specs=pl.BlockSpec(memory_space=pltpu.VMEM),
        scratch_shapes=[
            pltpu.SMEM((16,), i32),
            pltpu.SMEM((16,), i32),
            pltpu.VMEM((16, 64), i32),
            pltpu.VMEM((16, 2, KV), bf16),
            pltpu.VMEM((16, ROWS, KV), bf16),
            pltpu.VMEM((16, ROWS, KV), bf16),
            pltpu.VMEM((8, 128, KV), bf16),
            pltpu.VMEM((4, 128, KV), bf16),
            pltpu.VMEM((64, PAGE, KV), bf16),
            pltpu.VMEM((16, TILE, KV), bf16),
            pltpu.VMEM((24, 256), i32),
            pltpu.SMEM((24, 256), i32),
            pltpu.VMEM((SLOTS + 17, ROWS, LAT), f32),
            pltpu.VMEM((SLOTS + 17, ROWS, 128), f32),
            pltpu.VMEM((SLOTS + 17, ROWS, 128), f32),
            pltpu.VMEM((FUSED, ROWS, TILE), bf16),
            pltpu.VMEM((4, 32, TILE), bf16),
            pltpu.VMEM((8, 128, LAT), LINK),
            pltpu.VMEM((2, 8, 16, 128), f32),
            pltpu.VMEM((4, 128, LAT), LINK),
            pltpu.VMEM((2, 4, 16, 128), f32),
            pltpu.VMEM((4, 128, LAT), LINK),
            pltpu.VMEM((2, 4, 16, 128), f32),
            pltpu.VMEM((4, 128, LAT), LINK),
            pltpu.VMEM((2, 4, 16, 128), f32),
            pltpu.VMEM((4, 128, LAT), LINK),
            pltpu.VMEM((4, 4, 8, 128), f32),
            pltpu.VMEM((4, 128, LAT), LINK),
            pltpu.VMEM((4, 4, 8, 128), f32),
            pltpu.VMEM((16, 2, 4, LAT), bf16),
            pltpu.VMEM((4 * ROUND, 2, 4, LAT), bf16),
            dma((10,)),
            dma((3,)),
            dma((2, 2, 4)),
            dma((2, 2, 2)),
            dma((2, 4, 4)),
            dma((2, 2, 4)),
            dma((2, 4, 2, 4)),
            dma((2, 4)),
            dma((2, ROUND)),
        ],
        compiler_params=pltpu.CompilerParams(
            collective_id=1, has_side_effects=True, vmem_limit_bytes=52 << 20
        ),
        name="fused",
    )(counts, lens, lists, new_latent, queries, cache, suffix, spilled)


def local(queries, new_latent, prefix_cache, suffix_cache, page_lists, prefix_count, suffix_len):
    rows = queries.reshape(16, ROWS, KV)
    suffix = suffix_cache.reshape(16, TILE, KV)
    spilled = spill(prefix_count, page_lists, rows, prefix_cache)
    return fused(
        prefix_count, suffix_len, page_lists, new_latent, rows, prefix_cache, suffix, spilled
    )


def solution(mesh):
    return jax.shard_map(
        local,
        mesh=mesh,
        in_specs=(
            P("batch", None, "narrow", None),
            P("batch", None, None),
            P("prefix", None, None),
            P("batch", "narrow", None, None),
            P("batch", None),
            P("batch"),
            P("batch"),
        ),
        out_specs=P("batch", None, ("prefix", "narrow"), None),
        check_vma=False,
    )
```
